32 devices in a mesh: parts: 2 (over y), item: 4 (over z), user: 2 (over x), ka: 2 (over core).
Axes of the slice: x: 2, y: 2, z: 4, core: 2. Of those that a mesh axis runs over, the one named last changes fastest.
Arguments:
- counts: int32 [8, 2, 64, 128, 128], P(('parts', 'item'), 'user'), parts along dimension 0, may hold values from 0 to 5, as said below
- tile_user: int32 [8, 2, 64], P(('parts', 'item'), 'user'), parts along dimension 0, may hold values from 0 to 15, as said below
- tile_item: int32 [8, 2, 64], P(('parts', 'item'), 'user'), parts along dimension 0, may hold values from 0 to 7
- tile_live: int32 [8, 2], P(('parts', 'item'), 'user'), parts along dimension 0, may hold values from 1 to 64, as said below
- theta_shape: float32 [4, 2048, 512], P(('parts', 'user'), 'item', 'ka'), parts along dimension 0, may hold values from 0.3 to 3
- theta_rate: float32 [4, 2048, 512], P(('parts', 'user'), 'item', 'ka'), parts along dimension 0, may hold values from 512 to 32768
- user_activity: float32 [4, 2048], P(('parts', 'user'), 'item'), parts along dimension 0, may hold values from 0.3 to 3
- beta_shape: float32 [8, 1024, 512], P(('parts', 'item'), 'user', 'ka'), parts along dimension 0, may hold values from 0.3 to 3
- beta_rate: float32 [8, 1024, 512], P(('parts', 'item'), 'user', 'ka'), parts along dimension 0, may hold values from 512 to 32768
- item_popularity: float32 [8, 1024], P(('parts', 'item'), 'user'), parts along dimension 0, may hold values from 0.3 to 3
Outputs:
- new_theta_shape: float32 [4, 2048, 512], P(('parts', 'user'), 'item', 'ka'), parts along dimension 0
- new_theta_rate: float32 [4, 2048, 512], P(('parts', 'user'), 'item', 'ka'), parts along dimension 0
- new_beta_shape: float32 [8, 1024, 512], P(('parts', 'item'), 'user', 'ka'), parts along dimension 0
- new_beta_rate: float32 [8, 1024, 512], P(('parts', 'item'), 'user', 'ka'), parts along dimension 0
The draws below stay inside these ranges and needn't reach their ends.
There are 2 independent parts, one for each index of `parts`. The reference program is written for one: setup_inputs(seed, part) draws one part's arguments, and reference() takes and returns one part's arrays. A program takes and returns all parts, laid end to end along the dimension named above; each array names one. Nothing has to cross between parts.
Inputs may be any that keep to these rules, and one draw needn't show every extreme that they name: `tile_live`: slots at or beyond a device's live count hold stale tiles; some device has all 64 slots live. `counts`: most cells are 0. The pairs (tile_user, tile_item) of the 64 slots of one device are all different.
All inputs are finite; a program needn't handle non-finite values.
Results may differ from the reference program's by a relative error of at most 0.006.
Values may be sent and summed in bfloat16 or wider, within the bound.
No kernel may reach another device: no remote copies, remote signals or barrier semaphores. Data moves between devices by JAX's collectives and lax.ppermute only.
A program may use at most 64 MiB of HBM per device.

```python
import math
import jax
import jax.numpy as jnp
from jax import lax

K = 512
TILE = 128
UT_SUB = 16
IT_DEV = 8
NT = 64
U_SUB = 2048
ISH = 1024
USERS = 4096
ITEMS = 4096
N_ITEM = 4
N_USER = 2
N_KA = 2


def slot_pairs(key):
    device_keys = jax.random.split(key, N_ITEM * N_USER)

    def pick_pairs(single_key):
        return jax.random.permutation(single_key, UT_SUB * IT_DEV)[:NT]
    chosen = jax.vmap(pick_pairs)(device_keys)
    return chosen.reshape(N_ITEM, N_USER, NT).astype(jnp.int32)


def draw_tile_user(key, part):
    chosen = slot_pairs(key)
    return (chosen // IT_DEV).astype(jnp.int32)


def draw_tile_item(key, part):
    chosen = slot_pairs(key)
    return (chosen % IT_DEV).astype(jnp.int32)


def draw_counts(key, part):
    key = jax.random.fold_in(key, 11)
    value_key, keep_key = jax.random.split(key)
    shape_all = (N_ITEM, N_USER, NT, TILE, TILE)
    values = jax.random.randint(value_key, shape_all, 1, 6, dtype=jnp.int32)
    keep = jax.random.randint(keep_key, shape_all, 0, 32, dtype=jnp.int32)
    return jnp.where(keep == 0, values, 0).astype(jnp.int32)


def draw_tile_live(key, part):
    key = jax.random.fold_in(key, 23)
    first_key, second_key, place_key = jax.random.split(key, 3)
    first = jax.random.randint(first_key, (N_ITEM * N_USER,), 1, NT + 1, dtype=jnp.int32)
    second = jax.random.randint(second_key, (N_ITEM * N_USER,), 1, NT + 1, dtype=jnp.int32)
    live = jnp.minimum(first, second)
    place = jax.random.randint(place_key, (), 0, N_ITEM * N_USER, dtype=jnp.int32)
    live = jnp.where(jnp.arange(N_ITEM * N_USER, dtype=jnp.int32) == place, NT, live)
    return live.reshape(N_ITEM, N_USER).astype(jnp.int32)


def draw_theta_rate(key, part):
    key = jax.random.fold_in(key, 31)
    spread_key = jax.random.fold_in(key, 1)
    shape_all = (N_USER, U_SUB, K)
    offset = jax.random.uniform(spread_key, shape_all, jnp.float32, -2.079, 2.079)
    return (USERS * jnp.exp(offset)).astype(jnp.float32)


def draw_beta_rate(key, part):
    key = jax.random.fold_in(key, 37)
    spread_key = jax.random.fold_in(key, 1)
    shape_all = (N_ITEM, ISH, K)
    offset = jax.random.uniform(spread_key, shape_all, jnp.float32, -2.079, 2.079)
    return (ITEMS * jnp.exp(offset)).astype(jnp.float32)


def levels(rng, shape, cuts, smallest, top_value):
    loudness, own = 1.0, jax.random.fold_in(rng, 6)
    for axis_at, parts in cuts:
        heights = jnp.exp(jax.random.uniform(jax.random.fold_in(own, axis_at), (parts,), jnp.float32, smallest / len(cuts), top_value / len(cuts)))
        loudness = loudness * jnp.repeat(heights, shape[axis_at] // parts).reshape([-1 if axis == axis_at else 1 for axis in range(len(shape))])
    return loudness


def setup_inputs(seed: int = 0, part: int = 0) -> dict:
    key_list = jax.random.split(jax.random.key(seed), 11)
    part_splits = jax.random.split(jax.random.fold_in(key_list[10], part), 11)
    return {
        "counts": draw_counts(jax.random.fold_in(jax.random.fold_in(key_list[10], part), 71), part),
        "tile_user": draw_tile_user(jax.random.fold_in(jax.random.fold_in(key_list[10], part), 71), part),
        "tile_item": draw_tile_item(jax.random.fold_in(jax.random.fold_in(key_list[10], part), 71), part),
        "tile_live": draw_tile_live(jax.random.fold_in(jax.random.fold_in(key_list[10], part), 71), part),
        "theta_shape": jnp.clip(jnp.exp(math.log(3.0) - 2.3025851 * jax.random.uniform(part_splits[4], (N_USER, U_SUB, K), jnp.float32) ** levels(part_splits[4], (N_USER, U_SUB, K), ((0, 2), (1, 4), (2, 2)), -0.2, 0.2)), 0.3, 3.0),
        "theta_rate": draw_theta_rate(jax.random.fold_in(jax.random.fold_in(key_list[10], part), 71), part),
        "user_activity": jnp.clip(jnp.exp(math.log(3.0) - 2.3025851 * jax.random.uniform(part_splits[6], (N_USER, U_SUB), jnp.float32) ** levels(part_splits[6], (N_USER, U_SUB), ((0, 2), (1, 4)), -0.2, 0.2)), 0.3, 3.0),
        "beta_shape": jnp.clip(jnp.exp(math.log(3.0) - 2.3025851 * jax.random.uniform(part_splits[7], (N_ITEM, ISH, K), jnp.float32) ** levels(part_splits[7], (N_ITEM, ISH, K), ((0, 4), (1, 2), (2, 2)), -0.2, 0.2)), 0.3, 3.0),
        "beta_rate": draw_beta_rate(jax.random.fold_in(jax.random.fold_in(key_list[10], part), 71), part),
        "item_popularity": jnp.clip(jnp.exp(math.log(3.0) - 2.3025851 * jax.random.uniform(part_splits[9], (N_ITEM, ISH), jnp.float32) ** levels(part_splits[9], (N_ITEM, ISH), ((0, 4), (1, 2)), -0.2, 0.2)), 0.3, 3.0),
    }


def expected_exp(shape_arg, rate_arg):
    return jnp.exp(lax.digamma(shape_arg) - jnp.log(rate_arg)).astype(jnp.bfloat16)


def reference(counts, tile_user, tile_item, tile_live, theta_shape, theta_rate, user_activity, beta_shape, beta_rate, item_popularity):
    user_exp = expected_exp(theta_shape, theta_rate)
    item_exp = expected_exp(beta_shape, beta_rate)
    half = K // N_KA
    user_tiles = user_exp.reshape(N_USER, UT_SUB, TILE, K)
    item_tiles = item_exp.reshape(N_ITEM, IT_DEV, TILE, K)
    slot_index = jnp.arange(NT, dtype=jnp.int32)

    def device(carry, index):
        user_stat, item_stat = carry
        shard = index // N_USER
        block = index % N_USER
        users = tile_user[shard, block]
        items = tile_item[shard, block]
        left = user_tiles[block][users].astype(jnp.float32)
        right = item_tiles[shard][items].astype(jnp.float32)
        norms = jnp.zeros((NT, TILE, TILE), jnp.float32)
        for piece in range(N_KA):
            part = jnp.einsum("bik,bjk->bij", left[..., piece * half:(piece + 1) * half], right[..., piece * half:(piece + 1) * half]).astype(jnp.bfloat16)
            norms = norms + lax.optimization_barrier(part).astype(jnp.float32)
        live = (slot_index < tile_live[shard, block])[:, None, None]
        grid = counts[shard, block].astype(jnp.float32)
        ratio = jnp.where(live, grid / jnp.where(live, norms, 1.0), 0.0).astype(jnp.bfloat16)
        ratio = lax.optimization_barrier(ratio).astype(jnp.float32)
        user_part = jnp.einsum("bij,bjk->bik", ratio, right)
        item_part = jnp.einsum("bij,bik->bjk", ratio, left)
        user_stat = user_stat.at[block, users].add(user_part)
        item_stat = item_stat.at[shard, items].add(item_part)
        return (user_stat, item_stat), None

    start = (jnp.zeros((N_USER, UT_SUB, TILE, K), jnp.float32), jnp.zeros((N_ITEM, IT_DEV, TILE, K), jnp.float32))
    (user_stat, item_stat), unused = lax.scan(device, start, jnp.arange(N_ITEM * N_USER, dtype=jnp.int32))
    user_stat = user_stat.reshape(N_USER, UT_SUB * TILE, K)
    item_stat = item_stat.reshape(N_ITEM, IT_DEV * TILE, K)
    beta_total = jnp.sum(beta_shape / beta_rate, axis=(0, 1))
    theta_total = jnp.sum(theta_shape / theta_rate, axis=(0, 1))
    new_theta_shape = 0.3 + user_exp.astype(jnp.float32) * user_stat
    new_theta_rate = user_activity[..., None] + beta_total
    new_beta_shape = 0.3 + item_exp.astype(jnp.float32) * item_stat
    new_beta_rate = item_popularity[..., None] + theta_total
    return (new_theta_shape, new_theta_rate, new_beta_shape, new_beta_rate)
```

```python
import functools

import jax
import jax.numpy as jnp
from jax import lax
from jax.experimental import pallas as pl
from jax.experimental.pallas import tpu as pltpu
from jax.sharding import PartitionSpec as P

BF16 = jnp.bfloat16
F32 = jnp.float32
VMEM_LIMIT = 48 * 1024 * 1024


def exp_digamma_over(x, inv_rate):
    w = x * (x + 5.0)
    shift = (2.0 * x + 5.0) * (3.0 * w * w + 20.0 * w + 24.0) / (w * (w + 4.0) * (w + 6.0))
    y = x + 6.0
    iy = 1.0 / y
    iy2 = iy * iy
    series = iy * 0.5 + iy2 * (1.0 / 12.0 - iy2 * (1.0 / 120.0 - iy2 * (1.0 / 252.0)))
    return y * inv_rate * jnp.exp(-(series + shift))


def expected_kernel(shape_ref, rate_ref, exp_ref, total_ref):
    x = shape_ref[...]
    inv_rate = 1.0 / rate_ref[...]
    exp_ref[...] = exp_digamma_over(x, inv_rate).astype(BF16)
    part = jnp.sum(x * inv_rate, axis=0, keepdims=True)

    @pl.when(pl.program_id(0) == 0)
    def _():
        total_ref[...] = part

    @pl.when(pl.program_id(0) != 0)
    def _():
        total_ref[...] += part


def expected(shape_arg, rate_arg, name):
    rows, cols = shape_arg.shape
    block = min(rows, 128)
    spec = pl.BlockSpec((block, cols), lambda g: (g, 0))
    return pl.pallas_call(
        expected_kernel,
        grid=(rows // block,),
        in_specs=[spec, spec],
        out_specs=[spec, pl.BlockSpec((1, cols), lambda g: (0, 0))],
        out_shape=[
            jax.ShapeDtypeStruct((rows, cols), BF16),
            jax.ShapeDtypeStruct((1, cols), F32),
        ],
        cost_estimate=pl.CostEstimate(
            flops=40 * rows * cols, transcendentals=4 * rows * cols, bytes_accessed=10 * rows * cols
        ),
        name=name,
    )(shape_arg, rate_arg)


def dense_kernel(n_user, shard_tiles, chunk, users_ref, items_ref, live_ref, me_ref, counts_ref, out_ref):
    g = pl.program_id(0)
    tile = counts_ref.shape[1]

    @pl.when(g == 0)
    def _():
        out_ref[...] = jnp.zeros_like(out_ref)

    def place(t, carry):
        slot = g * chunk + t
        item = items_ref[slot]
        owner = lax.div(item, shard_tiles)
        position = lax.rem(me_ref[0] - owner + n_user, n_user)
        column = position * shard_tiles + lax.rem(item, shard_tiles)
        row = pl.multiple_of(users_ref[slot] * tile, tile)
        col = pl.multiple_of(column * tile, tile)
        out_ref[pl.ds(row, tile), pl.ds(col, tile)] = counts_ref[t].astype(F32).astype(BF16)
        return carry

    lax.fori_loop(0, jnp.clip(live_ref[0] - g * chunk, 0, chunk), place, 0)


def dense_counts(counts, users, items, live, me, user_rows, item_rows, n_user):
    slots, tile, _ = counts.shape
    chunk = 8
    shard_tiles = item_rows // n_user // tile
    return pl.pallas_call(
        functools.partial(dense_kernel, n_user, shard_tiles, chunk),
        grid_spec=pltpu.PrefetchScalarGridSpec(
            num_scalar_prefetch=4,
            grid=(slots // chunk,),
            in_specs=[pl.BlockSpec((chunk, tile, tile), lambda g, *_: (g, 0, 0))],
            out_specs=pl.BlockSpec((user_rows, item_rows), lambda g, *_: (0, 0)),
        ),
        out_shape=jax.ShapeDtypeStruct((user_rows, item_rows), BF16),
        compiler_params=pltpu.CompilerParams(vmem_limit_bytes=VMEM_LIMIT),
        cost_estimate=pl.CostEstimate(
            flops=slots * tile * tile,
            transcendentals=0,
            bytes_accessed=4 * slots * tile * tile + 2 * user_rows * item_rows,
        ),
        name="dense_counts",
    )(users, items, live, me, counts)


def stat_kernel(pieces, has_sum, has_acc, index_ref, mine_ref, other_ref, *refs):
    refs = list(refs)
    item_mine = [refs.pop(0) for _ in range(pieces)]
    item_other = [refs.pop(0) for _ in range(pieces)]
    counts_ref = refs.pop(0)
    sum_ref = refs.pop(0) if has_sum else None
    acc_in = [refs.pop(0) for _ in range(pieces)] if has_acc else None
    stat_ref = refs.pop(0)
    acc_out = [refs.pop(0) for _ in range(pieces)]
    acc = [refs.pop(0) for _ in range(pieces)]
    g = pl.program_id(0)

    @pl.when(g == 0)
    def _():
        for p in range(pieces):
            if has_acc:
                acc[p][...] = acc_in[p][...]
            else:
                acc[p][...] = jnp.zeros_like(acc[p])

    mine = mine_ref[...]
    other = other_ref[...]
    dims_nt = (((1,), (1,)), ((), ()))
    dims_tn = (((0,), (0,)), ((), ()))
    total = sum_ref[...].astype(F32) if has_sum else None
    width = 256
    for p in range(pieces):
        rows = item_mine[p].shape[0]
        for c in range(rows // width):
            part = slice(c * width, (c + 1) * width)
            left = item_mine[p][part, :]
            norm = lax.dot_general(mine, left, dims_nt, preferred_element_type=F32)
            norm += lax.dot_general(other, item_other[p][part, :], dims_nt, preferred_element_type=F32)
            grid = counts_ref[:, p * rows + c * width : p * rows + (c + 1) * width].astype(F32)
            ratio = (grid / norm).astype(BF16)
            stat = jnp.dot(ratio, left, preferred_element_type=F32)
            total = stat if total is None else total + stat
            acc[p][:, part] += lax.dot_general(mine, ratio, dims_tn, preferred_element_type=F32)
    stat_ref[...] = total.astype(stat_ref.dtype)

    @pl.when(g == pl.num_programs(0) - 1)
    def _():
        for p in range(pieces):
            acc_out[p][...] = acc[p][...].astype(acc_out[p].dtype)


def statistics(index, mine, other, item_mine, item_other, dense, running, acc, stat_dtype, acc_dtypes, name):
    rows, half = mine.shape
    pieces = len(item_mine)
    item_rows = dense.shape[1]
    block = min(rows, 256)
    steps = rows // block
    row_spec = pl.BlockSpec((block, half), lambda g, i: (g, 0))
    piece_spec = pl.BlockSpec((item_rows // pieces, half), lambda g, i: (0, 0))
    acc_spec = pl.BlockSpec((half, item_rows // pieces), lambda g, i: (0, 0))
    args = [mine, other, *item_mine, *item_other, dense]
    in_specs = [row_spec, row_spec] + [piece_spec] * (2 * pieces)
    in_specs.append(pl.BlockSpec((block, item_rows), lambda g, i: (i[0] * steps + g, 0)))
    if running is not None:
        args.append(running)
        in_specs.append(row_spec)
    if acc is not None:
        args += acc
        in_specs += [acc_spec] * pieces
    out = pl.pallas_call(
        functools.partial(stat_kernel, pieces, running is not None, acc is not None),
        grid_spec=pltpu.PrefetchScalarGridSpec(
            num_scalar_prefetch=1,
            grid=(steps,),
            in_specs=in_specs,
            out_specs=[row_spec] + [acc_spec] * pieces,
            scratch_shapes=[pltpu.VMEM((half, item_rows // pieces), F32)] * pieces,
        ),
        out_shape=[jax.ShapeDtypeStruct((rows, half), stat_dtype)]
        + [jax.ShapeDtypeStruct((half, item_rows // pieces), d) for d in acc_dtypes],
        compiler_params=pltpu.CompilerParams(vmem_limit_bytes=VMEM_LIMIT),
        cost_estimate=pl.CostEstimate(
            flops=8 * rows * item_rows * half,
            transcendentals=rows * item_rows,
            bytes_accessed=4 * rows * half + 4 * item_rows * half + 2 * rows * item_rows + 8 * item_rows * half,
        ),
        name=name,
    )(index, *args)
    return out[0], list(out[1:])


def finish_users_kernel(exp_ref, own_ref, came_ref, out_ref):
    total = own_ref[...] + came_ref[...].astype(F32)
    out_ref[...] = 0.3 + exp_ref[...].astype(F32) * total


def finish_items_kernel(pieces, exp_ref, own_ref, *refs):
    total = own_ref[...]
    for p in range(pieces):
        total += refs[p][...].astype(F32)
    refs[pieces][...] = 0.3 + exp_ref[...].astype(F32) * total.T


def ring(x, axis, n, shift):
    return lax.ppermute(x, axis, [(i, (i + shift) % n) for i in range(n)])


def body(
    n_item,
    n_user,
    n_ka,
    counts,
    tile_user,
    tile_item,
    tile_live,
    theta_shape,
    theta_rate,
    user_activity,
    beta_shape,
    beta_rate,
    item_popularity,
):
    def sibling(x):
        return ring(x, "ka", n_ka, 1)

    user_exp, theta_local = expected(theta_shape[0], theta_rate[0], "expected_users")
    item_exp, beta_local = expected(beta_shape[0], beta_rate[0], "expected_items")
    rows = user_exp.shape[0]
    user_rows = rows * n_item
    item_rows = item_exp.shape[0] * n_user

    item_mine = [item_exp]
    for t in range(1, n_user):
        item_mine.append(ring(item_mine[-1], "user", n_user, 1))
    item_other = [sibling(x) for x in item_mine]

    b_index = lax.axis_index("user").astype(jnp.int32)
    s_index = lax.axis_index("item").astype(jnp.int32)
    dense = dense_counts(
        counts[0, 0],
        tile_user[0, 0],
        tile_item[0, 0],
        tile_live[0],
        b_index[None],
        user_rows,
        item_rows,
        n_user,
    )

    own_stat = None
    running = None
    acc = None
    mine = user_exp
    for t in range(n_item):
        last = t == n_item - 1
        following = None if last else ring(mine, "item", n_item, 1)
        other = sibling(mine)
        index = lax.rem(s_index - t + n_item, n_item)[None]
        acc_dtypes = [F32] + [BF16 if last else F32] * (n_user - 1)
        stat, acc = statistics(
            index,
            mine,
            other,
            item_mine,
            item_other,
            dense,
            running,
            acc,
            F32 if t == 0 else BF16,
            acc_dtypes,
            "statistics_%d" % t,
        )
        if t == 0:
            own_stat = stat
        else:
            running = ring(stat, "item", n_item, 1)
        mine = following

    came = [ring(acc[t], "user", n_user, -t) for t in range(1, n_user)]

    totals = jnp.concatenate([theta_local, beta_local], axis=0)
    moving = totals
    for t in range(1, n_user):
        moving = ring(moving, "user", n_user, 1)
        totals = totals + moving
    moving = totals
    for t in range(1, n_item):
        moving = ring(moving, "item", n_item, 1)
        totals = totals + moving
    theta_total = totals[0]
    beta_total = totals[1]

    half = user_exp.shape[1]
    user_block = min(rows, 256)
    user_spec = pl.BlockSpec((user_block, half), lambda g: (g, 0))
    new_theta_shape = pl.pallas_call(
        finish_users_kernel,
        grid=(rows // user_block,),
        in_specs=[user_spec] * 3,
        out_specs=user_spec,
        out_shape=jax.ShapeDtypeStruct((rows, half), F32),
        cost_estimate=pl.CostEstimate(flops=3 * rows * half, transcendentals=0, bytes_accessed=12 * rows * half),
        name="finish_users",
    )(user_exp, own_stat, running)
    own_items = item_exp.shape[0]
    item_block = min(own_items, 256)
    item_spec = pl.BlockSpec((item_block, half), lambda g: (g, 0))
    acc_spec = pl.BlockSpec((half, item_block), lambda g: (0, g))
    new_beta_shape = pl.pallas_call(
        functools.partial(finish_items_kernel, n_user - 1),
        grid=(own_items // item_block,),
        in_specs=[item_spec] + [acc_spec] * n_user,
        out_specs=item_spec,
        out_shape=jax.ShapeDtypeStruct((own_items, half), F32),
        cost_estimate=pl.CostEstimate(
            flops=3 * own_items * half, transcendentals=0, bytes_accessed=12 * own_items * half
        ),
        name="finish_items",
    )(item_exp, acc[0], *came)
    new_theta_rate = user_activity[..., None] + beta_total
    new_beta_rate = item_popularity[..., None] + theta_total
    return (new_theta_shape[None], new_theta_rate, new_beta_shape[None], new_beta_rate)


def solution(mesh):
    in_specs = (
        P(("parts", "item"), "user", None, None, None),
        P(("parts", "item"), "user", None),
        P(("parts", "item"), "user", None),
        P(("parts", "item"), "user"),
        P(("parts", "user"), "item", "ka"),
        P(("parts", "user"), "item", "ka"),
        P(("parts", "user"), "item"),
        P(("parts", "item"), "user", "ka"),
        P(("parts", "item"), "user", "ka"),
        P(("parts", "item"), "user"),
    )
    out_specs = (
        P(("parts", "user"), "item", "ka"),
        P(("parts", "user"), "item", "ka"),
        P(("parts", "item"), "user", "ka"),
        P(("parts", "item"), "user", "ka"),
    )
    run = functools.partial(body, mesh.shape["item"], mesh.shape["user"], mesh.shape["ka"])
    return jax.shard_map(run, mesh=mesh, in_specs=in_specs, out_specs=out_specs, check_vma=False)
```

```python
import functools

import jax
import jax.numpy as jnp
from jax import lax
from jax.experimental import pallas as pl
from jax.experimental.pallas import tpu as pltpu
from jax.sharding import PartitionSpec as P

BF16 = jnp.bfloat16
F32 = jnp.float32
VMEM = pltpu.MemorySpace.VMEM
SMEM = pltpu.MemorySpace.SMEM
DIMS_NT = (((1,), (1,)), ((), ()))
DIMS_TN = (((0,), (0,)), ((), ()))


def exp_digamma(x, inv_rate):
    w = x * (x + 3.0)
    p = w * (w + 2.0)
    y = x + 4.0
    inv = 1.0 / (y * p)
    iy = inv * p
    iy2 = iy * iy
    shift = (2.0 * x + 3.0) * (2.0 * w + 2.0) * (inv * y)
    series = iy * 0.5 + iy2 * (1.0 / 12.0 - iy2 * (1.0 / 120.0 - iy2 * (1.0 / 252.0)))
    return y * inv_rate * jnp.exp(-(series + shift))


def users_kernel(steps, core_ref, shape_ref, rate_ref, keep_ref, give_ref, total_ref):
    g = pl.program_id(0)
    x = shape_ref[...]
    inv_rate = 1.0 / rate_ref[...]
    value = exp_digamma(x, inv_rate).astype(BF16)
    part = jnp.sum(x * inv_rate, axis=0, keepdims=True)

    @pl.when(g < steps)
    def _():
        give_ref[...] = value

    @pl.when(g >= steps)
    def _():
        keep_ref[...] = value

    @pl.when(g == 0)
    def _():
        total_ref[...] = part

    @pl.when(g != 0)
    def _():
        total_ref[...] += part


def expected_users(core, shape_arg, rate_arg):
    rows, cols = shape_arg.shape
    half = rows // 2
    block = min(half, 128)
    steps = half // block
    in_spec = pl.BlockSpec(
        (block, cols), lambda g, c: (lax.rem(c[0] + 1 + lax.div(g, steps), 2) * steps + lax.rem(g, steps), 0)
    )
    return pl.pallas_call(
        functools.partial(users_kernel, steps),
        grid_spec=pltpu.PrefetchScalarGridSpec(
            num_scalar_prefetch=1,
            grid=(2 * steps,),
            in_specs=[in_spec, in_spec],
            out_specs=[
                pl.BlockSpec((block, cols), lambda g, c: (jnp.maximum(g - steps, 0), 0)),
                pl.BlockSpec((block, cols), lambda g, c: (jnp.minimum(g, steps - 1), 0)),
                pl.BlockSpec((1, cols), lambda g, c: (0, 0)),
            ],
        ),
        out_shape=[
            jax.ShapeDtypeStruct((half, cols), BF16),
            jax.ShapeDtypeStruct((half, cols), BF16),
            jax.ShapeDtypeStruct((1, cols), F32),
        ],
        cost_estimate=pl.CostEstimate(
            flops=40 * rows * cols, transcendentals=3 * rows * cols, bytes_accessed=10 * rows * cols
        ),
        name="expected_users",
    )(core, shape_arg, rate_arg)


def items_kernel(shape_ref, rate_ref, exp_ref, total_ref):
    x = shape_ref[...]
    inv_rate = 1.0 / rate_ref[...]
    exp_ref[...] = exp_digamma(x, inv_rate).astype(BF16)
    part = jnp.sum(x * inv_rate, axis=0, keepdims=True)

    @pl.when(pl.program_id(0) == 0)
    def _():
        total_ref[...] = part

    @pl.when(pl.program_id(0) != 0)
    def _():
        total_ref[...] += part


def expected_items(shape_arg, rate_arg):
    rows, cols = shape_arg.shape
    block = min(rows, 128)
    spec = pl.BlockSpec((block, cols), lambda g: (g, 0))
    return pl.pallas_call(
        items_kernel,
        grid=(rows // block,),
        in_specs=[spec, spec],
        out_specs=[spec, pl.BlockSpec((1, cols), lambda g: (0, 0))],
        out_shape=[
            jax.ShapeDtypeStruct((rows, cols), BF16),
            jax.ShapeDtypeStruct((1, cols), F32),
        ],
        cost_estimate=pl.CostEstimate(
            flops=40 * rows * cols, transcendentals=3 * rows * cols, bytes_accessed=10 * rows * cols
        ),
        name="expected_items",
    )(shape_arg, rate_arg)


def dense_kernel(n_user, shard_tiles, chunk, rows, users_ref, items_ref, live_ref, me_ref, counts_ref, out_ref):
    g = pl.program_id(0)
    tile = counts_ref.shape[1]
    half = rows // 2
    piece = min(half, tile)

    @pl.when(g == 0)
    def _():
        out_ref[...] = jnp.zeros_like(out_ref)

    def place(t, carry):
        slot = g * chunk + t
        item = items_ref[slot]
        owner = lax.div(item, shard_tiles)
        column = (owner ^ me_ref[1]) * shard_tiles + lax.rem(item, shard_tiles)
        col = pl.multiple_of(column * tile, tile)
        for j in range(tile // piece):
            row = users_ref[slot] * tile + j * piece
            shard = lax.div(row, rows)
            within = lax.rem(row, rows)

            @pl.when(lax.div(within, half) == me_ref[2])
            def _():
                start = (shard ^ me_ref[0]) * half + lax.rem(within, half)
                start = pl.multiple_of(start, piece)
                value = counts_ref[t, j * piece : (j + 1) * piece, :].astype(F32).astype(BF16)
                out_ref[pl.ds(start, piece), pl.ds(col, tile)] = value

        return carry

    lax.fori_loop(0, jnp.clip(live_ref[0] - g * chunk, 0, chunk), place, 0)


def dense_counts(counts, users, items, live, me, rows, n_item, item_rows, n_user):
    slots, tile, _ = counts.shape
    chunk = 8
    shard_tiles = item_rows // n_user // tile
    out_rows = n_item * rows // 2
    return pl.pallas_call(
        functools.partial(dense_kernel, n_user, shard_tiles, chunk, rows),
        grid_spec=pltpu.PrefetchScalarGridSpec(
            num_scalar_prefetch=4,
            grid=(slots // chunk,),
            in_specs=[pl.BlockSpec((chunk, tile, tile), lambda g, *_: (g, 0, 0))],
            out_specs=pl.BlockSpec((out_rows, item_rows), lambda g, *_: (0, 0)),
        ),
        out_shape=jax.ShapeDtypeStruct((out_rows, item_rows), BF16),
        compiler_params=pltpu.CompilerParams(vmem_limit_bytes=12 * 1024 * 1024),
        cost_estimate=pl.CostEstimate(
            flops=slots * tile * tile,
            transcendentals=0,
            bytes_accessed=4 * slots * tile * tile + 2 * out_rows * item_rows,
        ),
        name="dense_counts",
    )(users, items, live, me, counts)


def stat_kernel(pieces, joined_in, joined_out, has_acc, at, *refs):
    refs = list(refs)
    take = lambda n: [refs.pop(0) for _ in range(n)]
    if joined_in:
        (both_ref,) = take(1)
        half = both_ref.shape[0] // 2
        mine = both_ref[:half, :]
        other = both_ref[half:, :]
    else:
        mine_ref, other_ref = take(2)
        half = mine_ref.shape[0]
        mine = mine_ref[...]
        other = other_ref[...]
    item_mine = take(pieces)
    item_other = take(pieces)
    (counts_ref,) = take(1)
    acc_mine_in = take(pieces) if has_acc else None
    acc_other_in = take(pieces) if has_acc else None
    stat_refs = take(1 if joined_out else 2)
    acc_mine = take(pieces)
    acc_other = take(pieces)
    total_mine = None
    total_other = None
    width = 256
    for p in range(pieces):
        rows = item_mine[p].shape[0]
        for c in range(rows // width):
            part = slice(c * width, (c + 1) * width)
            left = item_mine[p][part, :]
            right = item_other[p][part, :]
            norm = lax.dot_general(mine, left, DIMS_NT, preferred_element_type=F32)
            norm += lax.dot_general(other, right, DIMS_NT, preferred_element_type=F32)
            columns = slice(p * rows + c * width, p * rows + (c + 1) * width)
            grid = counts_ref[at * half : (at + 1) * half, columns].astype(F32)
            ratio = (grid / norm).astype(BF16)
            stat = jnp.dot(ratio, left, preferred_element_type=F32)
            total_mine = stat if total_mine is None else total_mine + stat
            stat = jnp.dot(ratio, right, preferred_element_type=F32)
            total_other = stat if total_other is None else total_other + stat
            update = lax.dot_general(mine, ratio, DIMS_TN, preferred_element_type=F32)
            if has_acc:
                update += acc_mine_in[p][:, part]
            acc_mine[p][:, part] = update.astype(acc_mine[p].dtype)
            update = lax.dot_general(other, ratio, DIMS_TN, preferred_element_type=F32)
            if has_acc:
                update += acc_other_in[p][:, part]
            acc_other[p][:, part] = update.astype(acc_other[p].dtype)
    if joined_out:
        stat_refs[0][:half, :] = total_mine.astype(stat_refs[0].dtype)
        stat_refs[0][half:, :] = total_other.astype(stat_refs[0].dtype)
    else:
        stat_refs[0][...] = total_mine.astype(stat_refs[0].dtype)
        stat_refs[1][...] = total_other.astype(stat_refs[1].dtype)


def statistics(at, users, item_mine, item_other, dense, acc, last, name):
    half_rows = users[0].shape[0] * len(users) // 2
    half = users[0].shape[1]
    pieces = len(item_mine)
    item_rows = dense.shape[1]
    piece_rows = item_rows // pieces
    args = [*users, *item_mine, *item_other, dense]
    if acc is not None:
        args += acc
    joined_out = at != 0 and not last
    if joined_out:
        out_shape = [jax.ShapeDtypeStruct((2 * half_rows, half), BF16)]
    else:
        out_shape = [jax.ShapeDtypeStruct((half_rows, half), BF16 if at else F32)] * 2
    n_stats = len(out_shape)
    for group in range(2):
        for p in range(pieces):
            kept = not last or (group == 0 and p == 0)
            out_shape.append(jax.ShapeDtypeStruct((half, piece_rows), F32 if kept else BF16))
    spec = pl.BlockSpec(memory_space=VMEM)
    out = pl.pallas_call(
        functools.partial(stat_kernel, pieces, len(users) == 1, joined_out, acc is not None, at),
        in_specs=[spec] * len(args),
        out_specs=[spec] * len(out_shape),
        out_shape=out_shape,
        compiler_params=pltpu.CompilerParams(vmem_limit_bytes=24 * 1024 * 1024),
        cost_estimate=pl.CostEstimate(
            flops=12 * half_rows * item_rows * half,
            transcendentals=half_rows * item_rows,
            bytes_accessed=8 * half_rows * half + 4 * item_rows * half + 2 * half_rows * item_rows,
        ),
        name=name,
    )(*args)
    return list(out[:n_stats]), list(out[n_stats:])


def finish_users_kernel(joined, core_ref, keep_ref, give_ref, own_ref, sum_ref, *refs):
    out_ref = refs[-1]
    g = pl.program_id(0)
    half = keep_ref.shape[0]

    @pl.when(g == 0)
    def _():
        total = own_ref[...]
        for k in range(joined):
            total += refs[k][:half, :].astype(F32)
        total += refs[joined][...].astype(F32)
        out_ref[...] = 0.3 + keep_ref[...].astype(F32) * total

    @pl.when(g == 1)
    def _():
        total = sum_ref[...].astype(F32) + refs[joined + 1][...].astype(F32)
        out_ref[...] = 0.3 + give_ref[...].astype(F32) * total


def finish_users(core, keep, give, own, other_sum, joined, same, cross):
    half_rows, half = keep.shape
    spec = pl.BlockSpec((half_rows, half), lambda g, c: (0, 0))
    joined_spec = pl.BlockSpec((2 * half_rows, half), lambda g, c: (0, 0))
    return pl.pallas_call(
        functools.partial(finish_users_kernel, len(joined)),
        grid_spec=pltpu.PrefetchScalarGridSpec(
            num_scalar_prefetch=1,
            grid=(2,),
            in_specs=[spec] * 4 + [joined_spec] * len(joined) + [spec] * 2,
            out_specs=pl.BlockSpec((half_rows, half), lambda g, c: (lax.rem(c[0] + g, 2), 0)),
        ),
        out_shape=jax.ShapeDtypeStruct((2 * half_rows, half), F32),
        cost_estimate=pl.CostEstimate(
            flops=8 * half_rows * half, transcendentals=0, bytes_accessed=24 * half_rows * half
        ),
        name="finish_users",
    )(core, keep, give, own, other_sum, *joined, same, cross)


def finish_items_kernel(n, exp_ref, own_ref, *refs):
    total = own_ref[...]
    for p in range(n):
        total += refs[p][...].astype(F32)
    refs[n][...] = 0.3 + exp_ref[...].astype(F32) * total.T


def finish_items(item_exp, own, came):
    rows, half = item_exp.shape
    block = min(rows, 256)
    spec = pl.BlockSpec((block, half), lambda g: (g, 0))
    acc_spec = pl.BlockSpec((half, block), lambda g: (0, g))
    return pl.pallas_call(
        functools.partial(finish_items_kernel, len(came)),
        grid=(rows // block,),
        in_specs=[spec] + [acc_spec] * (1 + len(came)),
        out_specs=spec,
        out_shape=jax.ShapeDtypeStruct((rows, half), F32),
        cost_estimate=pl.CostEstimate(flops=6 * rows * half, transcendentals=0, bytes_accessed=16 * rows * half),
        name="finish_items",
    )(item_exp, own, *came)


def move(x, axis, n, n_ka, distance, cross):
    if not cross:
        return lax.ppermute(x, axis, [(i, i ^ distance) for i in range(n)])
    pairs = [
        (i * n_ka + h, (i ^ distance) * n_ka + (n_ka - 1 - h)) for i in range(n) for h in range(n_ka)
    ]
    return lax.ppermute(x, (axis, "ka"), pairs)


def body(
    n_item,
    n_user,
    n_ka,
    counts,
    tile_user,
    tile_item,
    tile_live,
    theta_shape,
    theta_rate,
    user_activity,
    beta_shape,
    beta_rate,
    item_popularity,
):
    def sibling(x):
        return lax.ppermute(x, "ka", [(h, n_ka - 1 - h) for h in range(n_ka)])

    core = lax.axis_index("ka").astype(jnp.int32)[None]
    keep, give, theta_local = expected_users(core, theta_shape[0], theta_rate[0])
    beta_shape, beta_rate, keep, give = lax.optimization_barrier((beta_shape, beta_rate, keep, give))
    item_exp, beta_local = expected_items(beta_shape[0], beta_rate[0])
    half_rows = keep.shape[0]
    item_rows = item_exp.shape[0] * n_user

    came_give = sibling(give)
    users = {0: [keep, came_give]}
    for k in range(1, n_item):
        low = k & -k
        if k == 1:
            users[k] = [move(jnp.concatenate([keep, came_give]), "item", n_item, n_ka, k, False)]
        else:
            users[k] = [move(x, "item", n_item, n_ka, low, False) for x in users[k ^ low]]

    item_mine = [item_exp]
    for p in range(1, n_user):
        low = p & -p
        item_mine.append(move(item_mine[p ^ low], "user", n_user, n_ka, low, False))
    item_other = [sibling(x) for x in item_mine]

    me = jnp.stack([lax.axis_index(a) for a in ("item", "user", "ka")]).astype(jnp.int32)
    dense = dense_counts(
        counts[0, 0],
        tile_user[0, 0],
        tile_item[0, 0],
        tile_live[0],
        me,
        2 * half_rows,
        n_item,
        item_rows,
        n_user,
    )

    totals = jnp.concatenate([theta_local, beta_local], axis=0)
    hops = []
    for axis, n in (("user", n_user), ("item", n_item)):
        distance = 1
        while distance < n:
            hops.append((axis, n, distance))
            distance *= 2

    acc = None
    joined = []
    for k in range(n_item):
        last = k == n_item - 1
        stats, acc = statistics(k, users[k], item_mine, item_other, dense, acc, last, "statistics_%d" % k)
        if k < len(hops):
            totals, stats[-1] = lax.optimization_barrier((totals, stats[-1]))
            axis, n, distance = hops[k]
            totals = totals + move(totals, axis, n, n_ka, distance, False)
        if k == 0:
            own, other_sum = stats
        elif not last:
            joined.append(move(stats[0], "item", n_item, n_ka, k, False))
            other_sum = other_sum + joined[-1][half_rows:].astype(F32)
        else:
            same = move(stats[0], "item", n_item, n_ka, k, False)
            cross = move(stats[1], "item", n_item, n_ka, k, True)
    other_sum = sibling(other_sum.astype(BF16))

    came = [sibling(acc[n_user])]
    for p in range(1, n_user):
        came.append(move(acc[p], "user", n_user, n_ka, p, False))
        came.append(move(acc[n_user + p], "user", n_user, n_ka, p, True))
    theta_total = totals[0]
    beta_total = totals[1]

    new_theta_shape = finish_users(core, keep, give, own, other_sum, joined, same, cross)
    new_beta_shape = finish_items(item_exp, acc[0], came)
    new_theta_rate = user_activity[..., None] + beta_total
    new_beta_rate = item_popularity[..., None] + theta_total
    return (new_theta_shape[None], new_theta_rate, new_beta_shape[None], new_beta_rate)


def solution(mesh):
    in_specs = (
        P(("parts", "item"), "user", None, None, None),
        P(("parts", "item"), "user", None),
        P(("parts", "item"), "user", None),
        P(("parts", "item"), "user"),
        P(("parts", "user"), "item", "ka"),
        P(("parts", "user"), "item", "ka"),
        P(("parts", "user"), "item"),
        P(("parts", "item"), "user", "ka"),
        P(("parts", "item"), "user", "ka"),
        P(("parts", "item"), "user"),
    )
    out_specs = (
        P(("parts", "user"), "item", "ka"),
        P(("parts", "user"), "item", "ka"),
        P(("parts", "item"), "user", "ka"),
        P(("parts", "item"), "user", "ka"),
    )
    run = functools.partial(body, mesh.shape["item"], mesh.shape["user"], mesh.shape["ka"])
    return jax.shard_map(run, mesh=mesh, in_specs=in_specs, out_specs=out_specs, check_vma=False)
```

```python
import functools

import jax
import jax.numpy as jnp
from jax import lax
from jax.experimental import pallas as pl
from jax.experimental.pallas import tpu as pltpu
from jax.sharding import PartitionSpec as P

BF16 = jnp.bfloat16
F32 = jnp.float32
VMEM = pltpu.MemorySpace.VMEM
SMEM = pltpu.MemorySpace.SMEM
HBM = pltpu.MemorySpace.HBM
EXTRA = 16
MIB = 1024 * 1024
CHEAP = pl.CostEstimate(flops=1024, transcendentals=0, bytes_accessed=1024)
DIMS_NT = (((1,), (1,)), ((), ()))
DIMS_TN = (((0,), (0,)), ((), ()))


def pinned(x):
    return pltpu.with_memory_space_constraint(x, HBM)


def reciprocal(x):
    r = pl.reciprocal(x, approx=True)
    return r * (2.0 - x * r)


def exp_digamma(x, inv_rate):
    w = x * (x + 3.0)
    p = w * (w + 2.0)
    y = x + 4.0
    inv = reciprocal(y * p)
    iy = inv * p
    iy2 = iy * iy
    shift = (2.0 * x + 3.0) * (2.0 * w + 2.0) * (inv * y)
    series = iy * 0.5 + iy2 * (1.0 / 12.0 - iy2 * (1.0 / 120.0 - iy2 * (1.0 / 252.0)))
    return y * inv_rate * jnp.exp(-(series + shift))


def encode(values):
    row = lax.broadcasted_iota(jnp.int32, (EXTRA, values[0].shape[1]), 0)
    out = jnp.zeros(row.shape, F32)
    for i, rest in enumerate(values):
        for j in range(3):
            piece = rest.astype(BF16).astype(F32)
            rest = rest - piece
            out = jnp.where(row == 3 * i + j, piece, out)
    return out.astype(BF16)


def decode(block):
    block = block.astype(F32)
    return [block[3 * i : 3 * i + 1] + block[3 * i + 1 : 3 * i + 2] + block[3 * i + 2 : 3 * i + 3] for i in range(2)]


def chunk_copies(starts, chunk, refs, buffers, sems):
    copies = []
    for j, start in enumerate(starts):
        here = pl.ds(start, chunk)
        copies.append(
            [pltpu.make_async_copy(r.at[here], b.at[here], sems.at[i, j]) for i, (r, b) in enumerate(zip(refs, buffers))]
        )
    for group in copies:
        for copy in group:
            copy.start()
    return copies


def expected_kernel(chunk_u, chunk_i, theta_ref, trate_ref, beta_ref, brate_ref, *refs):
    both_ref, item_ref, pack_ref, theta_buf, trate_buf, beta_buf, brate_buf, user_sems, item_sems = refs
    core = lax.axis_index("ka")
    half = both_ref.shape[0] // 2
    rows = beta_ref.shape[0]
    steps = half // chunk_u
    starts = []
    for side in (1 - core, core):
        starts += [pl.multiple_of(side * half + j * chunk_u, chunk_u) for j in range(steps)]
    item_starts = list(range(0, rows, chunk_i))
    user_copies = chunk_copies(starts, chunk_u, (theta_ref, trate_ref), (theta_buf, trate_buf), user_sems)
    item_copies = chunk_copies(item_starts, chunk_i, (beta_ref, brate_ref), (beta_buf, brate_buf), item_sems)
    theta_total = jnp.zeros((1, both_ref.shape[1]), F32)
    for j, start in enumerate(starts):
        for copy in user_copies[j]:
            copy.wait()
        x = theta_buf[pl.ds(start, chunk_u), :]
        inv_rate = reciprocal(trate_buf[pl.ds(start, chunk_u), :])
        value = exp_digamma(x, inv_rate).astype(BF16)
        at = (j % steps) * chunk_u
        if j < steps:
            both_ref[half + at : half + at + chunk_u, :] = value
            pack_ref[at : at + chunk_u, :] = value
        else:
            both_ref[at : at + chunk_u, :] = value
        theta_total += jnp.sum(x * inv_rate, axis=0, keepdims=True)
    beta_total = jnp.zeros((1, both_ref.shape[1]), F32)
    for j, start in enumerate(item_starts):
        for copy in item_copies[j]:
            copy.wait()
        x = beta_buf[start : start + chunk_i, :]
        inv_rate = reciprocal(brate_buf[start : start + chunk_i, :])
        value = exp_digamma(x, inv_rate).astype(BF16)
        item_ref[start : start + chunk_i, :] = value
        pack_ref[half + start : half + start + chunk_i, :] = value
        beta_total += jnp.sum(x * inv_rate, axis=0, keepdims=True)
    extra = encode([theta_total, beta_total])
    item_ref[rows:, :] = extra
    pack_ref[half + rows :, :] = extra


def expected(theta, trate, beta, brate):
    rows, cols = theta.shape
    item_rows = beta.shape[0]
    half = rows // 2
    chunk_u = min(half, 128)
    chunk_i = min(item_rows, 128)
    shapes = [rows, item_rows + EXTRA, half + item_rows + EXTRA]
    return pl.pallas_call(
        functools.partial(expected_kernel, chunk_u, chunk_i),
        in_specs=[pl.BlockSpec(memory_space=HBM)] * 4,
        out_specs=[pl.BlockSpec(memory_space=VMEM)] * 3,
        out_shape=[jax.ShapeDtypeStruct((r, cols), BF16) for r in shapes],
        scratch_shapes=[
            pltpu.VMEM((rows, cols), F32),
            pltpu.VMEM((rows, cols), F32),
            pltpu.VMEM((item_rows, cols), F32),
            pltpu.VMEM((item_rows, cols), F32),
            pltpu.SemaphoreType.DMA((2, rows // chunk_u)),
            pltpu.SemaphoreType.DMA((2, item_rows // chunk_i)),
        ],
        compiler_params=pltpu.CompilerParams(vmem_limit_bytes=6 * MIB),
        cost_estimate=CHEAP,
        name="expected",
    )(pinned(theta), pinned(trate), pinned(beta), pinned(brate))


def dense_kernel(shard_tiles, chunk, rows, users_in, items_in, live_ref, counts_ref, out_ref, *scratch):
    users_ref, items_ref, buf, sems, index_sems = scratch
    tile = counts_ref.shape[1]
    half = rows // 2
    piece = min(half, tile)
    n_chunks = counts_ref.shape[0] // chunk
    copies = [
        pltpu.make_async_copy(
            counts_ref.at[pl.ds(c * chunk, chunk)], buf.at[pl.ds(c * chunk, chunk)], sems.at[c]
        )
        for c in range(n_chunks)
    ]
    index_copies = [
        pltpu.make_async_copy(users_in, users_ref, index_sems.at[0]),
        pltpu.make_async_copy(items_in, items_ref, index_sems.at[1]),
    ]
    for copy in index_copies + copies:
        copy.start()
    out_ref[...] = jnp.zeros_like(out_ref)
    for copy in index_copies:
        copy.wait()
    z = lax.axis_index("item")
    x = lax.axis_index("user")
    core = lax.axis_index("ka")
    live = live_ref[0]

    def place(slot, carry):
        item = items_ref[slot]
        owner = lax.div(item, shard_tiles)
        column = (owner ^ x) * shard_tiles + lax.rem(item, shard_tiles)
        col = pl.multiple_of(column * tile, tile)
        for j in range(tile // piece):
            row = users_ref[slot] * tile + j * piece
            shard = lax.div(row, rows)
            within = lax.rem(row, rows)

            @pl.when(lax.div(within, half) == core)
            def _():
                start = pl.multiple_of((shard ^ z) * half + lax.rem(within, half), piece)
                value = buf[slot, j * piece : (j + 1) * piece, :].astype(F32).astype(BF16)
                out_ref[pl.ds(start, piece), pl.ds(col, tile)] = value

        return carry

    for c in range(n_chunks):
        copies[c].wait()
        lax.fori_loop(c * chunk, jnp.clip(live, c * chunk, (c + 1) * chunk), place, 0)


def dense_counts(counts, users, items, live, rows, n_item, item_rows, n_user):
    slots, tile, _ = counts.shape
    chunk = 8
    out_rows = n_item * rows // 2
    return pl.pallas_call(
        functools.partial(dense_kernel, item_rows // n_user // tile, chunk, rows),
        in_specs=[pl.BlockSpec(memory_space=m) for m in (HBM, HBM, SMEM, HBM)],
        out_specs=pl.BlockSpec(memory_space=VMEM),
        out_shape=jax.ShapeDtypeStruct((out_rows, item_rows), BF16),
        scratch_shapes=[
            pltpu.SMEM(users.shape, jnp.int32),
            pltpu.SMEM(items.shape, jnp.int32),
            pltpu.VMEM((slots, tile, tile), jnp.int32),
            pltpu.SemaphoreType.DMA((slots // chunk,)),
            pltpu.SemaphoreType.DMA((2,)),
        ],
        compiler_params=pltpu.CompilerParams(vmem_limit_bytes=8 * MIB),
        cost_estimate=CHEAP,
        name="dense_counts",
    )(pinned(users), pinned(items), live, pinned(counts))


def stat_kernel(pieces, half, last, has_acc, at, *refs):
    refs = list(refs)
    take = lambda n: [refs.pop(0) for _ in range(n)]
    mine_ref, other_ref = take(2)
    mine = mine_ref[:half, :]
    other = other_ref[half : 2 * half, :] if at else other_ref[:half, :]
    item_mine = take(pieces)
    item_other = take(pieces)
    (counts_ref,) = take(1)
    (acc_in,) = take(1) if has_acc else (None,)
    joined_out = at != 0 and not last
    stat_refs = take(1 if joined_out else 2)
    acc_refs = take(2 * pieces if last else 1)
    cols = mine.shape[1]
    total_mine = None
    total_other = None
    width = 256
    for p in range(pieces):
        rows = item_mine[p].shape[0] - EXTRA
        skip = item_other[p].shape[0] - EXTRA - rows
        for c in range(rows // width):
            left = item_mine[p][c * width : (c + 1) * width, :]
            right = item_other[p][skip + c * width : skip + (c + 1) * width, :]
            norm = lax.dot_general(mine, left, DIMS_NT, preferred_element_type=F32)
            norm += lax.dot_general(other, right, DIMS_NT, preferred_element_type=F32)
            columns = slice(p * rows + c * width, p * rows + (c + 1) * width)
            grid = counts_ref[at * half : (at + 1) * half, columns].astype(F32)
            ratio = (grid * reciprocal(norm)).astype(BF16)
            stat = jnp.dot(ratio, left, preferred_element_type=F32)
            total_mine = stat if total_mine is None else total_mine + stat
            stat = jnp.dot(ratio, right, preferred_element_type=F32)
            total_other = stat if total_other is None else total_other + stat
            for i, factors in enumerate((mine, other)):
                update = lax.dot_general(factors, ratio, DIMS_TN, preferred_element_type=F32)
                if has_acc:
                    update += acc_in[i * cols : (i + 1) * cols, columns]
                if last:
                    target = acc_refs[i * pieces + p]
                    target[:, c * width : (c + 1) * width] = update.astype(target.dtype)
                else:
                    acc_refs[0][i * cols : (i + 1) * cols, columns] = update
    if joined_out:
        stat_refs[0][:half, :] = total_mine.astype(stat_refs[0].dtype)
        stat_refs[0][half : 2 * half, :] = total_other.astype(stat_refs[0].dtype)
    else:
        stat_refs[0][:half, :] = total_mine.astype(stat_refs[0].dtype)
        stat_refs[1][...] = total_other.astype(stat_refs[1].dtype)
    if at != 0:
        stat_refs[0][-EXTRA:, :] = encode(row_totals(item_mine))


def row_totals(item_refs):
    sums = None
    for ref in item_refs:
        came = decode(ref[-EXTRA:, :])
        sums = came if sums is None else [a + b for a, b in zip(sums, came)]
    return sums


def statistics(at, users, item_mine, item_other, dense, acc, last, half_rows):
    half = users[0].shape[1]
    item_rows = dense.shape[1]
    args = [*users, *item_mine, *item_other, dense]
    if acc is not None:
        args.append(acc)
    if at and not last:
        out_shape = [jax.ShapeDtypeStruct((2 * half_rows + EXTRA, half), BF16)]
    elif at:
        out_shape = [jax.ShapeDtypeStruct((half_rows + e, half), BF16) for e in (EXTRA, 0)]
    else:
        out_shape = [jax.ShapeDtypeStruct((half_rows, half), F32)] * 2
    n_stats = len(out_shape)
    if last:
        pieces = len(item_mine)
        out_shape += [
            jax.ShapeDtypeStruct((half, item_rows // pieces), BF16 if i else F32) for i in range(2 * pieces)
        ]
    else:
        out_shape.append(jax.ShapeDtypeStruct((2 * half, item_rows), F32))
    spec = pl.BlockSpec(memory_space=VMEM)
    out = pl.pallas_call(
        functools.partial(stat_kernel, len(item_mine), half_rows, last, acc is not None, at),
        in_specs=[spec] * len(args),
        out_specs=[spec] * len(out_shape),
        out_shape=out_shape,
        compiler_params=pltpu.CompilerParams(vmem_limit_bytes=16 * MIB),
        cost_estimate=CHEAP,
        name="statistics_%d" % at,
    )(*args)
    return list(out[:n_stats]), list(out[n_stats:])


def finish_users_kernel(n_joined, pieces, *refs):
    refs = list(refs)
    take = lambda n: [refs.pop(0) for _ in range(n)]
    both_ref, own_ref, sum_ref = take(3)
    joined = take(n_joined)
    same_ref, cross_ref = take(2)
    item_refs = take(pieces)
    activity_ref, popularity_ref = take(2)
    outs = take(3)
    bufs = take(3)
    (sems,) = take(1)
    core = lax.axis_index("ka")
    half = own_ref.shape[0]
    copies = []

    total = own_ref[...]
    for ref in joined:
        total += ref[:half, :].astype(F32)
    total += same_ref[:half, :].astype(F32)
    start = pl.multiple_of(core * half, half)
    bufs[0][pl.ds(start, half), :] = 0.3 + both_ref[:half, :].astype(F32) * total
    copies.append(pltpu.make_async_copy(bufs[0].at[pl.ds(start, half)], outs[0].at[pl.ds(start, half)], sems.at[0]))
    copies[-1].start()

    total = sum_ref[...].astype(F32) + cross_ref[...].astype(F32)
    start = pl.multiple_of((1 - core) * half, half)
    bufs[0][pl.ds(start, half), :] = 0.3 + both_ref[half:, :].astype(F32) * total
    copies.append(pltpu.make_async_copy(bufs[0].at[pl.ds(start, half)], outs[0].at[pl.ds(start, half)], sems.at[1]))
    copies[-1].start()

    theta_total, beta_total = row_totals(item_refs)
    for ref in joined + [same_ref]:
        came = decode(ref[-EXTRA:, :])
        theta_total += came[0]
        beta_total += came[1]
    for i, (column_ref, total) in enumerate(((activity_ref, beta_total), (popularity_ref, theta_total))):
        rows = column_ref.shape[1]
        column = jnp.broadcast_to(column_ref[...], (total.shape[1], rows)).T
        bufs[1 + i][...] = column + total
        copies.append(pltpu.make_async_copy(bufs[1 + i], outs[1 + i], sems.at[2 + i]))
        copies[-1].start()
    for copy in copies:
        copy.wait()


def finish_users(both, own, other_sum, joined, same, cross, items, activity, popularity):
    rows, half = both.shape
    args = [both, own, other_sum, *joined, same, cross, *items, activity, popularity]
    out_shape = [
        jax.ShapeDtypeStruct((rows, half), F32),
        jax.ShapeDtypeStruct((activity.shape[1], half), F32),
        jax.ShapeDtypeStruct((popularity.shape[1], half), F32),
    ]
    return pl.pallas_call(
        functools.partial(finish_users_kernel, len(joined), len(items)),
        in_specs=[pl.BlockSpec(memory_space=VMEM)] * len(args),
        out_specs=[pl.BlockSpec(memory_space=HBM)] * 3,
        out_shape=out_shape,
        scratch_shapes=[pltpu.VMEM(o.shape, F32) for o in out_shape] + [pltpu.SemaphoreType.DMA((4,))],
        compiler_params=pltpu.CompilerParams(vmem_limit_bytes=8 * MIB),
        cost_estimate=CHEAP,
        name="finish_users",
    )(*args)


def finish_items_kernel(n, exp_ref, own_ref, *refs):
    out_ref, buf, sems = refs[n:]
    rows = out_ref.shape[0]
    chunk = min(rows, 256)
    copies = []
    for j in range(rows // chunk):
        part = slice(j * chunk, (j + 1) * chunk)
        total = own_ref[:, part]
        for p in range(n):
            total += refs[p][:, part].astype(F32)
        buf[part, :] = 0.3 + exp_ref[part, :].astype(F32) * total.T
        here = pl.ds(j * chunk, chunk)
        copies.append(pltpu.make_async_copy(buf.at[here], out_ref.at[here], sems.at[j]))
        copies[-1].start()
    for copy in copies:
        copy.wait()


def finish_items(item_exp, own, came):
    half, rows = own.shape
    return pl.pallas_call(
        functools.partial(finish_items_kernel, len(came)),
        in_specs=[pl.BlockSpec(memory_space=VMEM)] * (2 + len(came)),
        out_specs=pl.BlockSpec(memory_space=HBM),
        out_shape=jax.ShapeDtypeStruct((rows, half), F32),
        scratch_shapes=[pltpu.VMEM((rows, half), F32), pltpu.SemaphoreType.DMA((rows // min(rows, 256),))],
        compiler_params=pltpu.CompilerParams(vmem_limit_bytes=6 * MIB),
        cost_estimate=CHEAP,
        name="finish_items",
    )(item_exp, own, *came)


def move(x, axis, n, n_ka, distance, cross):
    if not cross:
        return lax.ppermute(x, axis, [(i, i ^ distance) for i in range(n)])
    pairs = [
        (i * n_ka + h, (i ^ distance) * n_ka + (n_ka - 1 - h)) for i in range(n) for h in range(n_ka)
    ]
    return lax.ppermute(x, (axis, "ka"), pairs)


def body(
    n_item,
    n_user,
    n_ka,
    counts,
    tile_user,
    tile_item,
    tile_live,
    theta_shape,
    theta_rate,
    user_activity,
    beta_shape,
    beta_rate,
    item_popularity,
):
    def sibling(x):
        return lax.ppermute(x, "ka", [(h, n_ka - 1 - h) for h in range(n_ka)])

    def along_item(x, distance, cross):
        return move(x, "item", n_item, n_ka, distance, cross)

    both, item_exp, pack = expected(theta_shape[0], theta_rate[0], beta_shape[0], beta_rate[0])
    came_pack = sibling(pack)
    rows = both.shape[0]
    half_rows = rows // 2
    item_rows = beta_shape.shape[1] * n_user

    shards = [both]
    for k in range(1, n_item):
        low = k & -k
        shards.append(along_item(shards[k ^ low], low, False))
    users = [[both, came_pack]] + [[x, sibling(x)] for x in shards[1:]]

    item_mine = [item_exp]
    item_other = [came_pack]
    for p in range(1, n_user):
        item_mine.append(move(item_exp, "user", n_user, n_ka, p, False))
        item_other.append(move(item_exp, "user", n_user, n_ka, p, True))

    dense = dense_counts(
        counts[0, 0],
        tile_user[0, 0],
        tile_item[0, 0],
        tile_live[0],
        rows,
        n_item,
        item_rows,
        n_user,
    )

    order = sorted(range(1, n_item - 1), key=lambda k: (k & (k - 1) != 0, -k if k & (k - 1) == 0 else k))
    acc = None
    joined = []
    for k in order + [0, n_item - 1]:
        last = k == n_item - 1
        stats, accs = statistics(k, users[k], item_mine, item_other, dense, acc, last, half_rows)
        acc = accs[0]
        if k == 0:
            own, own_other = stats
        elif not last:
            joined.append(along_item(stats[0], k, False))
        else:
            same = along_item(stats[0], k, False)
            cross = along_item(stats[1], k, True)
    came = [sibling(accs[n_user])]
    for p in range(1, n_user):
        came.append(move(accs[p], "user", n_user, n_ka, p, False))
        came.append(move(accs[n_user + p], "user", n_user, n_ka, p, True))
    other_sum = own_other
    for x in joined:
        other_sum = other_sum + x[half_rows : 2 * half_rows].astype(F32)
    other_sum = sibling(other_sum.astype(BF16))

    new_beta_shape = finish_items(item_exp, accs[0], came)
    new_theta_shape, new_theta_rate, new_beta_rate = finish_users(
        both, own, other_sum, joined, same, cross, item_mine, user_activity, item_popularity
    )
    return (new_theta_shape[None], new_theta_rate[None], new_beta_shape[None], new_beta_rate[None])


def solution(mesh):
    in_specs = (
        P(("parts", "item"), "user", None, None, None),
        P(("parts", "item"), "user", None),
        P(("parts", "item"), "user", None),
        P(("parts", "item"), "user"),
        P(("parts", "user"), "item", "ka"),
        P(("parts", "user"), "item", "ka"),
        P(("parts", "user"), "item"),
        P(("parts", "item"), "user", "ka"),
        P(("parts", "item"), "user", "ka"),
        P(("parts", "item"), "user"),
    )
    out_specs = (
        P(("parts", "user"), "item", "ka"),
        P(("parts", "user"), "item", "ka"),
        P(("parts", "item"), "user", "ka"),
        P(("parts", "item"), "user", "ka"),
    )
    run = functools.partial(body, mesh.shape["item"], mesh.shape["user"], mesh.shape["ka"])
    return jax.shard_map(run, mesh=mesh, in_specs=in_specs, out_specs=out_specs, check_vma=False)
```

```python
import functools

import jax
import jax.numpy as jnp
from jax import lax
from jax.experimental import pallas as pl
from jax.experimental.pallas import tpu as pltpu
from jax.sharding import PartitionSpec as P

BF16 = jnp.bfloat16
F32 = jnp.float32
VMEM = pltpu.MemorySpace.VMEM
SMEM = pltpu.MemorySpace.SMEM
HBM = pltpu.MemorySpace.HBM
EXTRA = 16
MIB = 1024 * 1024
CHEAP = pl.CostEstimate(flops=1024, transcendentals=0, bytes_accessed=1024)
DIMS_NT = (((1,), (1,)), ((), ()))
DIMS_TN = (((0,), (0,)), ((), ()))


def pinned(x):
    return pltpu.with_memory_space_constraint(x, HBM)


def reciprocal(x):
    r = pl.reciprocal(x, approx=True)
    return r * (2.0 - x * r)


def exp_digamma(x, inv_rate):
    w = x * (x + 3.0)
    p = w * (w + 2.0)
    y = x + 4.0
    inv = reciprocal(y * p)
    iy = inv * p
    iy2 = iy * iy
    shift = (2.0 * x + 3.0) * (2.0 * w + 2.0) * (inv * y)
    series = iy * 0.5 + iy2 * (1.0 / 12.0 - iy2 * (1.0 / 120.0 - iy2 * (1.0 / 252.0)))
    return y * inv_rate * jnp.exp(-(series + shift))


def encode(values):
    row = lax.broadcasted_iota(jnp.int32, (EXTRA, values[0].shape[1]), 0)
    out = jnp.zeros(row.shape, F32)
    for i, rest in enumerate(values):
        for j in range(3):
            piece = rest.astype(BF16).astype(F32)
            rest = rest - piece
            out = jnp.where(row == 3 * i + j, piece, out)
    return out.astype(BF16)


def decode(block):
    block = block.astype(F32)
    return [block[3 * i : 3 * i + 1] + block[3 * i + 1 : 3 * i + 2] + block[3 * i + 2 : 3 * i + 3] for i in range(2)]


def chunk_copies(starts, chunk, refs, buffers, sems):
    copies = []
    for j, start in enumerate(starts):
        here = pl.ds(start, chunk)
        copies.append(
            [pltpu.make_async_copy(r.at[here], b.at[here], sems.at[i, j]) for i, (r, b) in enumerate(zip(refs, buffers))]
        )
    for group in copies:
        for copy in group:
            copy.start()
    return copies


def expected_kernel(chunk_u, chunk_i, theta_ref, trate_ref, beta_ref, brate_ref, *refs):
    both_ref, item_ref, pack_ref, theta_buf, trate_buf, beta_buf, brate_buf, user_sems, item_sems = refs
    core = lax.axis_index("ka")
    half = both_ref.shape[0] // 2
    rows = beta_ref.shape[0]
    steps = half // chunk_u
    starts = []
    for side in (1 - core, core):
        starts += [pl.multiple_of(side * half + j * chunk_u, chunk_u) for j in range(steps)]
    item_starts = list(range(0, rows, chunk_i))
    user_copies = chunk_copies(starts, chunk_u, (theta_ref, trate_ref), (theta_buf, trate_buf), user_sems)
    item_copies = chunk_copies(item_starts, chunk_i, (beta_ref, brate_ref), (beta_buf, brate_buf), item_sems)
    theta_total = jnp.zeros((1, both_ref.shape[1]), F32)
    for j, start in enumerate(starts):
        for copy in user_copies[j]:
            copy.wait()
        x = theta_buf[pl.ds(start, chunk_u), :]
        inv_rate = reciprocal(trate_buf[pl.ds(start, chunk_u), :])
        value = exp_digamma(x, inv_rate).astype(BF16)
        at = (j % steps) * chunk_u
        if j < steps:
            both_ref[half + at : half + at + chunk_u, :] = value
            pack_ref[at : at + chunk_u, :] = value
        else:
            both_ref[at : at + chunk_u, :] = value
        theta_total += jnp.sum(x * inv_rate, axis=0, keepdims=True)
    beta_total = jnp.zeros((1, both_ref.shape[1]), F32)
    for j, start in enumerate(item_starts):
        for copy in item_copies[j]:
            copy.wait()
        x = beta_buf[start : start + chunk_i, :]
        inv_rate = reciprocal(brate_buf[start : start + chunk_i, :])
        value = exp_digamma(x, inv_rate).astype(BF16)
        item_ref[start : start + chunk_i, :] = value
        pack_ref[half + start : half + start + chunk_i, :] = value
        beta_total += jnp.sum(x * inv_rate, axis=0, keepdims=True)
    extra = encode([theta_total, beta_total])
    item_ref[rows:, :] = extra
    pack_ref[half + rows :, :] = extra


def expected(theta, trate, beta, brate):
    rows, cols = theta.shape
    item_rows = beta.shape[0]
    half = rows // 2
    chunk_u = min(half, 128)
    chunk_i = min(item_rows, 128)
    shapes = [rows, item_rows + EXTRA, half + item_rows + EXTRA]
    return pl.pallas_call(
        functools.partial(expected_kernel, chunk_u, chunk_i),
        in_specs=[pl.BlockSpec(memory_space=HBM)] * 4,
        out_specs=[pl.BlockSpec(memory_space=VMEM)] * 3,
        out_shape=[jax.ShapeDtypeStruct((r, cols), BF16) for r in shapes],
        scratch_shapes=[
            pltpu.VMEM((rows, cols), F32),
            pltpu.VMEM((rows, cols), F32),
            pltpu.VMEM((item_rows, cols), F32),
            pltpu.VMEM((item_rows, cols), F32),
            pltpu.SemaphoreType.DMA((2, rows // chunk_u)),
            pltpu.SemaphoreType.DMA((2, item_rows // chunk_i)),
        ],
        compiler_params=pltpu.CompilerParams(vmem_limit_bytes=6 * MIB),
        cost_estimate=CHEAP,
        name="expected",
    )(pinned(theta), pinned(trate), pinned(beta), pinned(brate))


def dense_kernel(shard_tiles, chunk, rows, users_in, items_in, live_ref, counts_ref, out_ref, *scratch):
    users_ref, items_ref, buf, sems, index_sems = scratch
    tile = counts_ref.shape[1]
    half = rows // 2
    piece = min(half, tile)
    n_chunks = counts_ref.shape[0] // chunk
    copies = [
        pltpu.make_async_copy(
            counts_ref.at[pl.ds(c * chunk, chunk)], buf.at[pl.ds(c * chunk, chunk)], sems.at[c]
        )
        for c in range(n_chunks)
    ]
    index_copies = [
        pltpu.make_async_copy(users_in, users_ref, index_sems.at[0]),
        pltpu.make_async_copy(items_in, items_ref, index_sems.at[1]),
    ]
    for copy in index_copies + copies:
        copy.start()
    out_ref[...] = jnp.zeros_like(out_ref)
    for copy in index_copies:
        copy.wait()
    z = lax.axis_index("item")
    x = lax.axis_index("user")
    core = lax.axis_index("ka")
    live = live_ref[0]

    def place(slot, carry):
        item = items_ref[slot]
        owner = lax.div(item, shard_tiles)
        column = (owner ^ x) * shard_tiles + lax.rem(item, shard_tiles)
        col = pl.multiple_of(column * tile, tile)
        for j in range(tile // piece):
            row = users_ref[slot] * tile + j * piece
            shard = lax.div(row, rows)
            within = lax.rem(row, rows)

            @pl.when(lax.div(within, half) == core)
            def _():
                start = pl.multiple_of((shard ^ z) * half + lax.rem(within, half), piece)
                value = buf[slot, j * piece : (j + 1) * piece, :].astype(F32).astype(BF16)
                out_ref[pl.ds(start, piece), pl.ds(col, tile)] = value

        return carry

    for c in range(n_chunks):
        copies[c].wait()
        lax.fori_loop(c * chunk, jnp.clip(live, c * chunk, (c + 1) * chunk), place, 0)


def dense_counts(counts, users, items, live, rows, n_item, item_rows, n_user):
    slots, tile, _ = counts.shape
    chunk = 8
    out_rows = n_item * rows // 2
    return pl.pallas_call(
        functools.partial(dense_kernel, item_rows // n_user // tile, chunk, rows),
        in_specs=[pl.BlockSpec(memory_space=m) for m in (HBM, HBM, SMEM, HBM)],
        out_specs=pl.BlockSpec(memory_space=VMEM),
        out_shape=jax.ShapeDtypeStruct((out_rows, item_rows), BF16),
        scratch_shapes=[
            pltpu.SMEM(users.shape, jnp.int32),
            pltpu.SMEM(items.shape, jnp.int32),
            pltpu.VMEM((slots, tile, tile), jnp.int32),
            pltpu.SemaphoreType.DMA((slots // chunk,)),
            pltpu.SemaphoreType.DMA((2,)),
        ],
        compiler_params=pltpu.CompilerParams(vmem_limit_bytes=8 * MIB),
        cost_estimate=CHEAP,
        name="dense_counts",
    )(pinned(users), pinned(items), live, pinned(counts))


def stat_kernel(pieces, half, last, has_acc, at, *refs):
    refs = list(refs)
    take = lambda n: [refs.pop(0) for _ in range(n)]
    mine_ref, other_ref = take(2)
    mine = mine_ref[:half, :]
    other = other_ref[half : 2 * half, :] if at else other_ref[:half, :]
    item_mine = take(pieces)
    item_other = take(pieces)
    (counts_ref,) = take(1)
    (acc_in,) = take(1) if has_acc else (None,)
    stat_refs = take(1 if at else 2)
    acc_refs = take(1 + pieces if last else 1)
    cols = mine.shape[1]
    total_mine = None
    total_other = None
    width = 256
    for p in range(pieces):
        rows = item_mine[p].shape[0] - EXTRA
        skip = item_other[p].shape[0] - EXTRA - rows
        for c in range(rows // width):
            left = item_mine[p][c * width : (c + 1) * width, :]
            right = item_other[p][skip + c * width : skip + (c + 1) * width, :]
            norm = lax.dot_general(mine, left, DIMS_NT, preferred_element_type=F32)
            norm += lax.dot_general(other, right, DIMS_NT, preferred_element_type=F32)
            columns = slice(p * rows + c * width, p * rows + (c + 1) * width)
            grid = counts_ref[at * half : (at + 1) * half, columns].astype(F32)
            ratio = (grid * reciprocal(norm)).astype(BF16)
            stat = jnp.dot(ratio, left, preferred_element_type=F32)
            total_mine = stat if total_mine is None else total_mine + stat
            stat = jnp.dot(ratio, right, preferred_element_type=F32)
            total_other = stat if total_other is None else total_other + stat
            for i, factors in enumerate((mine, other)):
                update = lax.dot_general(factors, ratio, DIMS_TN, preferred_element_type=F32)
                if has_acc:
                    update += acc_in[i * cols : (i + 1) * cols, columns]
                if last and i == 0:
                    acc_refs[0][:, columns] = update
                elif last:
                    acc_refs[1 + p][:, c * width : (c + 1) * width] = update.astype(BF16)
                else:
                    acc_refs[0][i * cols : (i + 1) * cols, columns] = update
    if at:
        stat_refs[0][:half, :] = total_mine.astype(BF16)
        stat_refs[0][half : 2 * half, :] = total_other.astype(BF16)
        stat_refs[0][2 * half :, :] = encode(row_totals(item_mine))
    else:
        stat_refs[0][...] = total_mine
        stat_refs[1][...] = total_other


def row_totals(item_refs):
    sums = None
    for ref in item_refs:
        came = decode(ref[-EXTRA:, :])
        sums = came if sums is None else [a + b for a, b in zip(sums, came)]
    return sums


def statistics(at, users, item_mine, item_other, dense, acc, last, half_rows):
    half = users[0].shape[1]
    item_rows = dense.shape[1]
    args = [*users, *item_mine, *item_other, dense]
    if acc is not None:
        args.append(acc)
    if at:
        out_shape = [jax.ShapeDtypeStruct((2 * half_rows + EXTRA, half), BF16)]
    else:
        out_shape = [jax.ShapeDtypeStruct((half_rows, half), F32)] * 2
    n_stats = len(out_shape)
    if last:
        out_shape.append(jax.ShapeDtypeStruct((half, item_rows), F32))
        out_shape += [jax.ShapeDtypeStruct((half, item_rows // len(item_mine)), BF16) for _ in item_mine]
    else:
        out_shape.append(jax.ShapeDtypeStruct((2 * half, item_rows), F32))
    spec = pl.BlockSpec(memory_space=VMEM)
    out = pl.pallas_call(
        functools.partial(stat_kernel, len(item_mine), half_rows, last, acc is not None, at),
        in_specs=[spec] * len(args),
        out_specs=[spec] * len(out_shape),
        out_shape=out_shape,
        compiler_params=pltpu.CompilerParams(vmem_limit_bytes=16 * MIB),
        cost_estimate=CHEAP,
        name="statistics_%d" % at,
    )(*args)
    return list(out[:n_stats]), list(out[n_stats:])


def merge_items_kernel(p, mine_ref, came_ref, out_ref):
    width = out_ref.shape[1]
    out_ref[...] = (mine_ref[:, p * width : (p + 1) * width] + came_ref[...].astype(F32)).astype(BF16)


def merge_items(p, mine, came):
    return pl.pallas_call(
        functools.partial(merge_items_kernel, p),
        in_specs=[pl.BlockSpec(memory_space=VMEM)] * 2,
        out_specs=pl.BlockSpec(memory_space=VMEM),
        out_shape=jax.ShapeDtypeStruct(came.shape, BF16),
        compiler_params=pltpu.CompilerParams(vmem_limit_bytes=2 * MIB),
        cost_estimate=CHEAP,
        name="merge_items",
    )(mine, came)


def finish_users_kernel(n_joined, pieces, *refs):
    refs = list(refs)
    take = lambda n: [refs.pop(0) for _ in range(n)]
    both_ref, own_ref, sum_ref = take(3)
    joined = take(n_joined)
    (last_ref,) = take(1)
    item_refs = take(pieces)
    activity_ref, popularity_ref = take(2)
    outs = take(3)
    bufs = take(3)
    (sems,) = take(1)
    core = lax.axis_index("ka")
    half = own_ref.shape[0]
    copies = []

    total = own_ref[...]
    for ref in joined:
        total += ref[:half, :].astype(F32)
    start = pl.multiple_of(core * half, half)
    bufs[0][pl.ds(start, half), :] = 0.3 + both_ref[:half, :].astype(F32) * total
    copies.append(pltpu.make_async_copy(bufs[0].at[pl.ds(start, half)], outs[0].at[pl.ds(start, half)], sems.at[0]))
    copies[-1].start()

    total = sum_ref[...].astype(F32) + last_ref[...].astype(F32)
    start = pl.multiple_of((1 - core) * half, half)
    bufs[0][pl.ds(start, half), :] = 0.3 + both_ref[half:, :].astype(F32) * total
    copies.append(pltpu.make_async_copy(bufs[0].at[pl.ds(start, half)], outs[0].at[pl.ds(start, half)], sems.at[1]))
    copies[-1].start()

    theta_total, beta_total = row_totals(item_refs)
    for ref in joined:
        came = decode(ref[-EXTRA:, :])
        theta_total += came[0]
        beta_total += came[1]
    for i, (column_ref, total) in enumerate(((activity_ref, beta_total), (popularity_ref, theta_total))):
        rows = column_ref.shape[1]
        column = jnp.broadcast_to(column_ref[...], (total.shape[1], rows)).T
        bufs[1 + i][...] = column + total
        copies.append(pltpu.make_async_copy(bufs[1 + i], outs[1 + i], sems.at[2 + i]))
        copies[-1].start()
    for copy in copies:
        copy.wait()


def finish_users(both, own, other_sum, joined, other_last, items, activity, popularity):
    rows, half = both.shape
    args = [both, own, other_sum, *joined, other_last, *items, activity, popularity]
    out_shape = [
        jax.ShapeDtypeStruct((rows, half), F32),
        jax.ShapeDtypeStruct((activity.shape[1], half), F32),
        jax.ShapeDtypeStruct((popularity.shape[1], half), F32),
    ]
    return pl.pallas_call(
        functools.partial(finish_users_kernel, len(joined), len(items)),
        in_specs=[pl.BlockSpec(memory_space=VMEM)] * len(args),
        out_specs=[pl.BlockSpec(memory_space=HBM)] * 3,
        out_shape=out_shape,
        scratch_shapes=[pltpu.VMEM(o.shape, F32) for o in out_shape] + [pltpu.SemaphoreType.DMA((4,))],
        compiler_params=pltpu.CompilerParams(vmem_limit_bytes=8 * MIB),
        cost_estimate=CHEAP,
        name="finish_users",
    )(*args)


def finish_items_kernel(n, exp_ref, own_ref, *refs):
    out_ref, buf, sems = refs[n:]
    rows = out_ref.shape[0]
    chunk = min(rows, 256)
    copies = []
    for j in range(rows // chunk):
        part = slice(j * chunk, (j + 1) * chunk)
        total = own_ref[:, part]
        for p in range(n):
            total += refs[p][:, part].astype(F32)
        buf[part, :] = 0.3 + exp_ref[part, :].astype(F32) * total.T
        here = pl.ds(j * chunk, chunk)
        copies.append(pltpu.make_async_copy(buf.at[here], out_ref.at[here], sems.at[j]))
        copies[-1].start()
    for copy in copies:
        copy.wait()


def finish_items(item_exp, own, came):
    half, rows = came[0].shape
    return pl.pallas_call(
        functools.partial(finish_items_kernel, len(came)),
        in_specs=[pl.BlockSpec(memory_space=VMEM)] * (2 + len(came)),
        out_specs=pl.BlockSpec(memory_space=HBM),
        out_shape=jax.ShapeDtypeStruct((rows, half), F32),
        scratch_shapes=[pltpu.VMEM((rows, half), F32), pltpu.SemaphoreType.DMA((rows // min(rows, 256),))],
        compiler_params=pltpu.CompilerParams(vmem_limit_bytes=6 * MIB),
        cost_estimate=CHEAP,
        name="finish_items",
    )(item_exp, own, *came)


def after(x, y):
    return lax.optimization_barrier((x, y))[0]


def move(x, axis, n, n_ka, distance, cross):
    if not cross:
        return lax.ppermute(x, axis, [(i, i ^ distance) for i in range(n)])
    pairs = [
        (i * n_ka + h, (i ^ distance) * n_ka + (n_ka - 1 - h)) for i in range(n) for h in range(n_ka)
    ]
    return lax.ppermute(x, (axis, "ka"), pairs)


def body(
    n_item,
    n_user,
    n_ka,
    counts,
    tile_user,
    tile_item,
    tile_live,
    theta_shape,
    theta_rate,
    user_activity,
    beta_shape,
    beta_rate,
    item_popularity,
):
    def sibling(x):
        return lax.ppermute(x, "ka", [(h, n_ka - 1 - h) for h in range(n_ka)])

    def along_item(x, distance, cross):
        return move(x, "item", n_item, n_ka, distance, cross)

    both, item_exp, pack = expected(theta_shape[0], theta_rate[0], beta_shape[0], beta_rate[0])
    rows = both.shape[0]
    half_rows = rows // 2
    item_rows = beta_shape.shape[1] * n_user
    dense = dense_counts(
        counts[0, 0],
        tile_user[0, 0],
        tile_item[0, 0],
        tile_live[0],
        rows,
        n_item,
        item_rows,
        n_user,
    )
    pack, dense = lax.optimization_barrier((pack, dense))
    came_pack = sibling(pack)

    shards = [both]
    for k in range(1, n_item):
        low = k & -k
        shards.append(along_item(shards[k ^ low], low, False))
    users = [[both, came_pack]] + [[x, sibling(x)] for x in shards[1:-1]]

    item_mine = [item_exp]
    for p in range(1, n_user):
        low = p & -p
        item_mine.append(move(item_mine[p ^ low], "user", n_user, n_ka, low, False))
    item_other = [came_pack] + [sibling(x) for x in item_mine[1:]]

    order = sorted(range(1, n_item - 1), key=lambda k: (k & (k - 1) != 0, -k if k & (k - 1) == 0 else k))
    acc = None
    joined = []
    for k in order + [0, n_item - 1]:
        last = k == n_item - 1
        if last:
            users.append([shards[-1], sibling(after(shards[-1], latest))])
        stats, accs = statistics(k, users[k], item_mine, item_other, dense, acc, last, half_rows)
        acc = accs[0]
        if k == 0:
            own, own_other = stats
        else:
            joined.append(along_item(stats[0], k, False))
            if k == order[0]:
                latest = stats[0]

    came = [sibling(accs[1])]
    for p in range(1, n_user):
        came.append(move(merge_items(p, acc, sibling(accs[1 + p])), "user", n_user, n_ka, p, False))
    new_beta_shape = finish_items(item_exp, acc, came)

    other_sum = own_other
    for x in joined[:-1]:
        other_sum = lax.optimization_barrier(other_sum + x[half_rows:rows].astype(F32))
    other_sum = sibling(other_sum.astype(BF16))
    other_last = sibling(after(joined[-1], other_sum)[half_rows:rows])
    other_last = after(other_last, new_beta_shape)
    new_theta_shape, new_theta_rate, new_beta_rate = finish_users(
        both, own, other_sum, joined, other_last, item_mine, user_activity, item_popularity
    )
    return (new_theta_shape[None], new_theta_rate[None], new_beta_shape[None], new_beta_rate[None])


def solution(mesh):
    in_specs = (
        P(("parts", "item"), "user", None, None, None),
        P(("parts", "item"), "user", None),
        P(("parts", "item"), "user", None),
        P(("parts", "item"), "user"),
        P(("parts", "user"), "item", "ka"),
        P(("parts", "user"), "item", "ka"),
        P(("parts", "user"), "item"),
        P(("parts", "item"), "user", "ka"),
        P(("parts", "item"), "user", "ka"),
        P(("parts", "item"), "user"),
    )
    out_specs = (
        P(("parts", "user"), "item", "ka"),
        P(("parts", "user"), "item", "ka"),
        P(("parts", "item"), "user", "ka"),
        P(("parts", "item"), "user", "ka"),
    )
    run = functools.partial(body, mesh.shape["item"], mesh.shape["user"], mesh.shape["ka"])
    return jax.shard_map(run, mesh=mesh, in_specs=in_specs, out_specs=out_specs, check_vma=False)
```

```python
import functools

import jax
import jax.numpy as jnp
from jax import lax
from jax.experimental import pallas as pl
from jax.experimental.pallas import tpu as pltpu
from jax.sharding import PartitionSpec as P

BF16 = jnp.bfloat16
F32 = jnp.float32
VMEM = pltpu.MemorySpace.VMEM
SMEM = pltpu.MemorySpace.SMEM
HBM = pltpu.MemorySpace.HBM
EXTRA = 16
MIB = 1024 * 1024
CHEAP = pl.CostEstimate(flops=1024, transcendentals=0, bytes_accessed=1024)
DIMS_NT = (((1,), (1,)), ((), ()))
DIMS_TN = (((0,), (0,)), ((), ()))


def pinned(x):
    return pltpu.with_memory_space_constraint(x, HBM)


def reciprocal(x):
    r = pl.reciprocal(x, approx=True)
    return r * (2.0 - x * r)


def exp_digamma(x, inv_rate):
    w = x * (x + 3.0)
    p = w * (w + 2.0)
    y = x + 4.0
    inv = reciprocal(y * p)
    iy = inv * p
    iy2 = iy * iy
    shift = (2.0 * x + 3.0) * (2.0 * w + 2.0) * (inv * y)
    series = iy * 0.5 + iy2 * (1.0 / 12.0 - iy2 * (1.0 / 120.0 - iy2 * (1.0 / 252.0)))
    return y * inv_rate * jnp.exp(-(series + shift))


def encode(values):
    row = lax.broadcasted_iota(jnp.int32, (EXTRA, values[0].shape[1]), 0)
    out = jnp.zeros(row.shape, F32)
    for i, rest in enumerate(values):
        for j in range(3):
            piece = rest.astype(BF16).astype(F32)
            rest = rest - piece
            out = jnp.where(row == 3 * i + j, piece, out)
    return out.astype(BF16)


def decode(block):
    block = block.astype(F32)
    return [block[3 * i : 3 * i + 1] + block[3 * i + 1 : 3 * i + 2] + block[3 * i + 2 : 3 * i + 3] for i in range(2)]


def chunk_copies(starts, chunk, refs, buffers, sems):
    copies = []
    for j, start in enumerate(starts):
        here = pl.ds(start, chunk)
        copies.append(
            [pltpu.make_async_copy(r.at[here], b.at[here], sems.at[i, j]) for i, (r, b) in enumerate(zip(refs, buffers))]
        )
    for group in copies:
        for copy in group:
            copy.start()
    return copies


def expected_kernel(chunk_u, chunk_i, theta_ref, trate_ref, beta_ref, brate_ref, *refs):
    both_ref, item_ref, pack_ref, theta_buf, trate_buf, beta_buf, brate_buf, user_sems, item_sems = refs
    core = lax.axis_index("ka")
    half = both_ref.shape[0] // 2
    rows = beta_ref.shape[0]
    steps = half // chunk_u
    starts = []
    for side in (1 - core, core):
        starts += [pl.multiple_of(side * half + j * chunk_u, chunk_u) for j in range(steps)]
    item_starts = list(range(0, rows, chunk_i))
    user_copies = chunk_copies(starts, chunk_u, (theta_ref, trate_ref), (theta_buf, trate_buf), user_sems)
    item_copies = chunk_copies(item_starts, chunk_i, (beta_ref, brate_ref), (beta_buf, brate_buf), item_sems)
    theta_total = jnp.zeros((1, both_ref.shape[1]), F32)
    for j, start in enumerate(starts):
        for copy in user_copies[j]:
            copy.wait()
        x = theta_buf[pl.ds(start, chunk_u), :]
        inv_rate = reciprocal(trate_buf[pl.ds(start, chunk_u), :])
        value = exp_digamma(x, inv_rate).astype(BF16)
        at = (j % steps) * chunk_u
        if j < steps:
            both_ref[half + at : half + at + chunk_u, :] = value
            pack_ref[at : at + chunk_u, :] = value
        else:
            both_ref[at : at + chunk_u, :] = value
        theta_total += jnp.sum(x * inv_rate, axis=0, keepdims=True)
    beta_total = jnp.zeros((1, both_ref.shape[1]), F32)
    for j, start in enumerate(item_starts):
        for copy in item_copies[j]:
            copy.wait()
        x = beta_buf[start : start + chunk_i, :]
        inv_rate = reciprocal(brate_buf[start : start + chunk_i, :])
        value = exp_digamma(x, inv_rate).astype(BF16)
        item_ref[start : start + chunk_i, :] = value
        pack_ref[half + start : half + start + chunk_i, :] = value
        beta_total += jnp.sum(x * inv_rate, axis=0, keepdims=True)
    extra = encode([theta_total, beta_total])
    item_ref[rows:, :] = extra
    pack_ref[half + rows :, :] = extra


def expected(theta, trate, beta, brate):
    rows, cols = theta.shape
    item_rows = beta.shape[0]
    half = rows // 2
    chunk_u = min(half, 128)
    chunk_i = min(item_rows, 128)
    shapes = [rows, item_rows + EXTRA, half + item_rows + EXTRA]
    return pl.pallas_call(
        functools.partial(expected_kernel, chunk_u, chunk_i),
        in_specs=[pl.BlockSpec(memory_space=HBM)] * 4,
        out_specs=[pl.BlockSpec(memory_space=VMEM)] * 3,
        out_shape=[jax.ShapeDtypeStruct((r, cols), BF16) for r in shapes],
        scratch_shapes=[
            pltpu.VMEM((rows, cols), F32),
            pltpu.VMEM((rows, cols), F32),
            pltpu.VMEM((item_rows, cols), F32),
            pltpu.VMEM((item_rows, cols), F32),
            pltpu.SemaphoreType.DMA((2, rows // chunk_u)),
            pltpu.SemaphoreType.DMA((2, item_rows // chunk_i)),
        ],
        compiler_params=pltpu.CompilerParams(vmem_limit_bytes=6 * MIB),
        cost_estimate=CHEAP,
        name="expected",
    )(pinned(theta), pinned(trate), pinned(beta), pinned(brate))


def dense_kernel(n_item, shard_tiles, chunk, rows, users_in, items_in, live_ref, counts_ref, out_ref, *scratch):
    users_ref, items_ref, buf, sems, index_sems = scratch
    tile = counts_ref.shape[1]
    half = rows // 2
    piece = min(half, tile)
    n_chunks = counts_ref.shape[0] // chunk
    copies = [
        pltpu.make_async_copy(
            counts_ref.at[pl.ds(c * chunk, chunk)], buf.at[pl.ds(c * chunk, chunk)], sems.at[c]
        )
        for c in range(n_chunks)
    ]
    index_copies = [
        pltpu.make_async_copy(users_in, users_ref, index_sems.at[0]),
        pltpu.make_async_copy(items_in, items_ref, index_sems.at[1]),
    ]
    for copy in index_copies + copies:
        copy.start()
    out_ref[...] = jnp.zeros_like(out_ref)
    for copy in index_copies:
        copy.wait()
    z = lax.axis_index("item")
    x = lax.axis_index("user")
    core = lax.axis_index("ka")
    live = live_ref[0]

    def place(slot, carry):
        item = items_ref[slot]
        owner = lax.div(item, shard_tiles)
        column = (owner ^ x) * shard_tiles + lax.rem(item, shard_tiles)
        col = pl.multiple_of(column * tile, tile)
        for j in range(tile // piece):
            row = users_ref[slot] * tile + j * piece
            shard = lax.div(row, rows)
            within = lax.rem(row, rows)

            @pl.when(lax.div(within, half) == core)
            def _():
                distance = shard ^ z
                step = jnp.where(core == 0, distance, mirrored(distance, n_item))
                start = pl.multiple_of(step * half + lax.rem(within, half), piece)
                value = buf[slot, j * piece : (j + 1) * piece, :].astype(F32).astype(BF16)
                out_ref[pl.ds(start, piece), pl.ds(col, tile)] = value

        return carry

    for c in range(n_chunks):
        copies[c].wait()
        lax.fori_loop(c * chunk, jnp.clip(live, c * chunk, (c + 1) * chunk), place, 0)


def dense_counts(counts, users, items, live, rows, n_item, item_rows, n_user):
    slots, tile, _ = counts.shape
    chunk = 8
    out_rows = n_item * rows // 2
    return pl.pallas_call(
        functools.partial(dense_kernel, n_item, item_rows // n_user // tile, chunk, rows),
        in_specs=[pl.BlockSpec(memory_space=m) for m in (HBM, HBM, SMEM, HBM)],
        out_specs=pl.BlockSpec(memory_space=VMEM),
        out_shape=jax.ShapeDtypeStruct((out_rows, item_rows), BF16),
        scratch_shapes=[
            pltpu.SMEM(users.shape, jnp.int32),
            pltpu.SMEM(items.shape, jnp.int32),
            pltpu.VMEM((slots, tile, tile), jnp.int32),
            pltpu.SemaphoreType.DMA((slots // chunk,)),
            pltpu.SemaphoreType.DMA((2,)),
        ],
        compiler_params=pltpu.CompilerParams(vmem_limit_bytes=8 * MIB),
        cost_estimate=CHEAP,
        name="dense_counts",
    )(pinned(users), pinned(items), live, pinned(counts))


def stat_kernel(pieces, half, last, has_acc, at, *refs):
    refs = list(refs)
    take = lambda n: [refs.pop(0) for _ in range(n)]
    mine_ref, other_ref = take(2)
    mine = mine_ref[:half, :]
    other = other_ref[half : 2 * half, :] if at else other_ref[:half, :]
    item_mine = take(pieces)
    item_other = take(pieces)
    (counts_ref,) = take(1)
    (acc_in,) = take(1) if has_acc else (None,)
    stat_refs = take(1 if at else 2)
    acc_refs = take(1 + pieces if last else 1)
    cols = mine.shape[1]
    total_mine = None
    total_other = None
    width = 256
    for p in range(pieces):
        rows = item_mine[p].shape[0] - EXTRA
        skip = item_other[p].shape[0] - EXTRA - rows
        for c in range(rows // width):
            left = item_mine[p][c * width : (c + 1) * width, :]
            right = item_other[p][skip + c * width : skip + (c + 1) * width, :]
            norm = lax.dot_general(mine, left, DIMS_NT, preferred_element_type=F32)
            norm += lax.dot_general(other, right, DIMS_NT, preferred_element_type=F32)
            columns = slice(p * rows + c * width, p * rows + (c + 1) * width)
            grid = counts_ref[at * half : (at + 1) * half, columns].astype(F32)
            ratio = (grid * reciprocal(norm)).astype(BF16)
            stat = jnp.dot(ratio, left, preferred_element_type=F32)
            total_mine = stat if total_mine is None else total_mine + stat
            stat = jnp.dot(ratio, right, preferred_element_type=F32)
            total_other = stat if total_other is None else total_other + stat
            for i, factors in enumerate((mine, other)):
                update = lax.dot_general(factors, ratio, DIMS_TN, preferred_element_type=F32)
                if has_acc:
                    update += acc_in[i * cols : (i + 1) * cols, columns]
                if last and i == 0:
                    acc_refs[0][:, columns] = update
                elif last:
                    acc_refs[1 + p][:, c * width : (c + 1) * width] = update.astype(BF16)
                else:
                    acc_refs[0][i * cols : (i + 1) * cols, columns] = update
    if at:
        stat_refs[0][:half, :] = total_mine.astype(BF16)
        stat_refs[0][half : 2 * half, :] = total_other.astype(BF16)
        stat_refs[0][2 * half :, :] = encode(row_totals(item_mine))
    else:
        stat_refs[0][...] = total_mine
        stat_refs[1][...] = total_other


def row_totals(item_refs):
    sums = None
    for ref in item_refs:
        came = decode(ref[-EXTRA:, :])
        sums = came if sums is None else [a + b for a, b in zip(sums, came)]
    return sums


def statistics(at, users, item_mine, item_other, dense, acc, last, half_rows):
    half = users[0].shape[1]
    item_rows = dense.shape[1]
    args = [*users, *item_mine, *item_other, dense]
    if acc is not None:
        args.append(acc)
    if at:
        out_shape = [jax.ShapeDtypeStruct((2 * half_rows + EXTRA, half), BF16)]
    else:
        out_shape = [jax.ShapeDtypeStruct((half_rows, half), F32)] * 2
    n_stats = len(out_shape)
    if last:
        out_shape.append(jax.ShapeDtypeStruct((half, item_rows), F32))
        out_shape += [jax.ShapeDtypeStruct((half, item_rows // len(item_mine)), BF16) for _ in item_mine]
    else:
        out_shape.append(jax.ShapeDtypeStruct((2 * half, item_rows), F32))
    spec = pl.BlockSpec(memory_space=VMEM)
    out = pl.pallas_call(
        functools.partial(stat_kernel, len(item_mine), half_rows, last, acc is not None, at),
        in_specs=[spec] * len(args),
        out_specs=[spec] * len(out_shape),
        out_shape=out_shape,
        compiler_params=pltpu.CompilerParams(vmem_limit_bytes=16 * MIB),
        cost_estimate=CHEAP,
        name="statistics_%d" % at,
    )(*args)
    return list(out[:n_stats]), list(out[n_stats:])


def merge_items_kernel(p, mine_ref, came_ref, out_ref):
    width = out_ref.shape[1]
    out_ref[...] = (mine_ref[:, p * width : (p + 1) * width] + came_ref[...].astype(F32)).astype(BF16)


def merge_items(p, mine, came):
    return pl.pallas_call(
        functools.partial(merge_items_kernel, p),
        in_specs=[pl.BlockSpec(memory_space=VMEM)] * 2,
        out_specs=pl.BlockSpec(memory_space=VMEM),
        out_shape=jax.ShapeDtypeStruct(came.shape, BF16),
        compiler_params=pltpu.CompilerParams(vmem_limit_bytes=2 * MIB),
        cost_estimate=CHEAP,
        name="merge_items",
    )(mine, came)


def finish_users_kernel(n_joined, pieces, *refs):
    refs = list(refs)
    take = lambda n: [refs.pop(0) for _ in range(n)]
    both_ref, own_ref, sum_ref = take(3)
    joined = take(n_joined)
    (last_ref,) = take(1)
    item_refs = take(pieces)
    activity_ref, popularity_ref = take(2)
    outs = take(3)
    bufs = take(3)
    (sems,) = take(1)
    core = lax.axis_index("ka")
    half = own_ref.shape[0]
    copies = []

    total = own_ref[...]
    for ref in joined:
        total += ref[:half, :].astype(F32)
    start = pl.multiple_of(core * half, half)
    bufs[0][pl.ds(start, half), :] = 0.3 + both_ref[:half, :].astype(F32) * total
    copies.append(pltpu.make_async_copy(bufs[0].at[pl.ds(start, half)], outs[0].at[pl.ds(start, half)], sems.at[0]))
    copies[-1].start()

    total = sum_ref[...].astype(F32) + last_ref[...].astype(F32)
    start = pl.multiple_of((1 - core) * half, half)
    bufs[0][pl.ds(start, half), :] = 0.3 + both_ref[half:, :].astype(F32) * total
    copies.append(pltpu.make_async_copy(bufs[0].at[pl.ds(start, half)], outs[0].at[pl.ds(start, half)], sems.at[1]))
    copies[-1].start()

    theta_total, beta_total = row_totals(item_refs)
    for ref in joined:
        came = decode(ref[-EXTRA:, :])
        theta_total += came[0]
        beta_total += came[1]
    for i, (column_ref, total) in enumerate(((activity_ref, beta_total), (popularity_ref, theta_total))):
        rows = column_ref.shape[1]
        column = jnp.broadcast_to(column_ref[...], (total.shape[1], rows)).T
        bufs[1 + i][...] = column + total
        copies.append(pltpu.make_async_copy(bufs[1 + i], outs[1 + i], sems.at[2 + i]))
        copies[-1].start()
    for copy in copies:
        copy.wait()


def finish_users(both, own, other_sum, joined, other_last, items, activity, popularity):
    rows, half = both.shape
    args = [both, own, other_sum, *joined, other_last, *items, activity, popularity]
    out_shape = [
        jax.ShapeDtypeStruct((rows, half), F32),
        jax.ShapeDtypeStruct((activity.shape[1], half), F32),
        jax.ShapeDtypeStruct((popularity.shape[1], half), F32),
    ]
    return pl.pallas_call(
        functools.partial(finish_users_kernel, len(joined), len(items)),
        in_specs=[pl.BlockSpec(memory_space=VMEM)] * len(args),
        out_specs=[pl.BlockSpec(memory_space=HBM)] * 3,
        out_shape=out_shape,
        scratch_shapes=[pltpu.VMEM(o.shape, F32) for o in out_shape] + [pltpu.SemaphoreType.DMA((4,))],
        compiler_params=pltpu.CompilerParams(vmem_limit_bytes=8 * MIB),
        cost_estimate=CHEAP,
        name="finish_users",
    )(*args)


def finish_items_kernel(n, exp_ref, own_ref, *refs):
    out_ref, buf, sems = refs[n:]
    rows = out_ref.shape[0]
    chunk = min(rows, 256)
    copies = []
    for j in range(rows // chunk):
        part = slice(j * chunk, (j + 1) * chunk)
        total = own_ref[:, part]
        for p in range(n):
            total += refs[p][:, part].astype(F32)
        buf[part, :] = 0.3 + exp_ref[part, :].astype(F32) * total.T
        here = pl.ds(j * chunk, chunk)
        copies.append(pltpu.make_async_copy(buf.at[here], out_ref.at[here], sems.at[j]))
        copies[-1].start()
    for copy in copies:
        copy.wait()


def finish_items(item_exp, own, came):
    half, rows = came[0].shape
    return pl.pallas_call(
        functools.partial(finish_items_kernel, len(came)),
        in_specs=[pl.BlockSpec(memory_space=VMEM)] * (2 + len(came)),
        out_specs=pl.BlockSpec(memory_space=HBM),
        out_shape=jax.ShapeDtypeStruct((rows, half), F32),
        scratch_shapes=[pltpu.VMEM((rows, half), F32), pltpu.SemaphoreType.DMA((rows // min(rows, 256),))],
        compiler_params=pltpu.CompilerParams(vmem_limit_bytes=6 * MIB),
        cost_estimate=CHEAP,
        name="finish_items",
    )(item_exp, own, *came)


def mirrored(k, n):
    out = k * 0
    bit = 1
    while bit < n:
        out = out * 2 + (k & 1)
        k = k >> 1
        bit *= 2
    return out


def along_item(x, k, n, n_ka):
    pairs = []
    for i in range(n):
        for h in range(n_ka):
            pairs.append((i * n_ka + h, (i ^ (mirrored(k, n) if h else k)) * n_ka + h))
    return lax.ppermute(x, ("item", "ka"), pairs)


def after(x, y):
    return lax.optimization_barrier((x, y))[0]


def along_user(x, distance, n):
    return lax.ppermute(x, "user", [(i, i ^ distance) for i in range(n)])


def body(
    n_item,
    n_user,
    n_ka,
    counts,
    tile_user,
    tile_item,
    tile_live,
    theta_shape,
    theta_rate,
    user_activity,
    beta_shape,
    beta_rate,
    item_popularity,
):
    def sibling(x):
        return lax.ppermute(x, "ka", [(h, n_ka - 1 - h) for h in range(n_ka)])

    both, item_exp, pack = expected(theta_shape[0], theta_rate[0], beta_shape[0], beta_rate[0])
    rows = both.shape[0]
    half_rows = rows // 2
    item_rows = beta_shape.shape[1] * n_user
    dense = dense_counts(
        counts[0, 0],
        tile_user[0, 0],
        tile_item[0, 0],
        tile_live[0],
        rows,
        n_item,
        item_rows,
        n_user,
    )
    pack, dense = lax.optimization_barrier((pack, dense))
    came_pack = sibling(pack)

    shards = [both]
    for k in range(1, n_item):
        low = k & -k
        shards.append(along_item(shards[k ^ low], low, n_item, n_ka))

    item_mine = [item_exp]
    for p in range(1, n_user):
        low = p & -p
        item_mine.append(along_user(item_mine[p ^ low], low, n_user))
    item_other = [came_pack] + [sibling(x) for x in item_mine[1:]]

    order = sorted(range(1, n_item - 1), key=lambda k: (k & (k - 1) != 0, k)) + [0, n_item - 1]
    acc = None
    joined = []
    latest = None
    for k in order:
        last = k == n_item - 1
        if k == 0:
            other = came_pack
        else:
            passed = shards[mirrored(k, n_item)]
            other = sibling(after(passed, latest) if last else passed)
        stats, accs = statistics(k, [shards[k], other], item_mine, item_other, dense, acc, last, half_rows)
        acc = accs[0]
        if k == 0:
            own, own_other = stats
        else:
            joined.append(along_item(stats[0], k, n_item, n_ka))
            latest = stats[0] if latest is None else latest

    came = [sibling(accs[1])]
    for p in range(1, n_user):
        sent = merge_items(p, acc, sibling(accs[1 + p]))
        came.append(along_user(sent, p, n_user))
    new_beta_shape = finish_items(item_exp, acc, came)

    other_sum = own_other
    for x in joined[:-1]:
        other_sum = lax.optimization_barrier(other_sum + x[half_rows:rows].astype(F32))
    other_sum = other_sum.astype(BF16)
    other_sum = sibling(other_sum)
    other_last = sibling(after(joined[-1], other_sum)[half_rows:rows])
    other_last = after(other_last, new_beta_shape)
    new_theta_shape, new_theta_rate, new_beta_rate = finish_users(
        both, own, other_sum, joined, other_last, item_mine, user_activity, item_popularity
    )
    return (new_theta_shape[None], new_theta_rate[None], new_beta_shape[None], new_beta_rate[None])


def solution(mesh):
    in_specs = (
        P(("parts", "item"), "user", None, None, None),
        P(("parts", "item"), "user", None),
        P(("parts", "item"), "user", None),
        P(("parts", "item"), "user"),
        P(("parts", "user"), "item", "ka"),
        P(("parts", "user"), "item", "ka"),
        P(("parts", "user"), "item"),
        P(("parts", "item"), "user", "ka"),
        P(("parts", "item"), "user", "ka"),
        P(("parts", "item"), "user"),
    )
    out_specs = (
        P(("parts", "user"), "item", "ka"),
        P(("parts", "user"), "item", "ka"),
        P(("parts", "item"), "user", "ka"),
        P(("parts", "item"), "user", "ka"),
    )
    run = functools.partial(body, mesh.shape["item"], mesh.shape["user"], mesh.shape["ka"])
    return jax.shard_map(run, mesh=mesh, in_specs=in_specs, out_specs=out_specs, check_vma=False)
```

```python
import functools

import jax
import jax.numpy as jnp
from jax import lax
from jax.experimental import pallas as pl
from jax.experimental.pallas import tpu as pltpu
from jax.sharding import PartitionSpec as P

BF16 = jnp.bfloat16
F32 = jnp.float32
VMEM = pltpu.MemorySpace.VMEM
SMEM = pltpu.MemorySpace.SMEM
HBM = pltpu.MemorySpace.HBM
EXTRA = 16
MIB = 1024 * 1024
CHEAP = pl.CostEstimate(flops=1024, transcendentals=0, bytes_accessed=1024)
DIMS_NT = (((1,), (1,)), ((), ()))
DIMS_TN = (((0,), (0,)), ((), ()))


def pinned(x):
    return pltpu.with_memory_space_constraint(x, HBM)


def reciprocal(x):
    r = pl.reciprocal(x, approx=True)
    return r * (2.0 - x * r)


def exp_digamma(x, inv_rate):
    w = x * (x + 3.0)
    p = w * (w + 2.0)
    y = x + 4.0
    inv = reciprocal(y * p)
    iy = inv * p
    iy2 = iy * iy
    shift = (2.0 * x + 3.0) * (2.0 * w + 2.0) * (inv * y)
    series = iy * 0.5 + iy2 * (1.0 / 12.0 - iy2 * (1.0 / 120.0 - iy2 * (1.0 / 252.0)))
    return y * inv_rate * jnp.exp(-(series + shift))


def encode(values):
    row = lax.broadcasted_iota(jnp.int32, (EXTRA, values[0].shape[1]), 0)
    out = jnp.zeros(row.shape, F32)
    for i, rest in enumerate(values):
        for j in range(3):
            piece = rest.astype(BF16).astype(F32)
            rest = rest - piece
            out = jnp.where(row == 3 * i + j, piece, out)
    return out.astype(BF16)


def decode(block):
    block = block.astype(F32)
    return [block[3 * i : 3 * i + 1] + block[3 * i + 1 : 3 * i + 2] + block[3 * i + 2 : 3 * i + 3] for i in range(2)]


def chunk_copies(starts, chunk, refs, buffers, sems):
    copies = []
    for j, start in enumerate(starts):
        here = pl.ds(start, chunk)
        copies.append(
            [pltpu.make_async_copy(r.at[here], b.at[here], sems.at[i, j]) for i, (r, b) in enumerate(zip(refs, buffers))]
        )
    for group in copies:
        for copy in group:
            copy.start()
    return copies


def expected_kernel(chunk_u, chunk_i, theta_ref, trate_ref, beta_ref, brate_ref, *refs):
    both_ref, item_ref, pack_ref, theta_buf, trate_buf, beta_buf, brate_buf, user_sems, item_sems = refs
    core = lax.axis_index("ka")
    half = both_ref.shape[0] // 2
    rows = beta_ref.shape[0]
    steps = half // chunk_u
    starts = []
    for side in (1 - core, core):
        starts += [pl.multiple_of(side * half + j * chunk_u, chunk_u) for j in range(steps)]
    item_starts = list(range(0, rows, chunk_i))
    user_copies = chunk_copies(starts, chunk_u, (theta_ref, trate_ref), (theta_buf, trate_buf), user_sems)
    item_copies = chunk_copies(item_starts, chunk_i, (beta_ref, brate_ref), (beta_buf, brate_buf), item_sems)
    theta_total = jnp.zeros((1, both_ref.shape[1]), F32)
    for j, start in enumerate(starts):
        for copy in user_copies[j]:
            copy.wait()
        x = theta_buf[pl.ds(start, chunk_u), :]
        inv_rate = reciprocal(trate_buf[pl.ds(start, chunk_u), :])
        value = exp_digamma(x, inv_rate).astype(BF16)
        at = (j % steps) * chunk_u
        if j < steps:
            both_ref[half + at : half + at + chunk_u, :] = value
            pack_ref[at : at + chunk_u, :] = value
        else:
            both_ref[at : at + chunk_u, :] = value
        theta_total += jnp.sum(x * inv_rate, axis=0, keepdims=True)
    beta_total = jnp.zeros((1, both_ref.shape[1]), F32)
    for j, start in enumerate(item_starts):
        for copy in item_copies[j]:
            copy.wait()
        x = beta_buf[start : start + chunk_i, :]
        inv_rate = reciprocal(brate_buf[start : start + chunk_i, :])
        value = exp_digamma(x, inv_rate).astype(BF16)
        item_ref[start : start + chunk_i, :] = value
        pack_ref[half + start : half + start + chunk_i, :] = value
        beta_total += jnp.sum(x * inv_rate, axis=0, keepdims=True)
    extra = encode([theta_total, beta_total])
    item_ref[rows:, :] = extra
    pack_ref[half + rows :, :] = extra


def expected(theta, trate, beta, brate):
    rows, cols = theta.shape
    item_rows = beta.shape[0]
    half = rows // 2
    chunk_u = min(half, 128)
    chunk_i = min(item_rows, 128)
    shapes = [rows, item_rows + EXTRA, half + item_rows + EXTRA]
    return pl.pallas_call(
        functools.partial(expected_kernel, chunk_u, chunk_i),
        in_specs=[pl.BlockSpec(memory_space=HBM)] * 4,
        out_specs=[pl.BlockSpec(memory_space=VMEM)] * 3,
        out_shape=[jax.ShapeDtypeStruct((r, cols), BF16) for r in shapes],
        scratch_shapes=[
            pltpu.VMEM((rows, cols), F32),
            pltpu.VMEM((rows, cols), F32),
            pltpu.VMEM((item_rows, cols), F32),
            pltpu.VMEM((item_rows, cols), F32),
            pltpu.SemaphoreType.DMA((2, rows // chunk_u)),
            pltpu.SemaphoreType.DMA((2, item_rows // chunk_i)),
        ],
        compiler_params=pltpu.CompilerParams(vmem_limit_bytes=6 * MIB),
        cost_estimate=CHEAP,
        name="expected",
    )(pinned(theta), pinned(trate), pinned(beta), pinned(brate))


def dense_kernel(n_item, shard_tiles, chunk, rows, users_in, items_in, live_ref, counts_ref, out_ref, *scratch):
    users_ref, items_ref, buf, sems, index_sems = scratch
    tile = counts_ref.shape[1]
    half = rows // 2
    piece = min(half, tile)
    n_chunks = counts_ref.shape[0] // chunk
    copies = [
        pltpu.make_async_copy(
            counts_ref.at[pl.ds(c * chunk, chunk)], buf.at[pl.ds(c * chunk, chunk)], sems.at[c]
        )
        for c in range(n_chunks)
    ]
    index_copies = [
        pltpu.make_async_copy(users_in, users_ref, index_sems.at[0]),
        pltpu.make_async_copy(items_in, items_ref, index_sems.at[1]),
    ]
    for copy in index_copies + copies:
        copy.start()
    out_ref[...] = jnp.zeros_like(out_ref)
    for copy in index_copies:
        copy.wait()
    z = lax.axis_index("item")
    x = lax.axis_index("user")
    core = lax.axis_index("ka")
    live = live_ref[0]

    def place(slot, carry):
        item = items_ref[slot]
        owner = lax.div(item, shard_tiles)
        column = (owner ^ x) * shard_tiles + lax.rem(item, shard_tiles)
        col = pl.multiple_of(column * tile, tile)
        for j in range(tile // piece):
            row = users_ref[slot] * tile + j * piece
            shard = lax.div(row, rows)
            within = lax.rem(row, rows)

            @pl.when(lax.div(within, half) == core)
            def _():
                step = lax.rem(z - shard + n_item, n_item)
                start = pl.multiple_of(step * half + lax.rem(within, half), piece)
                value = buf[slot, j * piece : (j + 1) * piece, :].astype(F32).astype(BF16)
                out_ref[pl.ds(start, piece), pl.ds(col, tile)] = value

        return carry

    for c in range(n_chunks):
        copies[c].wait()
        lax.fori_loop(c * chunk, jnp.clip(live, c * chunk, (c + 1) * chunk), place, 0)


def dense_counts(counts, users, items, live, rows, n_item, item_rows, n_user):
    slots, tile, _ = counts.shape
    chunk = 8
    out_rows = n_item * rows // 2
    return pl.pallas_call(
        functools.partial(dense_kernel, n_item, item_rows // n_user // tile, chunk, rows),
        in_specs=[pl.BlockSpec(memory_space=m) for m in (HBM, HBM, SMEM, HBM)],
        out_specs=pl.BlockSpec(memory_space=VMEM),
        out_shape=jax.ShapeDtypeStruct((out_rows, item_rows), BF16),
        scratch_shapes=[
            pltpu.SMEM(users.shape, jnp.int32),
            pltpu.SMEM(items.shape, jnp.int32),
            pltpu.VMEM((slots, tile, tile), jnp.int32),
            pltpu.SemaphoreType.DMA((slots // chunk,)),
            pltpu.SemaphoreType.DMA((2,)),
        ],
        compiler_params=pltpu.CompilerParams(vmem_limit_bytes=8 * MIB),
        cost_estimate=CHEAP,
        name="dense_counts",
    )(pinned(users), pinned(items), live, pinned(counts))


def stat_kernel(pieces, half, last, has_sum, has_acc, at, *refs):
    refs = list(refs)
    take = lambda n: [refs.pop(0) for _ in range(n)]
    mine_ref, other_ref = take(2)
    mine = mine_ref[:half, :]
    other = other_ref[half : 2 * half, :] if at else other_ref[:half, :]
    item_mine = take(pieces)
    item_other = take(pieces)
    (counts_ref,) = take(1)
    (sum_ref,) = take(1) if has_sum else (None,)
    (acc_in,) = take(1) if has_acc else (None,)
    stat_refs = take(1 if at else 2)
    acc_refs = take(1 + pieces if last else 1)
    cols = mine.shape[1]
    total_mine = None
    total_other = None
    width = 256
    for p in range(pieces):
        rows = item_mine[p].shape[0] - EXTRA
        skip = item_other[p].shape[0] - EXTRA - rows
        for c in range(rows // width):
            left = item_mine[p][c * width : (c + 1) * width, :]
            right = item_other[p][skip + c * width : skip + (c + 1) * width, :]
            norm = lax.dot_general(mine, left, DIMS_NT, preferred_element_type=F32)
            norm += lax.dot_general(other, right, DIMS_NT, preferred_element_type=F32)
            columns = slice(p * rows + c * width, p * rows + (c + 1) * width)
            grid = counts_ref[at * half : (at + 1) * half, columns].astype(F32)
            ratio = (grid * reciprocal(norm)).astype(BF16)
            stat = jnp.dot(ratio, left, preferred_element_type=F32)
            total_mine = stat if total_mine is None else total_mine + stat
            stat = jnp.dot(ratio, right, preferred_element_type=F32)
            total_other = stat if total_other is None else total_other + stat
            for i, factors in enumerate((mine, other)):
                update = lax.dot_general(factors, ratio, DIMS_TN, preferred_element_type=F32)
                if has_acc:
                    update += acc_in[i * cols : (i + 1) * cols, columns]
                if last and i == 0:
                    acc_refs[0][:, columns] = update
                elif last:
                    acc_refs[1 + p][:, c * width : (c + 1) * width] = update.astype(BF16)
                else:
                    acc_refs[0][i * cols : (i + 1) * cols, columns] = update
    if not at:
        stat_refs[0][...] = total_mine
        stat_refs[1][...] = total_other
        return
    totals = row_totals(item_mine)
    if has_sum:
        total_mine += sum_ref[:half, :].astype(F32)
        total_other += sum_ref[half : 2 * half, :].astype(F32)
        totals = [a + b for a, b in zip(totals, decode(sum_ref[2 * half :, :]))]
    stat_refs[0][:half, :] = total_mine.astype(BF16)
    stat_refs[0][half : 2 * half, :] = total_other.astype(BF16)
    stat_refs[0][2 * half :, :] = encode(totals)


def row_totals(item_refs):
    sums = None
    for ref in item_refs:
        came = decode(ref[-EXTRA:, :])
        sums = came if sums is None else [a + b for a, b in zip(sums, came)]
    return sums


def statistics(at, users, item_mine, item_other, dense, running, acc, last, half_rows):
    half = users[0].shape[1]
    item_rows = dense.shape[1]
    args = [*users, *item_mine, *item_other, dense]
    if running is not None:
        args.append(running)
    if acc is not None:
        args.append(acc)
    if at:
        out_shape = [jax.ShapeDtypeStruct((2 * half_rows + EXTRA, half), BF16)]
    else:
        out_shape = [jax.ShapeDtypeStruct((half_rows, half), F32)] * 2
    n_stats = len(out_shape)
    if last:
        out_shape.append(jax.ShapeDtypeStruct((half, item_rows), F32))
        out_shape += [jax.ShapeDtypeStruct((half, item_rows // len(item_mine)), BF16) for _ in item_mine]
    else:
        out_shape.append(jax.ShapeDtypeStruct((2 * half, item_rows), F32))
    spec = pl.BlockSpec(memory_space=VMEM)
    out = pl.pallas_call(
        functools.partial(stat_kernel, len(item_mine), half_rows, last, running is not None, acc is not None, at),
        in_specs=[spec] * len(args),
        out_specs=[spec] * len(out_shape),
        out_shape=out_shape,
        compiler_params=pltpu.CompilerParams(vmem_limit_bytes=16 * MIB),
        cost_estimate=CHEAP,
        name="statistics_%d" % at,
    )(*args)
    return list(out[:n_stats]), list(out[n_stats:])


def merge_items_kernel(p, mine_ref, came_ref, out_ref):
    width = out_ref.shape[1]
    out_ref[...] = (mine_ref[:, p * width : (p + 1) * width] + came_ref[...].astype(F32)).astype(BF16)


def merge_items(p, mine, came):
    return pl.pallas_call(
        functools.partial(merge_items_kernel, p),
        in_specs=[pl.BlockSpec(memory_space=VMEM)] * 2,
        out_specs=pl.BlockSpec(memory_space=VMEM),
        out_shape=jax.ShapeDtypeStruct(came.shape, BF16),
        compiler_params=pltpu.CompilerParams(vmem_limit_bytes=2 * MIB),
        cost_estimate=CHEAP,
        name="merge_items",
    )(mine, came)


def finish_users_kernel(pieces, *refs):
    refs = list(refs)
    take = lambda n: [refs.pop(0) for _ in range(n)]
    both_ref, own_ref, came_ref, last_ref = take(4)
    item_refs = take(pieces)
    activity_ref, popularity_ref = take(2)
    outs = take(3)
    bufs = take(3)
    (sems,) = take(1)
    core = lax.axis_index("ka")
    half = own_ref.shape[0]
    copies = []

    total = own_ref[...] + came_ref[:half, :].astype(F32)
    start = pl.multiple_of(core * half, half)
    bufs[0][pl.ds(start, half), :] = 0.3 + both_ref[:half, :].astype(F32) * total
    copies.append(pltpu.make_async_copy(bufs[0].at[pl.ds(start, half)], outs[0].at[pl.ds(start, half)], sems.at[0]))
    copies[-1].start()

    total = last_ref[...].astype(F32)
    start = pl.multiple_of((1 - core) * half, half)
    bufs[0][pl.ds(start, half), :] = 0.3 + both_ref[half:, :].astype(F32) * total
    copies.append(pltpu.make_async_copy(bufs[0].at[pl.ds(start, half)], outs[0].at[pl.ds(start, half)], sems.at[1]))
    copies[-1].start()

    theta_total, beta_total = row_totals(item_refs)
    came = decode(came_ref[2 * half :, :])
    theta_total += came[0]
    beta_total += came[1]
    for i, (column_ref, total) in enumerate(((activity_ref, beta_total), (popularity_ref, theta_total))):
        rows = column_ref.shape[1]
        column = jnp.broadcast_to(column_ref[...], (total.shape[1], rows)).T
        bufs[1 + i][...] = column + total
        copies.append(pltpu.make_async_copy(bufs[1 + i], outs[1 + i], sems.at[2 + i]))
        copies[-1].start()
    for copy in copies:
        copy.wait()


def finish_users(both, own, came, came_other, items, activity, popularity):
    rows, half = both.shape
    args = [both, own, came, came_other, *items, activity, popularity]
    out_shape = [
        jax.ShapeDtypeStruct((rows, half), F32),
        jax.ShapeDtypeStruct((activity.shape[1], half), F32),
        jax.ShapeDtypeStruct((popularity.shape[1], half), F32),
    ]
    return pl.pallas_call(
        functools.partial(finish_users_kernel, len(items)),
        in_specs=[pl.BlockSpec(memory_space=VMEM)] * len(args),
        out_specs=[pl.BlockSpec(memory_space=HBM)] * 3,
        out_shape=out_shape,
        scratch_shapes=[pltpu.VMEM(o.shape, F32) for o in out_shape] + [pltpu.SemaphoreType.DMA((4,))],
        compiler_params=pltpu.CompilerParams(vmem_limit_bytes=8 * MIB),
        cost_estimate=CHEAP,
        name="finish_users",
    )(*args)


def finish_items_kernel(n, exp_ref, own_ref, *refs):
    out_ref, buf, sems = refs[n:]
    rows = out_ref.shape[0]
    chunk = min(rows, 256)
    copies = []
    for j in range(rows // chunk):
        part = slice(j * chunk, (j + 1) * chunk)
        total = own_ref[:, part]
        for p in range(n):
            total += refs[p][:, part].astype(F32)
        buf[part, :] = 0.3 + exp_ref[part, :].astype(F32) * total.T
        here = pl.ds(j * chunk, chunk)
        copies.append(pltpu.make_async_copy(buf.at[here], out_ref.at[here], sems.at[j]))
        copies[-1].start()
    for copy in copies:
        copy.wait()


def finish_items(item_exp, own, came):
    half, rows = came[0].shape
    return pl.pallas_call(
        functools.partial(finish_items_kernel, len(came)),
        in_specs=[pl.BlockSpec(memory_space=VMEM)] * (2 + len(came)),
        out_specs=pl.BlockSpec(memory_space=HBM),
        out_shape=jax.ShapeDtypeStruct((rows, half), F32),
        scratch_shapes=[pltpu.VMEM((rows, half), F32), pltpu.SemaphoreType.DMA((rows // min(rows, 256),))],
        compiler_params=pltpu.CompilerParams(vmem_limit_bytes=6 * MIB),
        cost_estimate=CHEAP,
        name="finish_items",
    )(item_exp, own, *came)


def around_item(x, n):
    return lax.ppermute(x, "item", [(i, (i + 1) % n) for i in range(n)])


def after(x, y):
    return lax.optimization_barrier((x, y))[0]


def along_user(x, distance, n):
    return lax.ppermute(x, "user", [(i, i ^ distance) for i in range(n)])


def body(
    n_item,
    n_user,
    n_ka,
    counts,
    tile_user,
    tile_item,
    tile_live,
    theta_shape,
    theta_rate,
    user_activity,
    beta_shape,
    beta_rate,
    item_popularity,
):
    def sibling(x):
        return lax.ppermute(x, "ka", [(h, n_ka - 1 - h) for h in range(n_ka)])

    both, item_exp, pack = expected(theta_shape[0], theta_rate[0], beta_shape[0], beta_rate[0])
    rows = both.shape[0]
    half_rows = rows // 2
    item_rows = beta_shape.shape[1] * n_user
    dense = dense_counts(
        counts[0, 0],
        tile_user[0, 0],
        tile_item[0, 0],
        tile_live[0],
        rows,
        n_item,
        item_rows,
        n_user,
    )
    pack, dense = lax.optimization_barrier((pack, dense))
    came_pack = sibling(pack)

    shards = [both]
    for t in range(1, n_item):
        shards.append(around_item(shards[-1], n_item))

    item_mine = [item_exp]
    for p in range(1, n_user):
        low = p & -p
        item_mine.append(along_user(item_mine[p ^ low], low, n_user))
    item_other = [came_pack] + [sibling(x) for x in item_mine[1:]]

    order = [1, 0] + list(range(2, n_item))
    acc = None
    running = None
    for t in order:
        last = t == order[-1]
        other = sibling(shards[t]) if t else came_pack
        users = [shards[t], other]
        came_sum = running if t else None
        stats, accs = statistics(t, users, item_mine, item_other, dense, came_sum, acc, last, half_rows)
        acc = accs[0]
        if t:
            running = around_item(stats[0], n_item)
        else:
            own, own_other = stats

    came = [sibling(accs[1])]
    for p in range(1, n_user):
        sent = merge_items(p, acc, sibling(accs[1 + p]))
        came.append(along_user(sent, p, n_user))
    new_beta_shape = finish_items(item_exp, acc, came)

    came_other = sibling((own_other + running[half_rows:rows].astype(F32)).astype(BF16))
    came_other = after(came_other, new_beta_shape)
    new_theta_shape, new_theta_rate, new_beta_rate = finish_users(
        both, own, running, came_other, item_mine, user_activity, item_popularity
    )
    return (new_theta_shape[None], new_theta_rate[None], new_beta_shape[None], new_beta_rate[None])


def solution(mesh):
    in_specs = (
        P(("parts", "item"), "user", None, None, None),
        P(("parts", "item"), "user", None),
        P(("parts", "item"), "user", None),
        P(("parts", "item"), "user"),
        P(("parts", "user"), "item", "ka"),
        P(("parts", "user"), "item", "ka"),
        P(("parts", "user"), "item"),
        P(("parts", "item"), "user", "ka"),
        P(("parts", "item"), "user", "ka"),
        P(("parts", "item"), "user"),
    )
    out_specs = (
        P(("parts", "user"), "item", "ka"),
        P(("parts", "user"), "item", "ka"),
        P(("parts", "item"), "user", "ka"),
        P(("parts", "item"), "user", "ka"),
    )
    run = functools.partial(body, mesh.shape["item"], mesh.shape["user"], mesh.shape["ka"])
    return jax.shard_map(run, mesh=mesh, in_specs=in_specs, out_specs=out_specs, check_vma=False)
```

```python
import functools

import jax
import jax.numpy as jnp
from jax import lax
from jax.experimental import pallas as pl
from jax.experimental.pallas import tpu as pltpu
from jax.sharding import PartitionSpec as P

BF16 = jnp.bfloat16
F32 = jnp.float32
VMEM = pltpu.MemorySpace.VMEM
SMEM = pltpu.MemorySpace.SMEM
HBM = pltpu.MemorySpace.HBM
EXTRA = 16
MIB = 1024 * 1024
CHEAP = pl.CostEstimate(flops=1024, transcendentals=0, bytes_accessed=1024)
DIMS_NT = (((1,), (1,)), ((), ()))
DIMS_TN = (((0,), (0,)), ((), ()))


def pinned(x):
    return pltpu.with_memory_space_constraint(x, HBM)


def reciprocal(x):
    r = pl.reciprocal(x, approx=True)
    return r * (2.0 - x * r)


def exp_digamma(x, inv_rate):
    w = x * (x + 3.0)
    p = w * (w + 2.0)
    y = x + 4.0
    inv = reciprocal(y * p)
    iy = inv * p
    iy2 = iy * iy
    shift = (2.0 * x + 3.0) * (2.0 * w + 2.0) * (inv * y)
    series = iy * 0.5 + iy2 * (1.0 / 12.0 - iy2 * (1.0 / 120.0 - iy2 * (1.0 / 252.0)))
    return y * inv_rate * jnp.exp(-(series + shift))


def encode(values):
    row = lax.broadcasted_iota(jnp.int32, (EXTRA, values[0].shape[1]), 0)
    out = jnp.zeros(row.shape, F32)
    for i, rest in enumerate(values):
        for j in range(3):
            piece = rest.astype(BF16).astype(F32)
            rest = rest - piece
            out = jnp.where(row == 3 * i + j, piece, out)
    return out.astype(BF16)


def decode(block):
    block = block.astype(F32)
    return [block[3 * i : 3 * i + 1] + block[3 * i + 1 : 3 * i + 2] + block[3 * i + 2 : 3 * i + 3] for i in range(2)]


def chunk_copies(starts, chunk, refs, buffers, sems):
    copies = []
    for j, start in enumerate(starts):
        here = pl.ds(start, chunk)
        copies.append(
            [pltpu.make_async_copy(r.at[here], b.at[here], sems.at[i, j]) for i, (r, b) in enumerate(zip(refs, buffers))]
        )
    for group in copies:
        for copy in group:
            copy.start()
    return copies


def expected_kernel(chunk_u, chunk_i, theta_ref, trate_ref, beta_ref, brate_ref, *refs):
    both_ref, item_ref, pack_ref, theta_buf, trate_buf, beta_buf, brate_buf, user_sems, item_sems = refs
    core = lax.axis_index("ka")
    half = both_ref.shape[0] // 2
    rows = beta_ref.shape[0]
    steps = half // chunk_u
    starts = []
    for side in (1 - core, core):
        starts += [pl.multiple_of(side * half + j * chunk_u, chunk_u) for j in range(steps)]
    item_starts = list(range(0, rows, chunk_i))
    user_copies = chunk_copies(starts, chunk_u, (theta_ref, trate_ref), (theta_buf, trate_buf), user_sems)
    item_copies = chunk_copies(item_starts, chunk_i, (beta_ref, brate_ref), (beta_buf, brate_buf), item_sems)
    theta_total = jnp.zeros((1, both_ref.shape[1]), F32)
    for j, start in enumerate(starts):
        for copy in user_copies[j]:
            copy.wait()
        x = theta_buf[pl.ds(start, chunk_u), :]
        inv_rate = reciprocal(trate_buf[pl.ds(start, chunk_u), :])
        value = exp_digamma(x, inv_rate).astype(BF16)
        at = (j % steps) * chunk_u
        if j < steps:
            both_ref[half + at : half + at + chunk_u, :] = value
            pack_ref[at : at + chunk_u, :] = value
        else:
            both_ref[at : at + chunk_u, :] = value
        theta_total += jnp.sum(x * inv_rate, axis=0, keepdims=True)
    beta_total = jnp.zeros((1, both_ref.shape[1]), F32)
    for j, start in enumerate(item_starts):
        for copy in item_copies[j]:
            copy.wait()
        x = beta_buf[start : start + chunk_i, :]
        inv_rate = reciprocal(brate_buf[start : start + chunk_i, :])
        value = exp_digamma(x, inv_rate).astype(BF16)
        item_ref[start : start + chunk_i, :] = value
        pack_ref[half + start : half + start + chunk_i, :] = value
        beta_total += jnp.sum(x * inv_rate, axis=0, keepdims=True)
    extra = encode([theta_total, beta_total])
    item_ref[rows:, :] = extra
    pack_ref[half + rows :, :] = extra


def expected(theta, trate, beta, brate):
    rows, cols = theta.shape
    item_rows = beta.shape[0]
    half = rows // 2
    chunk_u = min(half, 128)
    chunk_i = min(item_rows, 128)
    shapes = [rows, item_rows + EXTRA, half + item_rows + EXTRA]
    return pl.pallas_call(
        functools.partial(expected_kernel, chunk_u, chunk_i),
        in_specs=[pl.BlockSpec(memory_space=HBM)] * 4,
        out_specs=[pl.BlockSpec(memory_space=VMEM)] * 3,
        out_shape=[jax.ShapeDtypeStruct((r, cols), BF16) for r in shapes],
        scratch_shapes=[
            pltpu.VMEM((rows, cols), F32),
            pltpu.VMEM((rows, cols), F32),
            pltpu.VMEM((item_rows, cols), F32),
            pltpu.VMEM((item_rows, cols), F32),
            pltpu.SemaphoreType.DMA((2, rows // chunk_u)),
            pltpu.SemaphoreType.DMA((2, item_rows // chunk_i)),
        ],
        compiler_params=pltpu.CompilerParams(vmem_limit_bytes=6 * MIB),
        cost_estimate=CHEAP,
        name="expected",
    )(pinned(theta), pinned(trate), pinned(beta), pinned(brate))


def dense_kernel(n_item, shard_tiles, chunk, rows, users_in, items_in, live_ref, counts_ref, out_ref, *scratch):
    users_ref, items_ref, buf, sems, index_sems = scratch
    tile = counts_ref.shape[1]
    half = rows // 2
    piece = min(half, tile)
    n_chunks = counts_ref.shape[0] // chunk
    copies = [
        pltpu.make_async_copy(
            counts_ref.at[pl.ds(c * chunk, chunk)], buf.at[pl.ds(c * chunk, chunk)], sems.at[c]
        )
        for c in range(n_chunks)
    ]
    index_copies = [
        pltpu.make_async_copy(users_in, users_ref, index_sems.at[0]),
        pltpu.make_async_copy(items_in, items_ref, index_sems.at[1]),
    ]
    for copy in index_copies + copies:
        copy.start()
    out_ref[...] = jnp.zeros_like(out_ref)
    for copy in index_copies:
        copy.wait()
    z = lax.axis_index("item")
    x = lax.axis_index("user")
    core = lax.axis_index("ka")
    live = live_ref[0]

    def place(slot, carry):
        item = items_ref[slot]
        owner = lax.div(item, shard_tiles)
        column = (owner ^ x) * shard_tiles + lax.rem(item, shard_tiles)
        col = pl.multiple_of(column * tile, tile)
        for j in range(tile // piece):
            row = users_ref[slot] * tile + j * piece
            shard = lax.div(row, rows)
            within = lax.rem(row, rows)

            @pl.when(lax.div(within, half) == core)
            def _():
                back = lax.rem(z - shard + n_item, n_item)
                step = jnp.where(back == 0, 0, jnp.where(back * 2 <= n_item, 2 * back - 1, 2 * (n_item - back)))
                start = pl.multiple_of(step * half + lax.rem(within, half), piece)
                value = buf[slot, j * piece : (j + 1) * piece, :].astype(F32).astype(BF16)
                out_ref[pl.ds(start, piece), pl.ds(col, tile)] = value

        return carry

    for c in range(n_chunks):
        copies[c].wait()
        lax.fori_loop(c * chunk, jnp.clip(live, c * chunk, (c + 1) * chunk), place, 0)


def dense_counts(counts, users, items, live, rows, n_item, item_rows, n_user):
    slots, tile, _ = counts.shape
    chunk = 8
    out_rows = n_item * rows // 2
    return pl.pallas_call(
        functools.partial(dense_kernel, n_item, item_rows // n_user // tile, chunk, rows),
        in_specs=[pl.BlockSpec(memory_space=m) for m in (HBM, HBM, SMEM, HBM)],
        out_specs=pl.BlockSpec(memory_space=VMEM),
        out_shape=jax.ShapeDtypeStruct((out_rows, item_rows), BF16),
        scratch_shapes=[
            pltpu.SMEM(users.shape, jnp.int32),
            pltpu.SMEM(items.shape, jnp.int32),
            pltpu.VMEM((slots, tile, tile), jnp.int32),
            pltpu.SemaphoreType.DMA((slots // chunk,)),
            pltpu.SemaphoreType.DMA((2,)),
        ],
        compiler_params=pltpu.CompilerParams(vmem_limit_bytes=8 * MIB),
        cost_estimate=CHEAP,
        name="dense_counts",
    )(pinned(users), pinned(items), live, pinned(counts))


def stat_kernel(pieces, half, last, has_acc, at, *refs):
    refs = list(refs)
    take = lambda n: [refs.pop(0) for _ in range(n)]
    mine_ref, other_ref = take(2)
    mine = mine_ref[:half, :]
    other = other_ref[half : 2 * half, :] if at else other_ref[:half, :]
    item_mine = take(pieces)
    item_other = take(pieces)
    (counts_ref,) = take(1)
    (acc_in,) = take(1) if has_acc else (None,)
    stat_refs = take(1 if at else 2)
    acc_refs = take(1 + pieces if last else 1)
    cols = mine.shape[1]
    total_mine = None
    total_other = None
    width = 256
    for p in range(pieces):
        rows = item_mine[p].shape[0] - EXTRA
        skip = item_other[p].shape[0] - EXTRA - rows
        for c in range(rows // width):
            left = item_mine[p][c * width : (c + 1) * width, :]
            right = item_other[p][skip + c * width : skip + (c + 1) * width, :]
            norm = lax.dot_general(mine, left, DIMS_NT, preferred_element_type=F32)
            norm += lax.dot_general(other, right, DIMS_NT, preferred_element_type=F32)
            columns = slice(p * rows + c * width, p * rows + (c + 1) * width)
            grid = counts_ref[at * half : (at + 1) * half, columns].astype(F32)
            ratio = (grid * reciprocal(norm)).astype(BF16)
            stat = jnp.dot(ratio, left, preferred_element_type=F32)
            total_mine = stat if total_mine is None else total_mine + stat
            stat = jnp.dot(ratio, right, preferred_element_type=F32)
            total_other = stat if total_other is None else total_other + stat
            for i, factors in enumerate((mine, other)):
                update = lax.dot_general(factors, ratio, DIMS_TN, preferred_element_type=F32)
                if has_acc:
                    update += acc_in[i * cols : (i + 1) * cols, columns]
                if last and i == 0:
                    acc_refs[0][:, columns] = update
                elif last:
                    acc_refs[1 + p][:, c * width : (c + 1) * width] = update.astype(BF16)
                else:
                    acc_refs[0][i * cols : (i + 1) * cols, columns] = update
    if at:
        stat_refs[0][:half, :] = total_mine.astype(BF16)
        stat_refs[0][half : 2 * half, :] = total_other.astype(BF16)
        stat_refs[0][2 * half :, :] = encode(row_totals(item_mine))
    else:
        stat_refs[0][...] = total_mine
        stat_refs[1][...] = total_other


def row_totals(item_refs):
    sums = None
    for ref in item_refs:
        came = decode(ref[-EXTRA:, :])
        sums = came if sums is None else [a + b for a, b in zip(sums, came)]
    return sums


def statistics(at, users, item_mine, item_other, dense, acc, last, half_rows):
    half = users[0].shape[1]
    item_rows = dense.shape[1]
    args = [*users, *item_mine, *item_other, dense]
    if acc is not None:
        args.append(acc)
    if at:
        out_shape = [jax.ShapeDtypeStruct((2 * half_rows + EXTRA, half), BF16)]
    else:
        out_shape = [jax.ShapeDtypeStruct((half_rows, half), F32)] * 2
    n_stats = len(out_shape)
    if last:
        out_shape.append(jax.ShapeDtypeStruct((half, item_rows), F32))
        out_shape += [jax.ShapeDtypeStruct((half, item_rows // len(item_mine)), BF16) for _ in item_mine]
    else:
        out_shape.append(jax.ShapeDtypeStruct((2 * half, item_rows), F32))
    spec = pl.BlockSpec(memory_space=VMEM)
    out = pl.pallas_call(
        functools.partial(stat_kernel, len(item_mine), half_rows, last, acc is not None, at),
        in_specs=[spec] * len(args),
        out_specs=[spec] * len(out_shape),
        out_shape=out_shape,
        compiler_params=pltpu.CompilerParams(vmem_limit_bytes=16 * MIB),
        cost_estimate=CHEAP,
        name="statistics_%d" % at,
    )(*args)
    return list(out[:n_stats]), list(out[n_stats:])


def merge_items_kernel(p, mine_ref, came_ref, out_ref):
    width = out_ref.shape[1]
    out_ref[...] = (mine_ref[:, p * width : (p + 1) * width] + came_ref[...].astype(F32)).astype(BF16)


def merge_items(p, mine, came):
    return pl.pallas_call(
        functools.partial(merge_items_kernel, p),
        in_specs=[pl.BlockSpec(memory_space=VMEM)] * 2,
        out_specs=pl.BlockSpec(memory_space=VMEM),
        out_shape=jax.ShapeDtypeStruct(came.shape, BF16),
        compiler_params=pltpu.CompilerParams(vmem_limit_bytes=2 * MIB),
        cost_estimate=CHEAP,
        name="merge_items",
    )(mine, came)


def finish_users_kernel(n_joined, pieces, *refs):
    refs = list(refs)
    take = lambda n: [refs.pop(0) for _ in range(n)]
    both_ref, own_ref, sum_ref = take(3)
    joined = take(n_joined)
    (last_ref,) = take(1)
    item_refs = take(pieces)
    activity_ref, popularity_ref = take(2)
    outs = take(3)
    bufs = take(3)
    (sems,) = take(1)
    core = lax.axis_index("ka")
    half = own_ref.shape[0]
    copies = []

    total = own_ref[...]
    for ref in joined:
        total += ref[:half, :].astype(F32)
    start = pl.multiple_of(core * half, half)
    bufs[0][pl.ds(start, half), :] = 0.3 + both_ref[:half, :].astype(F32) * total
    copies.append(pltpu.make_async_copy(bufs[0].at[pl.ds(start, half)], outs[0].at[pl.ds(start, half)], sems.at[0]))
    copies[-1].start()

    total = sum_ref[...].astype(F32) + last_ref[...].astype(F32)
    start = pl.multiple_of((1 - core) * half, half)
    bufs[0][pl.ds(start, half), :] = 0.3 + both_ref[half:, :].astype(F32) * total
    copies.append(pltpu.make_async_copy(bufs[0].at[pl.ds(start, half)], outs[0].at[pl.ds(start, half)], sems.at[1]))
    copies[-1].start()

    theta_total, beta_total = row_totals(item_refs)
    for ref in joined:
        came = decode(ref[-EXTRA:, :])
        theta_total += came[0]
        beta_total += came[1]
    for i, (column_ref, total) in enumerate(((activity_ref, beta_total), (popularity_ref, theta_total))):
        rows = column_ref.shape[1]
        column = jnp.broadcast_to(column_ref[...], (total.shape[1], rows)).T
        bufs[1 + i][...] = column + total
        copies.append(pltpu.make_async_copy(bufs[1 + i], outs[1 + i], sems.at[2 + i]))
        copies[-1].start()
    for copy in copies:
        copy.wait()


def finish_users(both, own, other_sum, joined, other_last, items, activity, popularity):
    rows, half = both.shape
    args = [both, own, other_sum, *joined, other_last, *items, activity, popularity]
    out_shape = [
        jax.ShapeDtypeStruct((rows, half), F32),
        jax.ShapeDtypeStruct((activity.shape[1], half), F32),
        jax.ShapeDtypeStruct((popularity.shape[1], half), F32),
    ]
    return pl.pallas_call(
        functools.partial(finish_users_kernel, len(joined), len(items)),
        in_specs=[pl.BlockSpec(memory_space=VMEM)] * len(args),
        out_specs=[pl.BlockSpec(memory_space=HBM)] * 3,
        out_shape=out_shape,
        scratch_shapes=[pltpu.VMEM(o.shape, F32) for o in out_shape] + [pltpu.SemaphoreType.DMA((4,))],
        compiler_params=pltpu.CompilerParams(vmem_limit_bytes=8 * MIB),
        cost_estimate=CHEAP,
        name="finish_users",
    )(*args)


def finish_items_kernel(n, exp_ref, own_ref, *refs):
    out_ref, buf, sems = refs[n:]
    rows = out_ref.shape[0]
    chunk = min(rows, 256)
    copies = []
    for j in range(rows // chunk):
        part = slice(j * chunk, (j + 1) * chunk)
        total = own_ref[:, part]
        for p in range(n):
            total += refs[p][:, part].astype(F32)
        buf[part, :] = 0.3 + exp_ref[part, :].astype(F32) * total.T
        here = pl.ds(j * chunk, chunk)
        copies.append(pltpu.make_async_copy(buf.at[here], out_ref.at[here], sems.at[j]))
        copies[-1].start()
    for copy in copies:
        copy.wait()


def finish_items(item_exp, own, came):
    half, rows = came[0].shape
    return pl.pallas_call(
        functools.partial(finish_items_kernel, len(came)),
        in_specs=[pl.BlockSpec(memory_space=VMEM)] * (2 + len(came)),
        out_specs=pl.BlockSpec(memory_space=HBM),
        out_shape=jax.ShapeDtypeStruct((rows, half), F32),
        scratch_shapes=[pltpu.VMEM((rows, half), F32), pltpu.SemaphoreType.DMA((rows // min(rows, 256),))],
        compiler_params=pltpu.CompilerParams(vmem_limit_bytes=6 * MIB),
        cost_estimate=CHEAP,
        name="finish_items",
    )(item_exp, own, *came)


def along_item(x, shift, n):
    return lax.ppermute(x, "item", [(i, (i + shift) % n) for i in range(n)])


def after(x, y):
    return lax.optimization_barrier((x, y))[0]


def along_user(x, distance, n):
    return lax.ppermute(x, "user", [(i, i ^ distance) for i in range(n)])


def body(
    n_item,
    n_user,
    n_ka,
    counts,
    tile_user,
    tile_item,
    tile_live,
    theta_shape,
    theta_rate,
    user_activity,
    beta_shape,
    beta_rate,
    item_popularity,
):
    def sibling(x):
        return lax.ppermute(x, "ka", [(h, n_ka - 1 - h) for h in range(n_ka)])

    both, item_exp, pack = expected(theta_shape[0], theta_rate[0], beta_shape[0], beta_rate[0])
    rows = both.shape[0]
    half_rows = rows // 2
    item_rows = beta_shape.shape[1] * n_user
    dense = dense_counts(
        counts[0, 0],
        tile_user[0, 0],
        tile_item[0, 0],
        tile_live[0],
        rows,
        n_item,
        item_rows,
        n_user,
    )
    pack, dense = lax.optimization_barrier((pack, dense))
    came_pack = sibling(pack)

    places = [0]
    for d in range(1, n_item // 2 + 1):
        places += [d, -d][: n_item - len(places)]
    shards = [both]
    for i in range(1, n_item):
        step = 1 if places[i] > 0 else -1
        shards.append(along_item(shards[max(i - 2, 0)], step, n_item))

    item_mine = [item_exp]
    for p in range(1, n_user):
        low = p & -p
        item_mine.append(along_user(item_mine[p ^ low], low, n_user))
    item_other = [came_pack] + [sibling(x) for x in item_mine[1:]]

    acc = None
    joined = []
    latest = None
    for i in list(range(1, n_item - 1)) + [0, n_item - 1]:
        last = i == n_item - 1
        passed = after(shards[i], latest) if last else shards[i]
        other = sibling(passed) if i else came_pack
        stats, accs = statistics(i, [shards[i], other], item_mine, item_other, dense, acc, last, half_rows)
        acc = accs[0]
        if i:
            joined.append(along_item(stats[0], -places[i], n_item))
            latest = stats[0] if latest is None else latest
        else:
            own, own_other = stats

    came = [sibling(accs[1])]
    for p in range(1, n_user):
        sent = merge_items(p, acc, sibling(accs[1 + p]))
        came.append(along_user(sent, p, n_user))
    new_beta_shape = finish_items(item_exp, acc, came)

    other_sum = own_other
    for x in joined[:-1]:
        other_sum = lax.optimization_barrier(other_sum + x[half_rows:rows].astype(F32))
    other_sum = other_sum.astype(BF16)
    other_sum = sibling(other_sum)
    other_last = sibling(after(joined[-1], other_sum)[half_rows:rows])
    other_last = after(other_last, new_beta_shape)
    new_theta_shape, new_theta_rate, new_beta_rate = finish_users(
        both, own, other_sum, joined, other_last, item_mine, user_activity, item_popularity
    )
    return (new_theta_shape[None], new_theta_rate[None], new_beta_shape[None], new_beta_rate[None])


def solution(mesh):
    in_specs = (
        P(("parts", "item"), "user", None, None, None),
        P(("parts", "item"), "user", None),
        P(("parts", "item"), "user", None),
        P(("parts", "item"), "user"),
        P(("parts", "user"), "item", "ka"),
        P(("parts", "user"), "item", "ka"),
        P(("parts", "user"), "item"),
        P(("parts", "item"), "user", "ka"),
        P(("parts", "item"), "user", "ka"),
        P(("parts", "item"), "user"),
    )
    out_specs = (
        P(("parts", "user"), "item", "ka"),
        P(("parts", "user"), "item", "ka"),
        P(("parts", "item"), "user", "ka"),
        P(("parts", "item"), "user", "ka"),
    )
    run = functools.partial(body, mesh.shape["item"], mesh.shape["user"], mesh.shape["ka"])
    return jax.shard_map(run, mesh=mesh, in_specs=in_specs, out_specs=out_specs, check_vma=False)
```

```python
import functools

import jax
import jax.numpy as jnp
from jax import lax
from jax.experimental import pallas as pl
from jax.experimental.pallas import tpu as pltpu
from jax.sharding import PartitionSpec as P

BF16 = jnp.bfloat16
F32 = jnp.float32
VMEM = pltpu.MemorySpace.VMEM
SMEM = pltpu.MemorySpace.SMEM
HBM = pltpu.MemorySpace.HBM
EXTRA = 16
MIB = 1024 * 1024
CHEAP = pl.CostEstimate(flops=1024, transcendentals=0, bytes_accessed=1024)
DIMS_NT = (((1,), (1,)), ((), ()))
DIMS_TN = (((0,), (0,)), ((), ()))


def pinned(x):
    return pltpu.with_memory_space_constraint(x, HBM)


def reciprocal(x):
    r = pl.reciprocal(x, approx=True)
    return r * (2.0 - x * r)


def exp_digamma(x, inv_rate):
    w = x * (x + 3.0)
    p = w * (w + 2.0)
    y = x + 4.0
    inv = reciprocal(y * p)
    iy = inv * p
    iy2 = iy * iy
    shift = (2.0 * x + 3.0) * (2.0 * w + 2.0) * (inv * y)
    series = iy * 0.5 + iy2 * (1.0 / 12.0 - iy2 * (1.0 / 120.0 - iy2 * (1.0 / 252.0)))
    return y * inv_rate * jnp.exp(-(series + shift))


def encode(values):
    row = lax.broadcasted_iota(jnp.int32, (EXTRA, values[0].shape[1]), 0)
    out = jnp.zeros(row.shape, F32)
    for i, rest in enumerate(values):
        for j in range(3):
            piece = rest.astype(BF16).astype(F32)
            rest = rest - piece
            out = jnp.where(row == 3 * i + j, piece, out)
    return out.astype(BF16)


def decode(block):
    block = block.astype(F32)
    return [block[3 * i : 3 * i + 1] + block[3 * i + 1 : 3 * i + 2] + block[3 * i + 2 : 3 * i + 3] for i in range(2)]


def chunk_copies(starts, chunk, refs, buffers, sems):
    copies = []
    for j, start in enumerate(starts):
        here = pl.ds(start, chunk)
        copies.append(
            [pltpu.make_async_copy(r.at[here], b.at[here], sems.at[i, j]) for i, (r, b) in enumerate(zip(refs, buffers))]
        )
    for group in copies:
        for copy in group:
            copy.start()
    return copies


def expected_kernel(chunk_u, chunk_i, theta_ref, trate_ref, beta_ref, brate_ref, *refs):
    both_ref, wide_ref, item_ref, pack_ref, theta_buf, trate_buf, beta_buf, brate_buf, user_sems, item_sems = refs
    core = lax.axis_index("ka")
    half = both_ref.shape[0] // 2
    rows = beta_ref.shape[0]
    steps = half // chunk_u
    starts = []
    for side in (1 - core, core):
        starts += [pl.multiple_of(side * half + j * chunk_u, chunk_u) for j in range(steps)]
    item_starts = list(range(0, rows, chunk_i))
    user_copies = chunk_copies(starts, chunk_u, (theta_ref, trate_ref), (theta_buf, trate_buf), user_sems)
    item_copies = chunk_copies(item_starts, chunk_i, (beta_ref, brate_ref), (beta_buf, brate_buf), item_sems)
    theta_total = jnp.zeros((1, both_ref.shape[1]), F32)
    for j, start in enumerate(starts):
        for copy in user_copies[j]:
            copy.wait()
        x = theta_buf[pl.ds(start, chunk_u), :]
        inv_rate = reciprocal(trate_buf[pl.ds(start, chunk_u), :])
        value = exp_digamma(x, inv_rate).astype(BF16)
        at = (j % steps) * chunk_u
        if j < steps:
            both_ref[half + at : half + at + chunk_u, :] = value
            wide_ref[half + at : half + at + chunk_u, :] = value
            pack_ref[at : at + chunk_u, :] = value
        else:
            both_ref[at : at + chunk_u, :] = value
            wide_ref[at : at + chunk_u, :] = value
        theta_total += jnp.sum(x * inv_rate, axis=0, keepdims=True)
    beta_total = jnp.zeros((1, both_ref.shape[1]), F32)
    for j, start in enumerate(item_starts):
        for copy in item_copies[j]:
            copy.wait()
        x = beta_buf[start : start + chunk_i, :]
        inv_rate = reciprocal(brate_buf[start : start + chunk_i, :])
        value = exp_digamma(x, inv_rate).astype(BF16)
        item_ref[start : start + chunk_i, :] = value
        pack_ref[half + start : half + start + chunk_i, :] = value
        beta_total += jnp.sum(x * inv_rate, axis=0, keepdims=True)
    wide_ref[2 * half :, :] = jnp.zeros((2 * EXTRA, wide_ref.shape[1]), BF16)
    extra = encode([theta_total, beta_total])
    item_ref[rows:, :] = extra
    pack_ref[half + rows :, :] = extra


def expected(theta, trate, beta, brate):
    rows, cols = theta.shape
    item_rows = beta.shape[0]
    half = rows // 2
    chunk_u = min(half, 128)
    chunk_i = min(item_rows, 128)
    shapes = [rows, rows + 2 * EXTRA, item_rows + EXTRA, half + item_rows + EXTRA]
    return pl.pallas_call(
        functools.partial(expected_kernel, chunk_u, chunk_i),
        in_specs=[pl.BlockSpec(memory_space=HBM)] * 4,
        out_specs=[pl.BlockSpec(memory_space=VMEM)] * len(shapes),
        out_shape=[jax.ShapeDtypeStruct((r, cols), BF16) for r in shapes],
        scratch_shapes=[
            pltpu.VMEM((rows, cols), F32),
            pltpu.VMEM((rows, cols), F32),
            pltpu.VMEM((item_rows, cols), F32),
            pltpu.VMEM((item_rows, cols), F32),
            pltpu.SemaphoreType.DMA((2, rows // chunk_u)),
            pltpu.SemaphoreType.DMA((2, item_rows // chunk_i)),
        ],
        compiler_params=pltpu.CompilerParams(vmem_limit_bytes=6 * MIB),
        cost_estimate=CHEAP,
        name="expected",
    )(pinned(theta), pinned(trate), pinned(beta), pinned(brate))


def dense_kernel(n_item, shard_tiles, chunk, rows, users_in, items_in, live_ref, counts_ref, out_ref, *scratch):
    users_ref, items_ref, buf, sems, index_sems = scratch
    tile = counts_ref.shape[1]
    half = rows // 2
    piece = min(half, tile)
    n_chunks = counts_ref.shape[0] // chunk
    copies = [
        pltpu.make_async_copy(
            counts_ref.at[pl.ds(c * chunk, chunk)], buf.at[pl.ds(c * chunk, chunk)], sems.at[c]
        )
        for c in range(n_chunks)
    ]
    index_copies = [
        pltpu.make_async_copy(users_in, users_ref, index_sems.at[0]),
        pltpu.make_async_copy(items_in, items_ref, index_sems.at[1]),
    ]
    for copy in index_copies + copies:
        copy.start()
    out_ref[...] = jnp.zeros_like(out_ref)
    for copy in index_copies:
        copy.wait()
    z = lax.axis_index("item")
    x = lax.axis_index("user")
    core = lax.axis_index("ka")
    live = live_ref[0]

    def place(slot, carry):
        item = items_ref[slot]
        owner = lax.div(item, shard_tiles)
        column = (owner ^ x) * shard_tiles + lax.rem(item, shard_tiles)
        col = pl.multiple_of(column * tile, tile)
        for j in range(tile // piece):
            row = users_ref[slot] * tile + j * piece
            shard = lax.div(row, rows)
            within = lax.rem(row, rows)

            @pl.when(lax.div(within, half) == core)
            def _():
                back = lax.rem(z - shard + n_item, n_item)
                step = jnp.where(back == 0, 0, jnp.where(back * 2 <= n_item, 2 * back - 1, 2 * (n_item - back)))
                start = pl.multiple_of(step * half + lax.rem(within, half), piece)
                value = buf[slot, j * piece : (j + 1) * piece, :].astype(F32).astype(BF16)
                out_ref[pl.ds(start, piece), pl.ds(col, tile)] = value

        return carry

    for c in range(n_chunks):
        copies[c].wait()
        lax.fori_loop(c * chunk, jnp.clip(live, c * chunk, (c + 1) * chunk), place, 0)


def dense_counts(counts, users, items, live, rows, n_item, item_rows, n_user):
    slots, tile, _ = counts.shape
    chunk = 8
    out_rows = n_item * rows // 2
    return pl.pallas_call(
        functools.partial(dense_kernel, n_item, item_rows // n_user // tile, chunk, rows),
        in_specs=[pl.BlockSpec(memory_space=m) for m in (HBM, HBM, SMEM, HBM)],
        out_specs=pl.BlockSpec(memory_space=VMEM),
        out_shape=jax.ShapeDtypeStruct((out_rows, item_rows), BF16),
        scratch_shapes=[
            pltpu.SMEM(users.shape, jnp.int32),
            pltpu.SMEM(items.shape, jnp.int32),
            pltpu.VMEM((slots, tile, tile), jnp.int32),
            pltpu.SemaphoreType.DMA((slots // chunk,)),
            pltpu.SemaphoreType.DMA((2,)),
        ],
        compiler_params=pltpu.CompilerParams(vmem_limit_bytes=8 * MIB),
        cost_estimate=CHEAP,
        name="dense_counts",
    )(pinned(users), pinned(items), live, pinned(counts))


def stat_kernel(pieces, half, last, has_acc, at, *refs):
    refs = list(refs)
    take = lambda n: [refs.pop(0) for _ in range(n)]
    mine_ref, other_ref = take(2)
    mine = mine_ref[:half, :]
    other = other_ref[half : 2 * half, :] if at else other_ref[:half, :]
    item_mine = take(pieces)
    item_other = take(pieces)
    (counts_ref,) = take(1)
    (acc_in,) = take(1) if has_acc else (None,)
    stat_refs = take(1 if at else 2)
    acc_refs = take(1 + pieces if last else 1)
    cols = mine.shape[1]
    total_mine = None
    total_other = None
    width = 256
    for p in range(pieces):
        rows = item_mine[p].shape[0] - EXTRA
        skip = item_other[p].shape[0] - EXTRA - rows
        for c in range(rows // width):
            left = item_mine[p][c * width : (c + 1) * width, :]
            right = item_other[p][skip + c * width : skip + (c + 1) * width, :]
            norm = lax.dot_general(mine, left, DIMS_NT, preferred_element_type=F32)
            norm += lax.dot_general(other, right, DIMS_NT, preferred_element_type=F32)
            columns = slice(p * rows + c * width, p * rows + (c + 1) * width)
            grid = counts_ref[at * half : (at + 1) * half, columns].astype(F32)
            ratio = (grid * reciprocal(norm)).astype(BF16)
            stat = jnp.dot(ratio, left, preferred_element_type=F32)
            total_mine = stat if total_mine is None else total_mine + stat
            stat = jnp.dot(ratio, right, preferred_element_type=F32)
            total_other = stat if total_other is None else total_other + stat
            for i, factors in enumerate((mine, other)):
                update = lax.dot_general(factors, ratio, DIMS_TN, preferred_element_type=F32)
                if has_acc:
                    update += acc_in[i * cols : (i + 1) * cols, columns]
                if last and i == 0:
                    acc_refs[0][:, columns] = update
                elif last:
                    acc_refs[1 + p][:, c * width : (c + 1) * width] = update.astype(BF16)
                else:
                    acc_refs[0][i * cols : (i + 1) * cols, columns] = update
    if at:
        stat_refs[0][:half, :] = total_mine.astype(BF16)
        stat_refs[0][half : 2 * half, :] = total_other.astype(BF16)
        stat_refs[0][2 * half :, :] = encode(row_totals(item_mine))
    else:
        stat_refs[0][...] = total_mine
        stat_refs[1][...] = total_other


def sum_totals(blocks):
    sums = None
    for block in blocks:
        came = decode(block)
        sums = came if sums is None else [a + b for a, b in zip(sums, came)]
    return sums


def row_totals(item_refs):
    return sum_totals([ref[-EXTRA:, :] for ref in item_refs])


def statistics(at, users, item_mine, item_other, dense, acc, last, half_rows):
    half = users[0].shape[1]
    item_rows = dense.shape[1]
    args = [*users, *item_mine, *item_other, dense]
    if acc is not None:
        args.append(acc)
    if at:
        out_shape = [jax.ShapeDtypeStruct((2 * half_rows + EXTRA, half), BF16)]
    else:
        out_shape = [jax.ShapeDtypeStruct((half_rows, half), F32)] * 2
    n_stats = len(out_shape)
    if last:
        out_shape.append(jax.ShapeDtypeStruct((half, item_rows), F32))
        out_shape += [jax.ShapeDtypeStruct((half, item_rows // len(item_mine)), BF16) for _ in item_mine]
    else:
        out_shape.append(jax.ShapeDtypeStruct((2 * half, item_rows), F32))
    spec = pl.BlockSpec(memory_space=VMEM)
    out = pl.pallas_call(
        functools.partial(stat_kernel, len(item_mine), half_rows, last, acc is not None, at),
        in_specs=[spec] * len(args),
        out_specs=[spec] * len(out_shape),
        out_shape=out_shape,
        compiler_params=pltpu.CompilerParams(vmem_limit_bytes=16 * MIB),
        cost_estimate=CHEAP,
        name="statistics_%d" % at,
    )(*args)
    return list(out[:n_stats]), list(out[n_stats:])


def add_kernel(stat_ref, came_ref, out_ref):
    rows = stat_ref.shape[0] - EXTRA
    out_ref[:rows, :] = (stat_ref[:rows, :].astype(F32) + came_ref[:rows, :].astype(F32)).astype(BF16)
    out_ref[rows:, :] = encode(sum_totals([stat_ref[rows:, :], came_ref[rows:, :]]))


def add_came(stat, came):
    return pl.pallas_call(
        add_kernel,
        in_specs=[pl.BlockSpec(memory_space=VMEM)] * 2,
        out_specs=pl.BlockSpec(memory_space=VMEM),
        out_shape=jax.ShapeDtypeStruct(stat.shape, BF16),
        compiler_params=pltpu.CompilerParams(vmem_limit_bytes=2 * MIB),
        cost_estimate=CHEAP,
        name="add_came",
    )(stat, came)


def merge_items_kernel(p, mine_ref, came_ref, out_ref):
    width = out_ref.shape[1]
    out_ref[...] = (mine_ref[:, p * width : (p + 1) * width] + came_ref[...].astype(F32)).astype(BF16)


def merge_items(p, mine, came):
    return pl.pallas_call(
        functools.partial(merge_items_kernel, p),
        in_specs=[pl.BlockSpec(memory_space=VMEM)] * 2,
        out_specs=pl.BlockSpec(memory_space=VMEM),
        out_shape=jax.ShapeDtypeStruct(came.shape, BF16),
        compiler_params=pltpu.CompilerParams(vmem_limit_bytes=2 * MIB),
        cost_estimate=CHEAP,
        name="merge_items",
    )(mine, came)


def finish_users_kernel(n_joined, pieces, *refs):
    refs = list(refs)
    take = lambda n: [refs.pop(0) for _ in range(n)]
    both_ref, own_ref, sum_ref = take(3)
    joined = take(n_joined)
    (last_ref,) = take(1)
    item_refs = take(pieces)
    activity_ref, popularity_ref = take(2)
    outs = take(3)
    bufs = take(3)
    (sems,) = take(1)
    core = lax.axis_index("ka")
    half = own_ref.shape[0]
    copies = []

    total = own_ref[...]
    for ref in joined:
        total += ref[:half, :].astype(F32)
    start = pl.multiple_of(core * half, half)
    bufs[0][pl.ds(start, half), :] = 0.3 + both_ref[:half, :].astype(F32) * total
    copies.append(pltpu.make_async_copy(bufs[0].at[pl.ds(start, half)], outs[0].at[pl.ds(start, half)], sems.at[0]))
    copies[-1].start()

    total = sum_ref[...].astype(F32) + last_ref[half : 2 * half, :].astype(F32)
    start = pl.multiple_of((1 - core) * half, half)
    bufs[0][pl.ds(start, half), :] = 0.3 + both_ref[half:, :].astype(F32) * total
    copies.append(pltpu.make_async_copy(bufs[0].at[pl.ds(start, half)], outs[0].at[pl.ds(start, half)], sems.at[1]))
    copies[-1].start()

    theta_total, beta_total = row_totals(item_refs)
    for ref in joined:
        came = decode(ref[-EXTRA:, :])
        theta_total += came[0]
        beta_total += came[1]
    for i, (column_ref, total) in enumerate(((activity_ref, beta_total), (popularity_ref, theta_total))):
        rows = column_ref.shape[1]
        column = jnp.broadcast_to(column_ref[...], (total.shape[1], rows)).T
        bufs[1 + i][...] = column + total
        copies.append(pltpu.make_async_copy(bufs[1 + i], outs[1 + i], sems.at[2 + i]))
        copies[-1].start()
    for copy in copies:
        copy.wait()


def finish_users(both, own, other_sum, joined, other_last, items, activity, popularity):
    rows, half = both.shape
    args = [both, own, other_sum, *joined, other_last, *items, activity, popularity]
    out_shape = [
        jax.ShapeDtypeStruct((rows, half), F32),
        jax.ShapeDtypeStruct((activity.shape[1], half), F32),
        jax.ShapeDtypeStruct((popularity.shape[1], half), F32),
    ]
    return pl.pallas_call(
        functools.partial(finish_users_kernel, len(joined), len(items)),
        in_specs=[pl.BlockSpec(memory_space=VMEM)] * len(args),
        out_specs=[pl.BlockSpec(memory_space=HBM)] * 3,
        out_shape=out_shape,
        scratch_shapes=[pltpu.VMEM(o.shape, F32) for o in out_shape] + [pltpu.SemaphoreType.DMA((4,))],
        compiler_params=pltpu.CompilerParams(vmem_limit_bytes=8 * MIB),
        cost_estimate=CHEAP,
        name="finish_users",
    )(*args)


def finish_items_kernel(n, exp_ref, own_ref, *refs):
    out_ref, buf, sems = refs[n:]
    rows = out_ref.shape[0]
    chunk = min(rows, 256)
    copies = []
    for j in range(rows // chunk):
        part = slice(j * chunk, (j + 1) * chunk)
        total = own_ref[:, part]
        for p in range(n):
            total += refs[p][:, part].astype(F32)
        buf[part, :] = 0.3 + exp_ref[part, :].astype(F32) * total.T
        here = pl.ds(j * chunk, chunk)
        copies.append(pltpu.make_async_copy(buf.at[here], out_ref.at[here], sems.at[j]))
        copies[-1].start()
    for copy in copies:
        copy.wait()


def finish_items(item_exp, own, came):
    half, rows = came[0].shape
    return pl.pallas_call(
        functools.partial(finish_items_kernel, len(came)),
        in_specs=[pl.BlockSpec(memory_space=VMEM)] * (2 + len(came)),
        out_specs=pl.BlockSpec(memory_space=HBM),
        out_shape=jax.ShapeDtypeStruct((rows, half), F32),
        scratch_shapes=[pltpu.VMEM((rows, half), F32), pltpu.SemaphoreType.DMA((rows // min(rows, 256),))],
        compiler_params=pltpu.CompilerParams(vmem_limit_bytes=6 * MIB),
        cost_estimate=CHEAP,
        name="finish_items",
    )(item_exp, own, *came)


def along_item(x, shift, n):
    return lax.ppermute(x, "item", [(i, (i + shift) % n) for i in range(n)])


def after(x, y):
    return lax.optimization_barrier((x, y))[0]


def along_user(x, distance, n):
    return lax.ppermute(x, "user", [(i, i ^ distance) for i in range(n)])


def body(
    n_item,
    n_user,
    n_ka,
    counts,
    tile_user,
    tile_item,
    tile_live,
    theta_shape,
    theta_rate,
    user_activity,
    beta_shape,
    beta_rate,
    item_popularity,
):
    def sibling(x):
        return lax.ppermute(x, "ka", [(h, n_ka - 1 - h) for h in range(n_ka)])

    both, wide, item_exp, pack = expected(theta_shape[0], theta_rate[0], beta_shape[0], beta_rate[0])
    rows = both.shape[0]
    half_rows = rows // 2
    item_rows = beta_shape.shape[1] * n_user
    dense = dense_counts(
        counts[0, 0],
        tile_user[0, 0],
        tile_item[0, 0],
        tile_live[0],
        rows,
        n_item,
        item_rows,
        n_user,
    )
    pack, dense = lax.optimization_barrier((pack, dense))
    came_pack = sibling(pack)

    ahead = range(1, n_item // 2)
    behind = range(1, n_item // 2 + 1)
    shards = {0: both}
    for d in behind:
        shards[2 * d - 1] = along_item(shards[max(2 * d - 3, 0)], 1, n_item)
    for d in ahead:
        shards[2 * d] = along_item(after(wide, shards[1]) if d == 1 else shards[2 * d - 2], -1, n_item)

    item_mine = [item_exp]
    for p in range(1, n_user):
        low = p & -p
        item_mine.append(along_user(item_mine[p ^ low], low, n_user))
    item_other = [came_pack] + [sibling(x) for x in item_mine[1:]]

    order = [2 * d - 1 for d in behind] + [2 * d for d in ahead]
    order.insert(len(order) - 1, 0)
    acc = None
    stats = {}
    latest = None
    for i in order:
        other = sibling(shards[i][:rows]) if i else came_pack
        stats[i], accs = statistics(
            i, [shards[i], other], item_mine, item_other, dense, acc, i == order[-1], half_rows
        )
        acc = accs[0]
        latest = stats[i][0]
    own, own_other = stats[0]

    joined = []
    for distances, step in ((ahead, 1), (behind, -1)):
        moving = None
        for d in reversed(distances):
            stat = stats[2 * d - (step < 0)][0]
            moving = along_item(stat if moving is None else add_came(stat, moving), step, n_item)
        if moving is not None:
            joined.append(moving)

    came = [sibling(accs[1])]
    for p in range(1, n_user):
        sent = merge_items(p, acc, sibling(accs[1 + p]))
        came.append(along_user(sent, p, n_user))
    new_beta_shape = finish_items(item_exp, acc, came)

    other_sum = own_other
    for x in joined[:-1]:
        other_sum = lax.optimization_barrier(other_sum + x[half_rows:rows].astype(F32))
    other_sum = other_sum.astype(BF16)
    other_sum = sibling(other_sum)
    other_last = sibling(joined[-1])
    other_last = after(other_last, new_beta_shape)
    new_theta_shape, new_theta_rate, new_beta_rate = finish_users(
        both, own, other_sum, joined, other_last, item_mine, user_activity, item_popularity
    )
    return (new_theta_shape[None], new_theta_rate[None], new_beta_shape[None], new_beta_rate[None])


def solution(mesh):
    in_specs = (
        P(("parts", "item"), "user", None, None, None),
        P(("parts", "item"), "user", None),
        P(("parts", "item"), "user", None),
        P(("parts", "item"), "user"),
        P(("parts", "user"), "item", "ka"),
        P(("parts", "user"), "item", "ka"),
        P(("parts", "user"), "item"),
        P(("parts", "item"), "user", "ka"),
        P(("parts", "item"), "user", "ka"),
        P(("parts", "item"), "user"),
    )
    out_specs = (
        P(("parts", "user"), "item", "ka"),
        P(("parts", "user"), "item", "ka"),
        P(("parts", "item"), "user", "ka"),
        P(("parts", "item"), "user", "ka"),
    )
    run = functools.partial(body, mesh.shape["item"], mesh.shape["user"], mesh.shape["ka"])
    return jax.shard_map(run, mesh=mesh, in_specs=in_specs, out_specs=out_specs, check_vma=False)
```

```python
import functools

import jax
import jax.numpy as jnp
from jax import lax
from jax.experimental import pallas as pl
from jax.experimental.pallas import tpu as pltpu
from jax.sharding import PartitionSpec as P

BF16 = jnp.bfloat16
F32 = jnp.float32
VMEM = pltpu.MemorySpace.VMEM
SMEM = pltpu.MemorySpace.SMEM
HBM = pltpu.MemorySpace.HBM
EXTRA = 16
MIB = 1024 * 1024
CHEAP = pl.CostEstimate(flops=1024, transcendentals=0, bytes_accessed=1024)
DIMS_NT = (((1,), (1,)), ((), ()))
DIMS_TN = (((0,), (0,)), ((), ()))


def pinned(x):
    return pltpu.with_memory_space_constraint(x, HBM)


def reciprocal(x):
    r = pl.reciprocal(x, approx=True)
    return r * (2.0 - x * r)


def exp_digamma(x, inv_rate):
    w = x * (x + 3.0)
    p = w * (w + 2.0)
    y = x + 4.0
    inv = reciprocal(y * p)
    iy = inv * p
    iy2 = iy * iy
    shift = (2.0 * x + 3.0) * (2.0 * w + 2.0) * (inv * y)
    series = iy * 0.5 + iy2 * (1.0 / 12.0 - iy2 * (1.0 / 120.0 - iy2 * (1.0 / 252.0)))
    return y * inv_rate * jnp.exp(-(series + shift))


def encode(values):
    row = lax.broadcasted_iota(jnp.int32, (EXTRA, values[0].shape[1]), 0)
    out = jnp.zeros(row.shape, F32)
    for i, rest in enumerate(values):
        for j in range(3):
            piece = rest.astype(BF16).astype(F32)
            rest = rest - piece
            out = jnp.where(row == 3 * i + j, piece, out)
    return out.astype(BF16)


def decode(block):
    block = block.astype(F32)
    return [block[3 * i : 3 * i + 1] + block[3 * i + 1 : 3 * i + 2] + block[3 * i + 2 : 3 * i + 3] for i in range(2)]


def chunk_copies(starts, chunk, refs, buffers, sems):
    copies = []
    for j, start in enumerate(starts):
        here = pl.ds(start, chunk)
        copies.append(
            [pltpu.make_async_copy(r.at[here], b.at[here], sems.at[i, j]) for i, (r, b) in enumerate(zip(refs, buffers))]
        )
    for group in copies:
        for copy in group:
            copy.start()
    return copies


def expected_kernel(chunk_u, chunk_i, theta_ref, trate_ref, beta_ref, brate_ref, *refs):
    both_ref, wide_ref, item_ref, pack_ref, theta_buf, trate_buf, beta_buf, brate_buf, user_sems, item_sems = refs
    core = lax.axis_index("ka")
    half = both_ref.shape[0] // 2
    rows = beta_ref.shape[0]
    steps = half // chunk_u
    starts = []
    for side in (1 - core, core):
        starts += [pl.multiple_of(side * half + j * chunk_u, chunk_u) for j in range(steps)]
    item_starts = list(range(0, rows, chunk_i))
    user_copies = chunk_copies(starts, chunk_u, (theta_ref, trate_ref), (theta_buf, trate_buf), user_sems)
    item_copies = chunk_copies(item_starts, chunk_i, (beta_ref, brate_ref), (beta_buf, brate_buf), item_sems)
    theta_total = jnp.zeros((1, both_ref.shape[1]), F32)
    for j, start in enumerate(starts):
        for copy in user_copies[j]:
            copy.wait()
        x = theta_buf[pl.ds(start, chunk_u), :]
        inv_rate = reciprocal(trate_buf[pl.ds(start, chunk_u), :])
        value = exp_digamma(x, inv_rate).astype(BF16)
        at = (j % steps) * chunk_u
        if j < steps:
            both_ref[half + at : half + at + chunk_u, :] = value
            wide_ref[half + at : half + at + chunk_u, :] = value
            pack_ref[at : at + chunk_u, :] = value
        else:
            both_ref[at : at + chunk_u, :] = value
            wide_ref[at : at + chunk_u, :] = value
        theta_total += jnp.sum(x * inv_rate, axis=0, keepdims=True)
    beta_total = jnp.zeros((1, both_ref.shape[1]), F32)
    for j, start in enumerate(item_starts):
        for copy in item_copies[j]:
            copy.wait()
        x = beta_buf[start : start + chunk_i, :]
        inv_rate = reciprocal(brate_buf[start : start + chunk_i, :])
        value = exp_digamma(x, inv_rate).astype(BF16)
        item_ref[start : start + chunk_i, :] = value
        pack_ref[half + start : half + start + chunk_i, :] = value
        beta_total += jnp.sum(x * inv_rate, axis=0, keepdims=True)
    wide_ref[2 * half :, :] = jnp.zeros((3 * EXTRA, wide_ref.shape[1]), BF16)
    extra = encode([theta_total, beta_total])
    item_ref[rows:, :] = extra
    pack_ref[half + rows :, :] = extra


def expected(theta, trate, beta, brate):
    rows, cols = theta.shape
    item_rows = beta.shape[0]
    half = rows // 2
    chunk_u = min(half, 128)
    chunk_i = min(item_rows, 128)
    shapes = [rows, rows + 3 * EXTRA, item_rows + EXTRA, half + item_rows + EXTRA]
    return pl.pallas_call(
        functools.partial(expected_kernel, chunk_u, chunk_i),
        in_specs=[pl.BlockSpec(memory_space=HBM)] * 4,
        out_specs=[pl.BlockSpec(memory_space=VMEM)] * len(shapes),
        out_shape=[jax.ShapeDtypeStruct((r, cols), BF16) for r in shapes],
        scratch_shapes=[
            pltpu.VMEM((rows, cols), F32),
            pltpu.VMEM((rows, cols), F32),
            pltpu.VMEM((item_rows, cols), F32),
            pltpu.VMEM((item_rows, cols), F32),
            pltpu.SemaphoreType.DMA((2, rows // chunk_u)),
            pltpu.SemaphoreType.DMA((2, item_rows // chunk_i)),
        ],
        compiler_params=pltpu.CompilerParams(vmem_limit_bytes=6 * MIB),
        cost_estimate=CHEAP,
        name="expected",
    )(pinned(theta), pinned(trate), pinned(beta), pinned(brate))


def dense_kernel(n_item, shard_tiles, chunk, rows, users_in, items_in, live_ref, counts_ref, out_ref, *scratch):
    users_ref, items_ref, buf, sems, index_sems = scratch
    tile = counts_ref.shape[1]
    half = rows // 2
    piece = min(half, tile)
    n_chunks = counts_ref.shape[0] // chunk
    copies = [
        pltpu.make_async_copy(
            counts_ref.at[pl.ds(c * chunk, chunk)], buf.at[pl.ds(c * chunk, chunk)], sems.at[c]
        )
        for c in range(n_chunks)
    ]
    index_copies = [
        pltpu.make_async_copy(users_in, users_ref, index_sems.at[0]),
        pltpu.make_async_copy(items_in, items_ref, index_sems.at[1]),
    ]
    for copy in index_copies + copies:
        copy.start()
    out_ref[...] = jnp.zeros_like(out_ref)
    for copy in index_copies:
        copy.wait()
    z = lax.axis_index("item")
    x = lax.axis_index("user")
    core = lax.axis_index("ka")
    live = live_ref[0]

    def place(slot, carry):
        item = items_ref[slot]
        owner = lax.div(item, shard_tiles)
        column = (owner ^ x) * shard_tiles + lax.rem(item, shard_tiles)
        col = pl.multiple_of(column * tile, tile)
        for j in range(tile // piece):
            row = users_ref[slot] * tile + j * piece
            shard = lax.div(row, rows)
            within = lax.rem(row, rows)

            @pl.when(lax.div(within, half) == core)
            def _():
                back = lax.rem(z - shard + n_item, n_item)
                step = jnp.where(back == 0, 0, jnp.where(back * 2 <= n_item, 2 * back - 1, 2 * (n_item - back)))
                start = pl.multiple_of(step * half + lax.rem(within, half), piece)
                value = buf[slot, j * piece : (j + 1) * piece, :].astype(F32).astype(BF16)
                out_ref[pl.ds(start, piece), pl.ds(col, tile)] = value

        return carry

    for c in range(n_chunks):
        copies[c].wait()
        lax.fori_loop(c * chunk, jnp.clip(live, c * chunk, (c + 1) * chunk), place, 0)


def dense_counts(counts, users, items, live, rows, n_item, item_rows, n_user):
    slots, tile, _ = counts.shape
    chunk = 8
    out_rows = n_item * rows // 2
    return pl.pallas_call(
        functools.partial(dense_kernel, n_item, item_rows // n_user // tile, chunk, rows),
        in_specs=[pl.BlockSpec(memory_space=m) for m in (HBM, HBM, SMEM, HBM)],
        out_specs=pl.BlockSpec(memory_space=VMEM),
        out_shape=jax.ShapeDtypeStruct((out_rows, item_rows), BF16),
        scratch_shapes=[
            pltpu.SMEM(users.shape, jnp.int32),
            pltpu.SMEM(items.shape, jnp.int32),
            pltpu.VMEM((slots, tile, tile), jnp.int32),
            pltpu.SemaphoreType.DMA((slots // chunk,)),
            pltpu.SemaphoreType.DMA((2,)),
        ],
        compiler_params=pltpu.CompilerParams(vmem_limit_bytes=8 * MIB),
        cost_estimate=CHEAP,
        name="dense_counts",
    )(pinned(users), pinned(items), live, pinned(counts))


def stat_kernel(pieces, half, last, has_acc, at, *refs):
    refs = list(refs)
    take = lambda n: [refs.pop(0) for _ in range(n)]
    mine_ref, other_ref = take(2)
    mine = mine_ref[:half, :]
    other = other_ref[half : 2 * half, :] if at and not last else other_ref[:half, :]
    item_mine = take(pieces)
    item_other = take(pieces)
    (counts_ref,) = take(1)
    (acc_in,) = take(1) if has_acc else (None,)
    stat_refs = take(1 if at else 2)
    acc_refs = take(1 + pieces if last else 1)
    cols = mine.shape[1]
    total_mine = None
    total_other = None
    width = 256
    for p in range(pieces):
        rows = item_mine[p].shape[0] - EXTRA
        skip = item_other[p].shape[0] - EXTRA - rows
        for c in range(rows // width):
            left = item_mine[p][c * width : (c + 1) * width, :]
            right = item_other[p][skip + c * width : skip + (c + 1) * width, :]
            norm = lax.dot_general(mine, left, DIMS_NT, preferred_element_type=F32)
            norm += lax.dot_general(other, right, DIMS_NT, preferred_element_type=F32)
            columns = slice(p * rows + c * width, p * rows + (c + 1) * width)
            grid = counts_ref[at * half : (at + 1) * half, columns].astype(F32)
            ratio = (grid * reciprocal(norm)).astype(BF16)
            stat = jnp.dot(ratio, left, preferred_element_type=F32)
            total_mine = stat if total_mine is None else total_mine + stat
            stat = jnp.dot(ratio, right, preferred_element_type=F32)
            total_other = stat if total_other is None else total_other + stat
            for i, factors in enumerate((mine, other)):
                update = lax.dot_general(factors, ratio, DIMS_TN, preferred_element_type=F32)
                if has_acc:
                    update += acc_in[i * cols : (i + 1) * cols, columns]
                if last and i == 0:
                    acc_refs[0][:, columns] = update
                elif last:
                    acc_refs[1 + p][:, c * width : (c + 1) * width] = update.astype(BF16)
                else:
                    acc_refs[0][i * cols : (i + 1) * cols, columns] = update
    if at:
        stat_refs[0][:half, :] = total_mine.astype(BF16)
        stat_refs[0][half : 2 * half, :] = total_other.astype(BF16)
        stat_refs[0][2 * half :, :] = encode(row_totals(item_mine))
    else:
        stat_refs[0][...] = total_mine
        stat_refs[1][...] = total_other


def sum_totals(blocks):
    sums = None
    for block in blocks:
        came = decode(block)
        sums = came if sums is None else [a + b for a, b in zip(sums, came)]
    return sums


def row_totals(item_refs):
    return sum_totals([ref[-EXTRA:, :] for ref in item_refs])


def statistics(at, users, item_mine, item_other, dense, acc, last, half_rows):
    half = users[0].shape[1]
    item_rows = dense.shape[1]
    args = [*users, *item_mine, *item_other, dense]
    if acc is not None:
        args.append(acc)
    if at:
        out_shape = [jax.ShapeDtypeStruct((2 * half_rows + EXTRA, half), BF16)]
    else:
        out_shape = [jax.ShapeDtypeStruct((half_rows, half), F32)] * 2
    n_stats = len(out_shape)
    if last:
        out_shape.append(jax.ShapeDtypeStruct((half, item_rows), F32))
        out_shape += [jax.ShapeDtypeStruct((half, item_rows // len(item_mine)), BF16) for _ in item_mine]
    else:
        out_shape.append(jax.ShapeDtypeStruct((2 * half, item_rows), F32))
    spec = pl.BlockSpec(memory_space=VMEM)
    out = pl.pallas_call(
        functools.partial(stat_kernel, len(item_mine), half_rows, last, acc is not None, at),
        in_specs=[spec] * len(args),
        out_specs=[spec] * len(out_shape),
        out_shape=out_shape,
        compiler_params=pltpu.CompilerParams(vmem_limit_bytes=16 * MIB),
        cost_estimate=CHEAP,
        name="statistics_%d" % at,
    )(*args)
    return list(out[:n_stats]), list(out[n_stats:])


def add_kernel(stat_ref, came_ref, out_ref):
    rows = stat_ref.shape[0] - EXTRA
    out_ref[:rows, :] = (stat_ref[:rows, :].astype(F32) + came_ref[:rows, :].astype(F32)).astype(BF16)
    out_ref[rows:, :] = encode(sum_totals([stat_ref[rows:, :], came_ref[rows:, :]]))


def add_came(stat, came):
    return pl.pallas_call(
        add_kernel,
        in_specs=[pl.BlockSpec(memory_space=VMEM)] * 2,
        out_specs=pl.BlockSpec(memory_space=VMEM),
        out_shape=jax.ShapeDtypeStruct(stat.shape, BF16),
        compiler_params=pltpu.CompilerParams(vmem_limit_bytes=2 * MIB),
        cost_estimate=CHEAP,
        name="add_came",
    )(stat, came)


def merge_items_kernel(p, mine_ref, came_ref, out_ref):
    width = out_ref.shape[1]
    out_ref[...] = (mine_ref[:, p * width : (p + 1) * width] + came_ref[...].astype(F32)).astype(BF16)


def merge_items(p, mine, came):
    return pl.pallas_call(
        functools.partial(merge_items_kernel, p),
        in_specs=[pl.BlockSpec(memory_space=VMEM)] * 2,
        out_specs=pl.BlockSpec(memory_space=VMEM),
        out_shape=jax.ShapeDtypeStruct(came.shape, BF16),
        compiler_params=pltpu.CompilerParams(vmem_limit_bytes=2 * MIB),
        cost_estimate=CHEAP,
        name="merge_items",
    )(mine, came)


def finish_users_kernel(n_joined, pieces, *refs):
    refs = list(refs)
    take = lambda n: [refs.pop(0) for _ in range(n)]
    both_ref, own_ref, sum_ref = take(3)
    joined = take(n_joined)
    (last_ref,) = take(1)
    item_refs = take(pieces)
    activity_ref, popularity_ref = take(2)
    outs = take(3)
    bufs = take(3)
    (sems,) = take(1)
    core = lax.axis_index("ka")
    half = own_ref.shape[0]
    copies = []

    total = own_ref[...]
    for ref in joined:
        total += ref[:half, :].astype(F32)
    start = pl.multiple_of(core * half, half)
    bufs[0][pl.ds(start, half), :] = 0.3 + both_ref[:half, :].astype(F32) * total
    copies.append(pltpu.make_async_copy(bufs[0].at[pl.ds(start, half)], outs[0].at[pl.ds(start, half)], sems.at[0]))
    copies[-1].start()

    total = sum_ref[:half, :].astype(F32) + last_ref[...].astype(F32)
    start = pl.multiple_of((1 - core) * half, half)
    bufs[0][pl.ds(start, half), :] = 0.3 + both_ref[half:, :].astype(F32) * total
    copies.append(pltpu.make_async_copy(bufs[0].at[pl.ds(start, half)], outs[0].at[pl.ds(start, half)], sems.at[1]))
    copies[-1].start()

    theta_total, beta_total = row_totals(item_refs)
    for ref in joined:
        came = decode(ref[-EXTRA:, :])
        theta_total += came[0]
        beta_total += came[1]
    for i, (column_ref, total) in enumerate(((activity_ref, beta_total), (popularity_ref, theta_total))):
        rows = column_ref.shape[1]
        column = jnp.broadcast_to(column_ref[...], (total.shape[1], rows)).T
        bufs[1 + i][...] = column + total
        copies.append(pltpu.make_async_copy(bufs[1 + i], outs[1 + i], sems.at[2 + i]))
        copies[-1].start()
    for copy in copies:
        copy.wait()


def finish_users(both, own, other_sum, joined, other_last, items, activity, popularity):
    rows, half = both.shape
    args = [both, own, other_sum, *joined, other_last, *items, activity, popularity]
    out_shape = [
        jax.ShapeDtypeStruct((rows, half), F32),
        jax.ShapeDtypeStruct((activity.shape[1], half), F32),
        jax.ShapeDtypeStruct((popularity.shape[1], half), F32),
    ]
    return pl.pallas_call(
        functools.partial(finish_users_kernel, len(joined), len(items)),
        in_specs=[pl.BlockSpec(memory_space=VMEM)] * len(args),
        out_specs=[pl.BlockSpec(memory_space=HBM)] * 3,
        out_shape=out_shape,
        scratch_shapes=[pltpu.VMEM(o.shape, F32) for o in out_shape] + [pltpu.SemaphoreType.DMA((4,))],
        compiler_params=pltpu.CompilerParams(vmem_limit_bytes=8 * MIB),
        cost_estimate=CHEAP,
        name="finish_users",
    )(*args)


def finish_items_kernel(n, exp_ref, own_ref, *refs):
    out_ref, buf, sems = refs[n:]
    rows = out_ref.shape[0]
    chunk = min(rows, 256)
    copies = []
    for j in range(rows // chunk):
        part = slice(j * chunk, (j + 1) * chunk)
        total = own_ref[:, part]
        for p in range(n):
            total += refs[p][:, part].astype(F32)
        buf[part, :] = 0.3 + exp_ref[part, :].astype(F32) * total.T
        here = pl.ds(j * chunk, chunk)
        copies.append(pltpu.make_async_copy(buf.at[here], out_ref.at[here], sems.at[j]))
        copies[-1].start()
    for copy in copies:
        copy.wait()


def finish_items(item_exp, own, came):
    half, rows = came[0].shape
    return pl.pallas_call(
        functools.partial(finish_items_kernel, len(came)),
        in_specs=[pl.BlockSpec(memory_space=VMEM)] * (2 + len(came)),
        out_specs=pl.BlockSpec(memory_space=HBM),
        out_shape=jax.ShapeDtypeStruct((rows, half), F32),
        scratch_shapes=[pltpu.VMEM((rows, half), F32), pltpu.SemaphoreType.DMA((rows // min(rows, 256),))],
        compiler_params=pltpu.CompilerParams(vmem_limit_bytes=6 * MIB),
        cost_estimate=CHEAP,
        name="finish_items",
    )(item_exp, own, *came)


def along_item(x, shift, n):
    return lax.ppermute(x, "item", [(i, (i + shift) % n) for i in range(n)])


def after(x, y):
    return lax.optimization_barrier((x, y))[0]


def along_user(x, distance, n):
    return lax.ppermute(x, "user", [(i, i ^ distance) for i in range(n)])


def body(
    n_item,
    n_user,
    n_ka,
    counts,
    tile_user,
    tile_item,
    tile_live,
    theta_shape,
    theta_rate,
    user_activity,
    beta_shape,
    beta_rate,
    item_popularity,
):
    def sibling(x):
        return lax.ppermute(x, "ka", [(h, n_ka - 1 - h) for h in range(n_ka)])

    both, wide, item_exp, pack = expected(theta_shape[0], theta_rate[0], beta_shape[0], beta_rate[0])
    rows = both.shape[0]
    half_rows = rows // 2
    item_rows = beta_shape.shape[1] * n_user
    dense = dense_counts(
        counts[0, 0],
        tile_user[0, 0],
        tile_item[0, 0],
        tile_live[0],
        rows,
        n_item,
        item_rows,
        n_user,
    )
    came_pack = sibling(pack)

    ahead = range(1, n_item // 2)
    behind = range(1, n_item // 2 + 1)
    shards = {0: both}
    for d in behind:
        shards[2 * d - 1] = along_item(shards[max(2 * d - 3, 0)], 1, n_item)
    for d in ahead:
        shards[2 * d] = along_item(after(wide, shards[1]) if d == 1 else shards[2 * d - 2], -1, n_item)

    item_mine = [item_exp]
    for p in range(1, n_user):
        low = p & -p
        item_mine.append(along_user(after(item_mine[p ^ low], dense), low, n_user))
    item_other = [came_pack] + [sibling(x) for x in item_mine[1:]]

    order = [2 * d - 1 for d in behind] + [2 * d for d in ahead]
    order.insert(len(order) - 1, 0)
    acc = None
    stats = {}
    latest = None
    for i in order:
        passed = after(shards[i], stats[n_item - 1][0])[half_rows:rows] if i == order[-1] else shards[i]
        other = sibling(passed) if i else came_pack
        stats[i], accs = statistics(
            i, [shards[i], other], item_mine, item_other, dense, acc, i == order[-1], half_rows
        )
        acc = accs[0]
        latest = stats[i][0]
    own, own_other = stats[0]

    joined = []
    for distances, step in ((ahead, 1), (behind, -1)):
        moving = None
        for d in reversed(distances):
            stat = stats[2 * d - (step < 0)][0]
            moving = along_item(stat if moving is None else add_came(stat, moving), step, n_item)
        if moving is not None:
            joined.append(moving)

    came = [sibling(accs[1])]
    for p in range(1, n_user):
        sent = merge_items(p, acc, sibling(accs[1 + p]))
        came.append(along_user(sent, p, n_user))
    new_beta_shape = finish_items(item_exp, acc, came)

    other_sum = own_other
    for x in joined[:-1]:
        other_sum = lax.optimization_barrier(other_sum + x[half_rows:rows].astype(F32))
    other_sum = other_sum.astype(BF16)
    other_sum = sibling(jnp.concatenate([other_sum, other_sum[: half_rows // 2]]))
    other_last = sibling(joined[-1][half_rows:rows])
    other_last = after(other_last, new_beta_shape)
    new_theta_shape, new_theta_rate, new_beta_rate = finish_users(
        both, own, other_sum, joined, other_last, item_mine, user_activity, item_popularity
    )
    return (new_theta_shape[None], new_theta_rate[None], new_beta_shape[None], new_beta_rate[None])


def solution(mesh):
    in_specs = (
        P(("parts", "item"), "user", None, None, None),
        P(("parts", "item"), "user", None),
        P(("parts", "item"), "user", None),
        P(("parts", "item"), "user"),
        P(("parts", "user"), "item", "ka"),
        P(("parts", "user"), "item", "ka"),
        P(("parts", "user"), "item"),
        P(("parts", "item"), "user", "ka"),
        P(("parts", "item"), "user", "ka"),
        P(("parts", "item"), "user"),
    )
    out_specs = (
        P(("parts", "user"), "item", "ka"),
        P(("parts", "user"), "item", "ka"),
        P(("parts", "item"), "user", "ka"),
        P(("parts", "item"), "user", "ka"),
    )
    run = functools.partial(body, mesh.shape["item"], mesh.shape["user"], mesh.shape["ka"])
    return jax.shard_map(run, mesh=mesh, in_specs=in_specs, out_specs=out_specs, check_vma=False)
```

```python
import functools

import jax
import jax.numpy as jnp
from jax import lax
from jax.experimental import pallas as pl
from jax.experimental.pallas import tpu as pltpu
from jax.sharding import PartitionSpec as P

BF16 = jnp.bfloat16
F32 = jnp.float32
VMEM = pltpu.MemorySpace.VMEM
SMEM = pltpu.MemorySpace.SMEM
HBM = pltpu.MemorySpace.HBM
EXTRA = 16
MIB = 1024 * 1024
CHEAP = pl.CostEstimate(flops=1024, transcendentals=0, bytes_accessed=1024)
DIMS_NT = (((1,), (1,)), ((), ()))
DIMS_TN = (((0,), (0,)), ((), ()))


def pinned(x):
    return pltpu.with_memory_space_constraint(x, HBM)


def reciprocal(x):
    r = pl.reciprocal(x, approx=True)
    return r * (2.0 - x * r)


def exp_digamma(x, inv_rate):
    w = x * (x + 3.0)
    p = w * (w + 2.0)
    y = x + 4.0
    inv = reciprocal(y * p)
    iy = inv * p
    iy2 = iy * iy
    shift = (2.0 * x + 3.0) * (2.0 * w + 2.0) * (inv * y)
    series = iy * 0.5 + iy2 * (1.0 / 12.0 - iy2 * (1.0 / 120.0 - iy2 * (1.0 / 252.0)))
    return y * inv_rate * jnp.exp(-(series + shift))


def encode(values):
    row = lax.broadcasted_iota(jnp.int32, (EXTRA, values[0].shape[1]), 0)
    out = jnp.zeros(row.shape, F32)
    for i, rest in enumerate(values):
        for j in range(3):
            piece = rest.astype(BF16).astype(F32)
            rest = rest - piece
            out = jnp.where(row == 3 * i + j, piece, out)
    return out.astype(BF16)


def decode(block):
    block = block.astype(F32)
    return [block[3 * i : 3 * i + 1] + block[3 * i + 1 : 3 * i + 2] + block[3 * i + 2 : 3 * i + 3] for i in range(2)]


def chunk_copies(starts, chunk, refs, buffers, sems):
    copies = []
    for j, start in enumerate(starts):
        here = pl.ds(start, chunk)
        copies.append(
            [pltpu.make_async_copy(r.at[here], b.at[here], sems.at[i, j]) for i, (r, b) in enumerate(zip(refs, buffers))]
        )
    for group in copies:
        for copy in group:
            copy.start()
    return copies


def users_kernel(chunk, shape_ref, rate_ref, both_ref, wide_ref, total_ref, shape_buf, rate_buf, sems):
    core = lax.axis_index("ka")
    half = both_ref.shape[0] // 2
    steps = half // chunk
    starts = []
    for side in (core, 1 - core):
        starts += [pl.multiple_of(side * half + j * chunk, chunk) for j in range(steps)]
    copies = chunk_copies(starts, chunk, (shape_ref, rate_ref), (shape_buf, rate_buf), sems)
    total = jnp.zeros(total_ref.shape, F32)
    for j, start in enumerate(starts):
        for copy in copies[j]:
            copy.wait()
        x = shape_buf[pl.ds(start, chunk), :]
        inv_rate = reciprocal(rate_buf[pl.ds(start, chunk), :])
        value = exp_digamma(x, inv_rate).astype(BF16)
        both_ref[j * chunk : (j + 1) * chunk, :] = value
        wide_ref[j * chunk : (j + 1) * chunk, :] = value
        total += jnp.sum(x * inv_rate, axis=0, keepdims=True)
    total_ref[...] = total
    wide_ref[2 * half :, :] = jnp.zeros((wide_ref.shape[0] - 2 * half, wide_ref.shape[1]), BF16)


def expected_users(shape_arg, rate_arg):
    rows, cols = shape_arg.shape
    chunk = min(rows // 2, 128)
    return pl.pallas_call(
        functools.partial(users_kernel, chunk),
        in_specs=[pl.BlockSpec(memory_space=HBM)] * 2,
        out_specs=[pl.BlockSpec(memory_space=VMEM)] * 3,
        out_shape=[
            jax.ShapeDtypeStruct((rows, cols), BF16),
            jax.ShapeDtypeStruct((rows + 3 * EXTRA, cols), BF16),
            jax.ShapeDtypeStruct((1, cols), F32),
        ],
        scratch_shapes=[
            pltpu.VMEM((rows, cols), F32),
            pltpu.VMEM((rows, cols), F32),
            pltpu.SemaphoreType.DMA((2, rows // chunk)),
        ],
        compiler_params=pltpu.CompilerParams(vmem_limit_bytes=4 * MIB),
        cost_estimate=CHEAP,
        name="expected_users",
    )(pinned(shape_arg), pinned(rate_arg))


def items_kernel(chunk, shape_ref, rate_ref, both_ref, theta_ref, item_ref, pack_ref, shape_buf, rate_buf, sems):
    rows = shape_ref.shape[0]
    half = both_ref.shape[0] // 2
    starts = list(range(0, rows, chunk))
    copies = chunk_copies(starts, chunk, (shape_ref, rate_ref), (shape_buf, rate_buf), sems)
    pack_ref[:half, :] = both_ref[half:, :]
    total = jnp.zeros(theta_ref.shape, F32)
    for j, start in enumerate(starts):
        for copy in copies[j]:
            copy.wait()
        x = shape_buf[start : start + chunk, :]
        inv_rate = reciprocal(rate_buf[start : start + chunk, :])
        value = exp_digamma(x, inv_rate).astype(BF16)
        item_ref[start : start + chunk, :] = value
        pack_ref[half + start : half + start + chunk, :] = value
        total += jnp.sum(x * inv_rate, axis=0, keepdims=True)
    extra = encode([theta_ref[...], total])
    item_ref[rows:, :] = extra
    pack_ref[half + rows :, :] = extra


def expected_items(shape_arg, rate_arg, both, theta_local):
    rows, cols = shape_arg.shape
    chunk = min(rows, 128)
    return pl.pallas_call(
        functools.partial(items_kernel, chunk),
        in_specs=[pl.BlockSpec(memory_space=m) for m in (HBM, HBM, VMEM, VMEM)],
        out_specs=[pl.BlockSpec(memory_space=VMEM)] * 2,
        out_shape=[jax.ShapeDtypeStruct((r + EXTRA, cols), BF16) for r in (rows, both.shape[0] // 2 + rows)],
        scratch_shapes=[
            pltpu.VMEM((rows, cols), F32),
            pltpu.VMEM((rows, cols), F32),
            pltpu.SemaphoreType.DMA((2, rows // chunk)),
        ],
        compiler_params=pltpu.CompilerParams(vmem_limit_bytes=4 * MIB),
        cost_estimate=CHEAP,
        name="expected_items",
    )(pinned(shape_arg), pinned(rate_arg), both, theta_local)


def dense_kernel(n_item, shard_tiles, chunk, rows, users_in, items_in, live_ref, counts_ref, out_ref, *scratch):
    users_ref, items_ref, buf, sems, index_sems = scratch
    tile = counts_ref.shape[1]
    half = rows // 2
    piece = min(half, tile)
    n_chunks = counts_ref.shape[0] // chunk
    copies = [
        pltpu.make_async_copy(
            counts_ref.at[pl.ds(c * chunk, chunk)], buf.at[pl.ds(c * chunk, chunk)], sems.at[c]
        )
        for c in range(n_chunks)
    ]
    index_copies = [
        pltpu.make_async_copy(users_in, users_ref, index_sems.at[0]),
        pltpu.make_async_copy(items_in, items_ref, index_sems.at[1]),
    ]
    for copy in index_copies + copies:
        copy.start()
    out_ref[...] = jnp.zeros_like(out_ref)
    for copy in index_copies:
        copy.wait()
    z = lax.axis_index("item")
    x = lax.axis_index("user")
    core = lax.axis_index("ka")
    live = live_ref[0]

    def place(slot, carry):
        item = items_ref[slot]
        owner = lax.div(item, shard_tiles)
        column = (owner ^ x) * shard_tiles + lax.rem(item, shard_tiles)
        col = pl.multiple_of(column * tile, tile)
        for j in range(tile // piece):
            row = users_ref[slot] * tile + j * piece
            shard = lax.div(row, rows)
            within = lax.rem(row, rows)

            @pl.when(lax.div(within, half) == core)
            def _():
                back = lax.rem(z - shard + n_item, n_item)
                step = jnp.where(back == 0, 0, jnp.where(back * 2 <= n_item, 2 * back - 1, 2 * (n_item - back)))
                start = pl.multiple_of(step * half + lax.rem(within, half), piece)
                value = buf[slot, j * piece : (j + 1) * piece, :].astype(F32).astype(BF16)
                out_ref[pl.ds(start, piece), pl.ds(col, tile)] = value

        return carry

    for c in range(n_chunks):
        copies[c].wait()
        lax.fori_loop(c * chunk, jnp.clip(live, c * chunk, (c + 1) * chunk), place, 0)


def dense_counts(counts, users, items, live, rows, n_item, item_rows, n_user):
    slots, tile, _ = counts.shape
    chunk = 8
    out_rows = n_item * rows // 2
    return pl.pallas_call(
        functools.partial(dense_kernel, n_item, item_rows // n_user // tile, chunk, rows),
        in_specs=[pl.BlockSpec(memory_space=m) for m in (HBM, HBM, SMEM, HBM)],
        out_specs=pl.BlockSpec(memory_space=VMEM),
        out_shape=jax.ShapeDtypeStruct((out_rows, item_rows), BF16),
        scratch_shapes=[
            pltpu.SMEM(users.shape, jnp.int32),
            pltpu.SMEM(items.shape, jnp.int32),
            pltpu.VMEM((slots, tile, tile), jnp.int32),
            pltpu.SemaphoreType.DMA((slots // chunk,)),
            pltpu.SemaphoreType.DMA((2,)),
        ],
        compiler_params=pltpu.CompilerParams(vmem_limit_bytes=8 * MIB),
        cost_estimate=CHEAP,
        name="dense_counts",
    )(pinned(users), pinned(items), live, pinned(counts))


def stat_kernel(pieces, half, last, has_acc, at, *refs):
    refs = list(refs)
    take = lambda n: [refs.pop(0) for _ in range(n)]
    mine_ref, other_ref = take(2)
    mine = mine_ref[:half, :]
    other = other_ref[half : 2 * half, :] if at and not last else other_ref[:half, :]
    item_mine = take(pieces)
    item_other = take(pieces)
    (counts_ref,) = take(1)
    (acc_in,) = take(1) if has_acc else (None,)
    stat_refs = take(1 if at else 2)
    acc_refs = take(1 + pieces if last else 1)
    cols = mine.shape[1]
    total_mine = None
    total_other = None
    width = 256
    for p in range(pieces):
        rows = item_mine[p].shape[0] - EXTRA
        skip = item_other[p].shape[0] - EXTRA - rows
        for c in range(rows // width):
            left = item_mine[p][c * width : (c + 1) * width, :]
            right = item_other[p][skip + c * width : skip + (c + 1) * width, :]
            norm = lax.dot_general(mine, left, DIMS_NT, preferred_element_type=F32)
            norm += lax.dot_general(other, right, DIMS_NT, preferred_element_type=F32)
            columns = slice(p * rows + c * width, p * rows + (c + 1) * width)
            grid = counts_ref[at * half : (at + 1) * half, columns].astype(F32)
            ratio = (grid * reciprocal(norm)).astype(BF16)
            stat = jnp.dot(ratio, left, preferred_element_type=F32)
            total_mine = stat if total_mine is None else total_mine + stat
            stat = jnp.dot(ratio, right, preferred_element_type=F32)
            total_other = stat if total_other is None else total_other + stat
            for i, factors in enumerate((mine, other)):
                update = lax.dot_general(factors, ratio, DIMS_TN, preferred_element_type=F32)
                if has_acc:
                    update += acc_in[i * cols : (i + 1) * cols, columns]
                if last and i == 0:
                    acc_refs[0][:, columns] = update
                elif last:
                    acc_refs[1 + p][:, c * width : (c + 1) * width] = update.astype(BF16)
                else:
                    acc_refs[0][i * cols : (i + 1) * cols, columns] = update
    if at:
        stat_refs[0][:half, :] = total_mine.astype(BF16)
        stat_refs[0][half : 2 * half, :] = total_other.astype(BF16)
        stat_refs[0][2 * half :, :] = encode(row_totals(item_mine))
    else:
        stat_refs[0][...] = total_mine
        stat_refs[1][...] = total_other


def sum_totals(blocks):
    sums = None
    for block in blocks:
        came = decode(block)
        sums = came if sums is None else [a + b for a, b in zip(sums, came)]
    return sums


def row_totals(item_refs):
    return sum_totals([ref[-EXTRA:, :] for ref in item_refs])


def statistics(at, users, item_mine, item_other, dense, acc, last, half_rows):
    half = users[0].shape[1]
    item_rows = dense.shape[1]
    args = [*users, *item_mine, *item_other, dense]
    if acc is not None:
        args.append(acc)
    if at:
        out_shape = [jax.ShapeDtypeStruct((2 * half_rows + EXTRA, half), BF16)]
    else:
        out_shape = [jax.ShapeDtypeStruct((half_rows, half), F32)] * 2
    n_stats = len(out_shape)
    if last:
        out_shape.append(jax.ShapeDtypeStruct((half, item_rows), F32))
        out_shape += [jax.ShapeDtypeStruct((half, item_rows // len(item_mine)), BF16) for _ in item_mine]
    else:
        out_shape.append(jax.ShapeDtypeStruct((2 * half, item_rows), F32))
    spec = pl.BlockSpec(memory_space=VMEM)
    out = pl.pallas_call(
        functools.partial(stat_kernel, len(item_mine), half_rows, last, acc is not None, at),
        in_specs=[spec] * len(args),
        out_specs=[spec] * len(out_shape),
        out_shape=out_shape,
        compiler_params=pltpu.CompilerParams(vmem_limit_bytes=16 * MIB),
        cost_estimate=CHEAP,
        name="statistics_%d" % at,
    )(*args)
    return list(out[:n_stats]), list(out[n_stats:])


def add_kernel(stat_ref, came_ref, out_ref):
    rows = stat_ref.shape[0] - EXTRA
    out_ref[:rows, :] = (stat_ref[:rows, :].astype(F32) + came_ref[:rows, :].astype(F32)).astype(BF16)
    out_ref[rows:, :] = encode(sum_totals([stat_ref[rows:, :], came_ref[rows:, :]]))


def add_came(stat, came):
    return pl.pallas_call(
        add_kernel,
        in_specs=[pl.BlockSpec(memory_space=VMEM)] * 2,
        out_specs=pl.BlockSpec(memory_space=VMEM),
        out_shape=jax.ShapeDtypeStruct(stat.shape, BF16),
        compiler_params=pltpu.CompilerParams(vmem_limit_bytes=2 * MIB),
        cost_estimate=CHEAP,
        name="add_came",
    )(stat, came)


def merge_items_kernel(p, mine_ref, came_ref, out_ref):
    width = out_ref.shape[1]
    out_ref[...] = (mine_ref[:, p * width : (p + 1) * width] + came_ref[...].astype(F32)).astype(BF16)


def merge_items(p, mine, came):
    return pl.pallas_call(
        functools.partial(merge_items_kernel, p),
        in_specs=[pl.BlockSpec(memory_space=VMEM)] * 2,
        out_specs=pl.BlockSpec(memory_space=VMEM),
        out_shape=jax.ShapeDtypeStruct(came.shape, BF16),
        compiler_params=pltpu.CompilerParams(vmem_limit_bytes=2 * MIB),
        cost_estimate=CHEAP,
        name="merge_items",
    )(mine, came)


def finish_users_kernel(n_joined, pieces, *refs):
    refs = list(refs)
    take = lambda n: [refs.pop(0) for _ in range(n)]
    both_ref, own_ref, sum_ref = take(3)
    joined = take(n_joined)
    (last_ref,) = take(1)
    item_refs = take(pieces)
    activity_ref, popularity_ref = take(2)
    outs = take(3)
    bufs = take(3)
    (sems,) = take(1)
    core = lax.axis_index("ka")
    half = own_ref.shape[0]
    copies = []

    total = own_ref[...]
    for ref in joined:
        total += ref[:half, :].astype(F32)
    start = pl.multiple_of(core * half, half)
    bufs[0][pl.ds(start, half), :] = 0.3 + both_ref[:half, :].astype(F32) * total
    copies.append(pltpu.make_async_copy(bufs[0].at[pl.ds(start, half)], outs[0].at[pl.ds(start, half)], sems.at[0]))
    copies[-1].start()

    total = sum_ref[:half, :].astype(F32) + last_ref[...].astype(F32)
    start = pl.multiple_of((1 - core) * half, half)
    bufs[0][pl.ds(start, half), :] = 0.3 + both_ref[half:, :].astype(F32) * total
    copies.append(pltpu.make_async_copy(bufs[0].at[pl.ds(start, half)], outs[0].at[pl.ds(start, half)], sems.at[1]))
    copies[-1].start()

    theta_total, beta_total = row_totals(item_refs)
    for ref in joined:
        came = decode(ref[-EXTRA:, :])
        theta_total += came[0]
        beta_total += came[1]
    for i, (column_ref, total) in enumerate(((activity_ref, beta_total), (popularity_ref, theta_total))):
        rows = column_ref.shape[1]
        column = jnp.broadcast_to(column_ref[...], (total.shape[1], rows)).T
        bufs[1 + i][...] = column + total
        copies.append(pltpu.make_async_copy(bufs[1 + i], outs[1 + i], sems.at[2 + i]))
        copies[-1].start()
    for copy in copies:
        copy.wait()


def finish_users(both, own, other_sum, joined, other_last, items, activity, popularity):
    rows, half = both.shape
    args = [both, own, other_sum, *joined, other_last, *items, activity, popularity]
    out_shape = [
        jax.ShapeDtypeStruct((rows, half), F32),
        jax.ShapeDtypeStruct((activity.shape[1], half), F32),
        jax.ShapeDtypeStruct((popularity.shape[1], half), F32),
    ]
    return pl.pallas_call(
        functools.partial(finish_users_kernel, len(joined), len(items)),
        in_specs=[pl.BlockSpec(memory_space=VMEM)] * len(args),
        out_specs=[pl.BlockSpec(memory_space=HBM)] * 3,
        out_shape=out_shape,
        scratch_shapes=[pltpu.VMEM(o.shape, F32) for o in out_shape] + [pltpu.SemaphoreType.DMA((4,))],
        compiler_params=pltpu.CompilerParams(vmem_limit_bytes=8 * MIB),
        cost_estimate=CHEAP,
        name="finish_users",
    )(*args)


def finish_items_kernel(n, exp_ref, own_ref, *refs):
    out_ref, buf, sems = refs[n:]
    rows = out_ref.shape[0]
    chunk = min(rows, 256)
    copies = []
    for j in range(rows // chunk):
        part = slice(j * chunk, (j + 1) * chunk)
        total = own_ref[:, part]
        for p in range(n):
            total += refs[p][:, part].astype(F32)
        buf[part, :] = 0.3 + exp_ref[part, :].astype(F32) * total.T
        here = pl.ds(j * chunk, chunk)
        copies.append(pltpu.make_async_copy(buf.at[here], out_ref.at[here], sems.at[j]))
        copies[-1].start()
    for copy in copies:
        copy.wait()


def finish_items(item_exp, own, came):
    half, rows = came[0].shape
    return pl.pallas_call(
        functools.partial(finish_items_kernel, len(came)),
        in_specs=[pl.BlockSpec(memory_space=VMEM)] * (2 + len(came)),
        out_specs=pl.BlockSpec(memory_space=HBM),
        out_shape=jax.ShapeDtypeStruct((rows, half), F32),
        scratch_shapes=[pltpu.VMEM((rows, half), F32), pltpu.SemaphoreType.DMA((rows // min(rows, 256),))],
        compiler_params=pltpu.CompilerParams(vmem_limit_bytes=6 * MIB),
        cost_estimate=CHEAP,
        name="finish_items",
    )(item_exp, own, *came)


def along_item(x, shift, n):
    return lax.ppermute(x, "item", [(i, (i + shift) % n) for i in range(n)])


def after(x, y):
    return lax.optimization_barrier((x, y))[0]


def along_user(x, distance, n):
    return lax.ppermute(x, "user", [(i, i ^ distance) for i in range(n)])


def body(
    n_item,
    n_user,
    n_ka,
    counts,
    tile_user,
    tile_item,
    tile_live,
    theta_shape,
    theta_rate,
    user_activity,
    beta_shape,
    beta_rate,
    item_popularity,
):
    def sibling(x):
        return lax.ppermute(x, "ka", [(h, n_ka - 1 - h) for h in range(n_ka)])

    both, wide, theta_local = expected_users(theta_shape[0], theta_rate[0])
    item_exp, pack = expected_items(beta_shape[0], beta_rate[0], both, theta_local)
    rows = both.shape[0]
    half_rows = rows // 2
    item_rows = beta_shape.shape[1] * n_user
    dense = dense_counts(
        counts[0, 0],
        tile_user[0, 0],
        tile_item[0, 0],
        tile_live[0],
        rows,
        n_item,
        item_rows,
        n_user,
    )
    came_pack = sibling(pack)

    ahead = range(1, n_item // 2)
    behind = range(1, n_item // 2 + 1)
    shards = {0: both}
    for d in behind:
        shards[2 * d - 1] = along_item(shards[max(2 * d - 3, 0)], 1, n_item)
    for d in ahead:
        shards[2 * d] = along_item(after(wide, shards[1]) if d == 1 else shards[2 * d - 2], -1, n_item)

    item_mine = [item_exp]
    for p in range(1, n_user):
        low = p & -p
        item_mine.append(along_user(after(item_mine[p ^ low], dense), low, n_user))
    item_other = [came_pack] + [sibling(x) for x in item_mine[1:]]

    order = [2 * d - 1 for d in behind] + [2 * d for d in ahead]
    order.insert(len(order) - 1, 0)
    acc = None
    stats = {}
    latest = None
    for i in order:
        passed = after(shards[i], stats[n_item - 1][0])[half_rows:rows] if i == order[-1] else shards[i]
        other = sibling(passed) if i else came_pack
        stats[i], accs = statistics(
            i, [shards[i], other], item_mine, item_other, dense, acc, i == order[-1], half_rows
        )
        acc = accs[0]
        latest = stats[i][0]
    own, own_other = stats[0]

    joined = []
    for distances, step in ((ahead, 1), (behind, -1)):
        moving = None
        for d in reversed(distances):
            stat = stats[2 * d - (step < 0)][0]
            moving = along_item(stat if moving is None else add_came(stat, moving), step, n_item)
        if moving is not None:
            joined.append(moving)

    came = [sibling(accs[1])]
    for p in range(1, n_user):
        sent = merge_items(p, acc, sibling(accs[1 + p]))
        came.append(along_user(sent, p, n_user))
    new_beta_shape = finish_items(item_exp, acc, came)

    other_sum = own_other
    for x in joined[:-1]:
        other_sum = lax.optimization_barrier(other_sum + x[half_rows:rows].astype(F32))
    other_sum = other_sum.astype(BF16)
    other_sum = sibling(jnp.concatenate([other_sum, other_sum[: half_rows // 2]]))
    other_last = sibling(joined[-1][half_rows:rows])
    other_last = after(other_last, new_beta_shape)
    new_theta_shape, new_theta_rate, new_beta_rate = finish_users(
        both, own, other_sum, joined, other_last, item_mine, user_activity, item_popularity
    )
    return (new_theta_shape[None], new_theta_rate[None], new_beta_shape[None], new_beta_rate[None])


def solution(mesh):
    in_specs = (
        P(("parts", "item"), "user", None, None, None),
        P(("parts", "item"), "user", None),
        P(("parts", "item"), "user", None),
        P(("parts", "item"), "user"),
        P(("parts", "user"), "item", "ka"),
        P(("parts", "user"), "item", "ka"),
        P(("parts", "user"), "item"),
        P(("parts", "item"), "user", "ka"),
        P(("parts", "item"), "user", "ka"),
        P(("parts", "item"), "user"),
    )
    out_specs = (
        P(("parts", "user"), "item", "ka"),
        P(("parts", "user"), "item", "ka"),
        P(("parts", "item"), "user", "ka"),
        P(("parts", "item"), "user", "ka"),
    )
    run = functools.partial(body, mesh.shape["item"], mesh.shape["user"], mesh.shape["ka"])
    return jax.shard_map(run, mesh=mesh, in_specs=in_specs, out_specs=out_specs, check_vma=False)
```

```python
import functools

import jax
import jax.numpy as jnp
from jax import lax
from jax.experimental import pallas as pl
from jax.experimental.pallas import tpu as pltpu
from jax.sharding import PartitionSpec as P

BF16 = jnp.bfloat16
F32 = jnp.float32
VMEM = pltpu.MemorySpace.VMEM
SMEM = pltpu.MemorySpace.SMEM
HBM = pltpu.MemorySpace.HBM
EXTRA = 16
MIB = 1024 * 1024
CHEAP = pl.CostEstimate(flops=1024, transcendentals=0, bytes_accessed=1024)
DIMS_NT = (((1,), (1,)), ((), ()))
DIMS_TN = (((0,), (0,)), ((), ()))


def pinned(x):
    return pltpu.with_memory_space_constraint(x, HBM)


def reciprocal(x):
    r = pl.reciprocal(x, approx=True)
    return r * (2.0 - x * r)


def exp_digamma(x, inv_rate):
    w = x * (x + 3.0)
    p = w * (w + 2.0)
    y = x + 4.0
    inv = reciprocal(y * p)
    iy = inv * p
    iy2 = iy * iy
    shift = (2.0 * x + 3.0) * (2.0 * w + 2.0) * (inv * y)
    series = iy * 0.5 + iy2 * (1.0 / 12.0 - iy2 * (1.0 / 120.0 - iy2 * (1.0 / 252.0)))
    return y * inv_rate * jnp.exp(-(series + shift))


def encode(values):
    row = lax.broadcasted_iota(jnp.int32, (EXTRA, values[0].shape[1]), 0)
    out = jnp.zeros(row.shape, F32)
    for i, rest in enumerate(values):
        for j in range(3):
            piece = rest.astype(BF16).astype(F32)
            rest = rest - piece
            out = jnp.where(row == 3 * i + j, piece, out)
    return out.astype(BF16)


def decode(block):
    block = block.astype(F32)
    return [block[3 * i : 3 * i + 1] + block[3 * i + 1 : 3 * i + 2] + block[3 * i + 2 : 3 * i + 3] for i in range(2)]


def chunk_copies(starts, chunk, refs, buffers, sems):
    copies = []
    for j, start in enumerate(starts):
        here = pl.ds(start, chunk)
        copies.append(
            [pltpu.make_async_copy(r.at[here], b.at[here], sems.at[i, j]) for i, (r, b) in enumerate(zip(refs, buffers))]
        )
    for group in copies:
        for copy in group:
            copy.start()
    return copies


def users_kernel(chunk, shape_ref, rate_ref, both_ref, wide_ref, total_ref, shape_buf, rate_buf, sems):
    core = lax.axis_index("ka")
    half = both_ref.shape[0] // 2
    steps = half // chunk
    starts = []
    for side in (core, 1 - core):
        starts += [pl.multiple_of(side * half + j * chunk, chunk) for j in range(steps)]
    copies = chunk_copies(starts, chunk, (shape_ref, rate_ref), (shape_buf, rate_buf), sems)
    total = jnp.zeros(total_ref.shape, F32)
    for j, start in enumerate(starts):
        for copy in copies[j]:
            copy.wait()
        x = shape_buf[pl.ds(start, chunk), :]
        inv_rate = reciprocal(rate_buf[pl.ds(start, chunk), :])
        value = exp_digamma(x, inv_rate).astype(BF16)
        both_ref[j * chunk : (j + 1) * chunk, :] = value
        wide_ref[j * chunk : (j + 1) * chunk, :] = value
        total += jnp.sum(x * inv_rate, axis=0, keepdims=True)
    total_ref[...] = total
    wide_ref[2 * half :, :] = jnp.zeros((wide_ref.shape[0] - 2 * half, wide_ref.shape[1]), BF16)


def expected_users(shape_arg, rate_arg):
    rows, cols = shape_arg.shape
    chunk = min(rows // 2, 128)
    return pl.pallas_call(
        functools.partial(users_kernel, chunk),
        in_specs=[pl.BlockSpec(memory_space=HBM)] * 2,
        out_specs=[pl.BlockSpec(memory_space=VMEM)] * 3,
        out_shape=[
            jax.ShapeDtypeStruct((rows, cols), BF16),
            jax.ShapeDtypeStruct((rows + 3 * EXTRA, cols), BF16),
            jax.ShapeDtypeStruct((1, cols), F32),
        ],
        scratch_shapes=[
            pltpu.VMEM((rows, cols), F32),
            pltpu.VMEM((rows, cols), F32),
            pltpu.SemaphoreType.DMA((2, rows // chunk)),
        ],
        compiler_params=pltpu.CompilerParams(vmem_limit_bytes=4 * MIB),
        cost_estimate=CHEAP,
        name="expected_users",
    )(pinned(shape_arg), pinned(rate_arg))


def items_kernel(chunk, shape_ref, rate_ref, both_ref, theta_ref, item_ref, pack_ref, shape_buf, rate_buf, sems):
    rows = shape_ref.shape[0]
    half = both_ref.shape[0] // 2
    starts = list(range(0, rows, chunk))
    copies = chunk_copies(starts, chunk, (shape_ref, rate_ref), (shape_buf, rate_buf), sems)
    pack_ref[:half, :] = both_ref[half:, :]
    total = jnp.zeros(theta_ref.shape, F32)
    for j, start in enumerate(starts):
        for copy in copies[j]:
            copy.wait()
        x = shape_buf[start : start + chunk, :]
        inv_rate = reciprocal(rate_buf[start : start + chunk, :])
        value = exp_digamma(x, inv_rate).astype(BF16)
        item_ref[start : start + chunk, :] = value
        pack_ref[half + start : half + start + chunk, :] = value
        total += jnp.sum(x * inv_rate, axis=0, keepdims=True)
    extra = encode([theta_ref[...], total])
    item_ref[rows:, :] = extra
    pack_ref[half + rows :, :] = extra


def expected_items(shape_arg, rate_arg, both, theta_local):
    rows, cols = shape_arg.shape
    chunk = min(rows, 128)
    return pl.pallas_call(
        functools.partial(items_kernel, chunk),
        in_specs=[pl.BlockSpec(memory_space=m) for m in (HBM, HBM, VMEM, VMEM)],
        out_specs=[pl.BlockSpec(memory_space=VMEM)] * 2,
        out_shape=[jax.ShapeDtypeStruct((r + EXTRA, cols), BF16) for r in (rows, both.shape[0] // 2 + rows)],
        scratch_shapes=[
            pltpu.VMEM((rows, cols), F32),
            pltpu.VMEM((rows, cols), F32),
            pltpu.SemaphoreType.DMA((2, rows // chunk)),
        ],
        compiler_params=pltpu.CompilerParams(vmem_limit_bytes=4 * MIB),
        cost_estimate=CHEAP,
        name="expected_items",
    )(pinned(shape_arg), pinned(rate_arg), both, theta_local)


def dense_kernel(n_item, shard_tiles, chunk, rows, users_in, items_in, live_ref, counts_ref, out_ref, *scratch):
    users_ref, items_ref, buf, sems, index_sems = scratch
    tile = counts_ref.shape[1]
    half = rows // 2
    piece = min(half, tile)
    n_chunks = counts_ref.shape[0] // chunk
    copies = [
        pltpu.make_async_copy(
            counts_ref.at[pl.ds(c * chunk, chunk)], buf.at[pl.ds(c * chunk, chunk)], sems.at[c]
        )
        for c in range(n_chunks)
    ]
    index_copies = [
        pltpu.make_async_copy(users_in, users_ref, index_sems.at[0]),
        pltpu.make_async_copy(items_in, items_ref, index_sems.at[1]),
    ]
    for copy in index_copies + copies:
        copy.start()
    out_ref[...] = jnp.zeros_like(out_ref)
    for copy in index_copies:
        copy.wait()
    z = lax.axis_index("item")
    x = lax.axis_index("user")
    core = lax.axis_index("ka")
    live = live_ref[0]

    def place(slot, carry):
        item = items_ref[slot]
        owner = lax.div(item, shard_tiles)
        column = (owner ^ x) * shard_tiles + lax.rem(item, shard_tiles)
        col = pl.multiple_of(column * tile, tile)
        for j in range(tile // piece):
            row = users_ref[slot] * tile + j * piece
            shard = lax.div(row, rows)
            within = lax.rem(row, rows)

            @pl.when(lax.div(within, half) == core)
            def _():
                back = lax.rem(z - shard + n_item, n_item)
                step = jnp.where(back == 0, 0, jnp.where(back * 2 <= n_item, 2 * back - 1, 2 * (n_item - back)))
                start = pl.multiple_of(step * half + lax.rem(within, half), piece)
                value = buf[slot, j * piece : (j + 1) * piece, :].astype(F32).astype(BF16)
                out_ref[pl.ds(start, piece), pl.ds(col, tile)] = value

        return carry

    for c in range(n_chunks):
        copies[c].wait()
        lax.fori_loop(c * chunk, jnp.clip(live, c * chunk, (c + 1) * chunk), place, 0)


def dense_counts(counts, users, items, live, rows, n_item, item_rows, n_user):
    slots, tile, _ = counts.shape
    chunk = 8
    out_rows = n_item * rows // 2
    return pl.pallas_call(
        functools.partial(dense_kernel, n_item, item_rows // n_user // tile, chunk, rows),
        in_specs=[pl.BlockSpec(memory_space=m) for m in (HBM, HBM, SMEM, HBM)],
        out_specs=pl.BlockSpec(memory_space=VMEM),
        out_shape=jax.ShapeDtypeStruct((out_rows, item_rows), BF16),
        scratch_shapes=[
            pltpu.SMEM(users.shape, jnp.int32),
            pltpu.SMEM(items.shape, jnp.int32),
            pltpu.VMEM((slots, tile, tile), jnp.int32),
            pltpu.SemaphoreType.DMA((slots // chunk,)),
            pltpu.SemaphoreType.DMA((2,)),
        ],
        compiler_params=pltpu.CompilerParams(vmem_limit_bytes=8 * MIB),
        cost_estimate=CHEAP,
        name="dense_counts",
    )(pinned(users), pinned(items), live, pinned(counts))


def stat_kernel(pieces, half, last, has_acc, at, *refs):
    refs = list(refs)
    take = lambda n: [refs.pop(0) for _ in range(n)]
    mine_ref, other_ref = take(2)
    mine = mine_ref[:half, :]
    other = other_ref[half : 2 * half, :] if at and not last else other_ref[:half, :]
    item_mine = take(pieces)
    item_other = take(pieces)
    (counts_ref,) = take(1)
    (acc_in,) = take(1) if has_acc else (None,)
    stat_refs = take(1 if at else 2)
    acc_refs = take(1 + pieces if last else 1)
    cols = mine.shape[1]
    total_mine = None
    total_other = None
    width = 256
    for p in range(pieces):
        rows = item_mine[p].shape[0] - EXTRA
        skip = item_other[p].shape[0] - EXTRA - rows
        for c in range(rows // width):
            left = item_mine[p][c * width : (c + 1) * width, :]
            right = item_other[p][skip + c * width : skip + (c + 1) * width, :]
            norm = lax.dot_general(mine, left, DIMS_NT, preferred_element_type=F32)
            norm += lax.dot_general(other, right, DIMS_NT, preferred_element_type=F32)
            columns = slice(p * rows + c * width, p * rows + (c + 1) * width)
            grid = counts_ref[at * half : (at + 1) * half, columns].astype(F32)
            ratio = (grid * reciprocal(norm)).astype(BF16)
            stat = jnp.dot(ratio, left, preferred_element_type=F32)
            total_mine = stat if total_mine is None else total_mine + stat
            stat = jnp.dot(ratio, right, preferred_element_type=F32)
            total_other = stat if total_other is None else total_other + stat
            for i, factors in enumerate((mine, other)):
                update = lax.dot_general(factors, ratio, DIMS_TN, preferred_element_type=F32)
                if has_acc:
                    update += acc_in[i * cols : (i + 1) * cols, columns]
                if last and i == 0:
                    acc_refs[0][:, columns] = update
                elif last:
                    acc_refs[1 + p][:, c * width : (c + 1) * width] = update.astype(BF16)
                else:
                    acc_refs[0][i * cols : (i + 1) * cols, columns] = update
    if at:
        stat_refs[0][:half, :] = total_mine.astype(BF16)
        stat_refs[0][half : 2 * half, :] = total_other.astype(BF16)
        stat_refs[0][2 * half :, :] = encode(row_totals(item_mine))
    else:
        stat_refs[0][...] = total_mine
        stat_refs[1][...] = total_other


def sum_totals(blocks):
    sums = None
    for block in blocks:
        came = decode(block)
        sums = came if sums is None else [a + b for a, b in zip(sums, came)]
    return sums


def row_totals(item_refs):
    return sum_totals([ref[-EXTRA:, :] for ref in item_refs])


def statistics(at, users, item_mine, item_other, dense, acc, last, half_rows):
    half = users[0].shape[1]
    item_rows = dense.shape[1]
    args = [*users, *item_mine, *item_other, dense]
    if acc is not None:
        args.append(acc)
    if at:
        out_shape = [jax.ShapeDtypeStruct((2 * half_rows + EXTRA, half), BF16)]
    else:
        out_shape = [jax.ShapeDtypeStruct((half_rows, half), F32)] * 2
    n_stats = len(out_shape)
    if last:
        out_shape.append(jax.ShapeDtypeStruct((half, item_rows), F32))
        out_shape += [jax.ShapeDtypeStruct((half, item_rows // len(item_mine)), BF16) for _ in item_mine]
    else:
        out_shape.append(jax.ShapeDtypeStruct((2 * half, item_rows), F32))
    spec = pl.BlockSpec(memory_space=VMEM)
    out = pl.pallas_call(
        functools.partial(stat_kernel, len(item_mine), half_rows, last, acc is not None, at),
        in_specs=[spec] * len(args),
        out_specs=[spec] * len(out_shape),
        out_shape=out_shape,
        compiler_params=pltpu.CompilerParams(vmem_limit_bytes=16 * MIB),
        cost_estimate=CHEAP,
        name="statistics_%d" % at,
    )(*args)
    return list(out[:n_stats]), list(out[n_stats:])


def add_kernel(stat_ref, came_ref, out_ref):
    rows = stat_ref.shape[0] - EXTRA
    out_ref[:rows, :] = (stat_ref[:rows, :].astype(F32) + came_ref[:rows, :].astype(F32)).astype(BF16)
    out_ref[rows:, :] = encode(sum_totals([stat_ref[rows:, :], came_ref[rows:, :]]))


def split_kernel(stat_ref, came_ref, other_ref, mine_ref):
    half = other_ref.shape[0] - EXTRA
    total = stat_ref[: 2 * half, :].astype(F32) + came_ref[: 2 * half, :].astype(F32)
    other_ref[:half, :] = total[half:, :].astype(BF16)
    other_ref[half:, :] = encode(sum_totals([stat_ref[2 * half :, :], came_ref[2 * half :, :]]))
    mine_ref[:half, :] = total[:half, :].astype(BF16)
    mine_ref[half:, :] = jnp.zeros((2 * EXTRA, mine_ref.shape[1]), BF16)


def add_came(stat, came, split):
    rows, cols = stat.shape
    half = (rows - EXTRA) // 2
    shapes = [half + EXTRA, half + 2 * EXTRA] if split else [rows]
    out = pl.pallas_call(
        split_kernel if split else add_kernel,
        in_specs=[pl.BlockSpec(memory_space=VMEM)] * 2,
        out_specs=[pl.BlockSpec(memory_space=VMEM)] * len(shapes),
        out_shape=[jax.ShapeDtypeStruct((r, cols), BF16) for r in shapes],
        compiler_params=pltpu.CompilerParams(vmem_limit_bytes=2 * MIB),
        cost_estimate=CHEAP,
        name="add_came",
    )(stat, came)
    return list(out)


def merge_items_kernel(p, mine_ref, came_ref, out_ref):
    width = out_ref.shape[1]
    out_ref[...] = (mine_ref[:, p * width : (p + 1) * width] + came_ref[...].astype(F32)).astype(BF16)


def merge_items(p, mine, came):
    return pl.pallas_call(
        functools.partial(merge_items_kernel, p),
        in_specs=[pl.BlockSpec(memory_space=VMEM)] * 2,
        out_specs=pl.BlockSpec(memory_space=VMEM),
        out_shape=jax.ShapeDtypeStruct(came.shape, BF16),
        compiler_params=pltpu.CompilerParams(vmem_limit_bytes=2 * MIB),
        cost_estimate=CHEAP,
        name="merge_items",
    )(mine, came)


def finish_rates_kernel(pieces, n_came, *refs):
    refs = list(refs)
    take = lambda n: [refs.pop(0) for _ in range(n)]
    item_refs = take(pieces)
    came = take(n_came)
    columns = take(2)
    outs = take(2)
    bufs = take(2)
    (sems,) = take(1)
    theta_total, beta_total = sum_totals([ref[-EXTRA:, :] for ref in item_refs + came])
    copies = []
    for i, total in enumerate((beta_total, theta_total)):
        rows = columns[i].shape[1]
        column = jnp.broadcast_to(columns[i][...], (total.shape[1], rows)).T
        bufs[i][...] = column + total
        copies.append(pltpu.make_async_copy(bufs[i], outs[i], sems.at[i]))
        copies[-1].start()
    for copy in copies:
        copy.wait()


def finish_rates(items, came, activity, popularity):
    args = [*items, *came, activity, popularity]
    out_shape = [jax.ShapeDtypeStruct((c.shape[1], items[0].shape[1]), F32) for c in (activity, popularity)]
    return pl.pallas_call(
        functools.partial(finish_rates_kernel, len(items), len(came)),
        in_specs=[pl.BlockSpec(memory_space=VMEM)] * len(args),
        out_specs=[pl.BlockSpec(memory_space=HBM)] * 2,
        out_shape=out_shape,
        scratch_shapes=[pltpu.VMEM(o.shape, F32) for o in out_shape] + [pltpu.SemaphoreType.DMA((2,))],
        compiler_params=pltpu.CompilerParams(vmem_limit_bytes=6 * MIB),
        cost_estimate=CHEAP,
        name="finish_rates",
    )(*args)


def finish_users_kernel(n_ahead, *refs):
    refs = list(refs)
    take = lambda n: [refs.pop(0) for _ in range(n)]
    both_ref, own_ref, other_ref, last_ref, mine_ref = take(5)
    ahead = take(n_ahead)
    out_ref, buf, sems = take(3)
    core = lax.axis_index("ka")
    half = own_ref.shape[0]

    def send(i, side, rows, total):
        here = pl.ds(pl.multiple_of(side * half, half), half)
        buf[here, :] = 0.3 + both_ref[rows, :].astype(F32) * total
        copy = pltpu.make_async_copy(buf.at[here], out_ref.at[here], sems.at[i])
        copy.start()
        return copy

    total = own_ref[...] + mine_ref[:half, :].astype(F32)
    for ref in ahead:
        total += ref[:half, :].astype(F32)
    other = other_ref[...].astype(F32) + last_ref[:half, :].astype(F32)
    copies = [send(0, core, slice(0, half), total), send(1, 1 - core, slice(half, 2 * half), other)]
    for copy in copies:
        copy.wait()


def finish_users(both, own, other_sum, other_last, mine, ahead):
    rows, half = both.shape
    args = [both, own, other_sum, other_last, mine, *ahead]
    return pl.pallas_call(
        functools.partial(finish_users_kernel, len(ahead)),
        in_specs=[pl.BlockSpec(memory_space=VMEM)] * len(args),
        out_specs=pl.BlockSpec(memory_space=HBM),
        out_shape=jax.ShapeDtypeStruct((rows, half), F32),
        scratch_shapes=[pltpu.VMEM((rows, half), F32), pltpu.SemaphoreType.DMA((2,))],
        compiler_params=pltpu.CompilerParams(vmem_limit_bytes=4 * MIB),
        cost_estimate=CHEAP,
        name="finish_users",
    )(*args)


def finish_items_kernel(n, exp_ref, own_ref, *refs):
    out_ref, buf, sems = refs[n:]
    rows = out_ref.shape[0]
    chunk = min(rows, 256)
    copies = []
    for j in range(rows // chunk):
        part = slice(j * chunk, (j + 1) * chunk)
        total = own_ref[:, part]
        for p in range(n):
            total += refs[p][:, part].astype(F32)
        buf[part, :] = 0.3 + exp_ref[part, :].astype(F32) * total.T
        here = pl.ds(j * chunk, chunk)
        copies.append(pltpu.make_async_copy(buf.at[here], out_ref.at[here], sems.at[j]))
        copies[-1].start()
    for copy in copies:
        copy.wait()


def finish_items(item_exp, own, came):
    half, rows = came[0].shape
    return pl.pallas_call(
        functools.partial(finish_items_kernel, len(came)),
        in_specs=[pl.BlockSpec(memory_space=VMEM)] * (2 + len(came)),
        out_specs=pl.BlockSpec(memory_space=HBM),
        out_shape=jax.ShapeDtypeStruct((rows, half), F32),
        scratch_shapes=[pltpu.VMEM((rows, half), F32), pltpu.SemaphoreType.DMA((rows // min(rows, 256),))],
        compiler_params=pltpu.CompilerParams(vmem_limit_bytes=6 * MIB),
        cost_estimate=CHEAP,
        name="finish_items",
    )(item_exp, own, *came)


def along_item(x, shift, n):
    return lax.ppermute(x, "item", [(i, (i + shift) % n) for i in range(n)])


def after(x, y):
    return lax.optimization_barrier((x, y))[0]


def along_user(x, distance, n):
    return lax.ppermute(x, "user", [(i, i ^ distance) for i in range(n)])


def body(
    n_item,
    n_user,
    n_ka,
    counts,
    tile_user,
    tile_item,
    tile_live,
    theta_shape,
    theta_rate,
    user_activity,
    beta_shape,
    beta_rate,
    item_popularity,
):
    def sibling(x):
        return lax.ppermute(x, "ka", [(h, n_ka - 1 - h) for h in range(n_ka)])

    both, wide, theta_local = expected_users(theta_shape[0], theta_rate[0])
    item_exp, pack = expected_items(beta_shape[0], beta_rate[0], both, theta_local)
    rows = both.shape[0]
    half_rows = rows // 2
    item_rows = beta_shape.shape[1] * n_user
    dense = dense_counts(
        counts[0, 0],
        tile_user[0, 0],
        tile_item[0, 0],
        tile_live[0],
        rows,
        n_item,
        item_rows,
        n_user,
    )
    came_pack = sibling(pack)

    ahead = range(1, n_item // 2)
    behind = range(1, n_item // 2 + 1)
    shards = {0: both}
    for d in behind:
        shards[2 * d - 1] = along_item(shards[max(2 * d - 3, 0)], 1, n_item)
    for d in ahead:
        shards[2 * d] = along_item(after(wide, shards[1]) if d == 1 else shards[2 * d - 2], -1, n_item)

    item_mine = [item_exp]
    for p in range(1, n_user):
        low = p & -p
        item_mine.append(along_user(after(item_mine[p ^ low], dense), low, n_user))
    item_other = [came_pack] + [sibling(x) for x in item_mine[1:]]

    order = [2 * d - 1 for d in behind] + [2 * d for d in ahead]
    order.insert(len(order) - 1, 0)
    acc = None
    stats = {}
    latest = None
    for i in order:
        passed = after(shards[i], stats[n_item - 1][0])[half_rows:rows] if i == order[-1] else shards[i]
        other = sibling(passed) if i else came_pack
        stats[i], accs = statistics(
            i, [shards[i], other], item_mine, item_other, dense, acc, i == order[-1], half_rows
        )
        acc = accs[0]
        latest = stats[i][0]
    own, own_other = stats[0]

    came = [sibling(accs[1])]
    for p in range(1, n_user):
        sent = merge_items(p, acc, sibling(accs[1 + p]))
        came.append(along_user(sent, p, n_user))
    new_beta_shape = finish_items(item_exp, acc, came)

    moving = []
    for d in reversed(ahead):
        stat = stats[2 * d][0]
        parts = add_came(stat, moving[0], False) if moving else [stat]
        moving = [along_item(x, 1, n_item) for x in parts]
    came_ahead = moving
    moving = []
    for d in reversed(behind):
        stat = stats[2 * d - 1][0]
        if d == 1 and n_user > 1:
            stat = after(stat, sent)
        parts = add_came(stat, moving[0], d == 1) if moving else [stat]
        moving = [along_item(x, -1, n_item) for x in parts]
    other_behind, mine_behind = moving

    other_sum = own_other
    for x in came_ahead:
        other_sum = lax.optimization_barrier(other_sum + x[half_rows:rows].astype(F32))
    other_sum = other_sum.astype(BF16)
    other_sum = sibling(other_sum)
    other_last = after(sibling(other_behind), new_beta_shape)
    new_theta_rate, new_beta_rate = finish_rates(
        item_mine, [*came_ahead, other_behind], user_activity, item_popularity
    )
    mine_behind = after(mine_behind, new_theta_rate)
    new_theta_shape = finish_users(both, own, other_sum, other_last, mine_behind, came_ahead)
    return (new_theta_shape[None], new_theta_rate[None], new_beta_shape[None], new_beta_rate[None])


def solution(mesh):
    in_specs = (
        P(("parts", "item"), "user", None, None, None),
        P(("parts", "item"), "user", None),
        P(("parts", "item"), "user", None),
        P(("parts", "item"), "user"),
        P(("parts", "user"), "item", "ka"),
        P(("parts", "user"), "item", "ka"),
        P(("parts", "user"), "item"),
        P(("parts", "item"), "user", "ka"),
        P(("parts", "item"), "user", "ka"),
        P(("parts", "item"), "user"),
    )
    out_specs = (
        P(("parts", "user"), "item", "ka"),
        P(("parts", "user"), "item", "ka"),
        P(("parts", "item"), "user", "ka"),
        P(("parts", "item"), "user", "ka"),
    )
    run = functools.partial(body, mesh.shape["item"], mesh.shape["user"], mesh.shape["ka"])
    return jax.shard_map(run, mesh=mesh, in_specs=in_specs, out_specs=out_specs, check_vma=False)
```

```python
import functools

import jax
import jax.numpy as jnp
from jax import lax
from jax.experimental import pallas as pl
from jax.experimental.pallas import tpu as pltpu
from jax.sharding import PartitionSpec as P

BF16 = jnp.bfloat16
F32 = jnp.float32
VMEM = pltpu.MemorySpace.VMEM
SMEM = pltpu.MemorySpace.SMEM
HBM = pltpu.MemorySpace.HBM
EXTRA = 16
MIB = 1024 * 1024
CHEAP = pl.CostEstimate(flops=1024, transcendentals=0, bytes_accessed=1024)
DIMS_NT = (((1,), (1,)), ((), ()))
DIMS_TN = (((0,), (0,)), ((), ()))


def pinned(x):
    return pltpu.with_memory_space_constraint(x, HBM)


def reciprocal(x):
    r = pl.reciprocal(x, approx=True)
    return r * (2.0 - x * r)


def exp_digamma(x, inv_rate):
    w = x * (x + 3.0)
    p = w * (w + 2.0)
    y = x + 4.0
    inv = reciprocal(y * p)
    iy = inv * p
    iy2 = iy * iy
    shift = (2.0 * x + 3.0) * (2.0 * w + 2.0) * (inv * y)
    series = iy * 0.5 + iy2 * (1.0 / 12.0 - iy2 * (1.0 / 120.0 - iy2 * (1.0 / 252.0)))
    return y * inv_rate * jnp.exp(-(series + shift))


def encode(values):
    row = lax.broadcasted_iota(jnp.int32, (EXTRA, values[0].shape[1]), 0)
    out = jnp.zeros(row.shape, F32)
    for i, rest in enumerate(values):
        for j in range(3):
            piece = rest.astype(BF16).astype(F32)
            rest = rest - piece
            out = jnp.where(row == 3 * i + j, piece, out)
    return out.astype(BF16)


def decode(block):
    block = block.astype(F32)
    return [block[3 * i : 3 * i + 1] + block[3 * i + 1 : 3 * i + 2] + block[3 * i + 2 : 3 * i + 3] for i in range(2)]


def chunk_copies(starts, chunk, refs, buffers, sems):
    copies = []
    for j, start in enumerate(starts):
        here = pl.ds(start, chunk)
        copies.append(
            [pltpu.make_async_copy(r.at[here], b.at[here], sems.at[i, j]) for i, (r, b) in enumerate(zip(refs, buffers))]
        )
    for group in copies:
        for copy in group:
            copy.start()
    return copies


def users_kernel(chunk, shape_ref, rate_ref, both_ref, wide_ref, total_ref, shape_buf, rate_buf, sems):
    core = lax.axis_index("ka")
    half = both_ref.shape[0] // 2
    steps = half // chunk
    starts = []
    for side in (core, 1 - core):
        starts += [pl.multiple_of(side * half + j * chunk, chunk) for j in range(steps)]
    copies = chunk_copies(starts, chunk, (shape_ref, rate_ref), (shape_buf, rate_buf), sems)
    total = jnp.zeros(total_ref.shape, F32)
    for j, start in enumerate(starts):
        for copy in copies[j]:
            copy.wait()
        x = shape_buf[pl.ds(start, chunk), :]
        inv_rate = reciprocal(rate_buf[pl.ds(start, chunk), :])
        value = exp_digamma(x, inv_rate).astype(BF16)
        both_ref[j * chunk : (j + 1) * chunk, :] = value
        wide_ref[j * chunk : (j + 1) * chunk, :] = value
        total += jnp.sum(x * inv_rate, axis=0, keepdims=True)
    total_ref[...] = total
    wide_ref[2 * half :, :] = jnp.zeros((wide_ref.shape[0] - 2 * half, wide_ref.shape[1]), BF16)


def expected_users(shape_arg, rate_arg):
    rows, cols = shape_arg.shape
    chunk = min(rows // 2, 128)
    return pl.pallas_call(
        functools.partial(users_kernel, chunk),
        in_specs=[pl.BlockSpec(memory_space=HBM)] * 2,
        out_specs=[pl.BlockSpec(memory_space=VMEM)] * 3,
        out_shape=[
            jax.ShapeDtypeStruct((rows, cols), BF16),
            jax.ShapeDtypeStruct((rows + 3 * EXTRA, cols), BF16),
            jax.ShapeDtypeStruct((1, cols), F32),
        ],
        scratch_shapes=[
            pltpu.VMEM((rows, cols), F32),
            pltpu.VMEM((rows, cols), F32),
            pltpu.SemaphoreType.DMA((2, rows // chunk)),
        ],
        compiler_params=pltpu.CompilerParams(vmem_limit_bytes=4 * MIB),
        cost_estimate=CHEAP,
        name="expected_users",
    )(pinned(shape_arg), pinned(rate_arg))


def items_kernel(chunk, shape_ref, rate_ref, both_ref, theta_ref, item_ref, pack_ref, shape_buf, rate_buf, sems):
    rows = shape_ref.shape[0]
    half = both_ref.shape[0] // 2
    starts = list(range(0, rows, chunk))
    copies = chunk_copies(starts, chunk, (shape_ref, rate_ref), (shape_buf, rate_buf), sems)
    pack_ref[:half, :] = both_ref[half:, :]
    total = jnp.zeros(theta_ref.shape, F32)
    for j, start in enumerate(starts):
        for copy in copies[j]:
            copy.wait()
        x = shape_buf[start : start + chunk, :]
        inv_rate = reciprocal(rate_buf[start : start + chunk, :])
        value = exp_digamma(x, inv_rate).astype(BF16)
        item_ref[start : start + chunk, :] = value
        pack_ref[half + start : half + start + chunk, :] = value
        total += jnp.sum(x * inv_rate, axis=0, keepdims=True)
    extra = encode([theta_ref[...], total])
    item_ref[rows:, :] = extra
    pack_ref[half + rows :, :] = extra


def expected_items(shape_arg, rate_arg, both, theta_local):
    rows, cols = shape_arg.shape
    chunk = min(rows, 128)
    return pl.pallas_call(
        functools.partial(items_kernel, chunk),
        in_specs=[pl.BlockSpec(memory_space=m) for m in (HBM, HBM, VMEM, VMEM)],
        out_specs=[pl.BlockSpec(memory_space=VMEM)] * 2,
        out_shape=[jax.ShapeDtypeStruct((r + EXTRA, cols), BF16) for r in (rows, both.shape[0] // 2 + rows)],
        scratch_shapes=[
            pltpu.VMEM((rows, cols), F32),
            pltpu.VMEM((rows, cols), F32),
            pltpu.SemaphoreType.DMA((2, rows // chunk)),
        ],
        compiler_params=pltpu.CompilerParams(vmem_limit_bytes=4 * MIB),
        cost_estimate=CHEAP,
        name="expected_items",
    )(pinned(shape_arg), pinned(rate_arg), both, theta_local)


def dense_kernel(n_item, shard_tiles, chunk, rows, users_in, items_in, live_ref, counts_ref, out_ref, *scratch):
    users_ref, items_ref, buf, sems, index_sems = scratch
    tile = counts_ref.shape[1]
    half = rows // 2
    piece = min(half, tile)
    n_chunks = counts_ref.shape[0] // chunk
    copies = [
        pltpu.make_async_copy(
            counts_ref.at[pl.ds(c * chunk, chunk)], buf.at[pl.ds(c * chunk, chunk)], sems.at[c]
        )
        for c in range(n_chunks)
    ]
    index_copies = [
        pltpu.make_async_copy(users_in, users_ref, index_sems.at[0]),
        pltpu.make_async_copy(items_in, items_ref, index_sems.at[1]),
    ]
    for copy in index_copies + copies:
        copy.start()
    out_ref[...] = jnp.zeros_like(out_ref)
    for copy in index_copies:
        copy.wait()
    z = lax.axis_index("item")
    x = lax.axis_index("user")
    core = lax.axis_index("ka")
    live = live_ref[0]

    def place(slot, carry):
        item = items_ref[slot]
        owner = lax.div(item, shard_tiles)
        column = (owner ^ x) * shard_tiles + lax.rem(item, shard_tiles)
        col = pl.multiple_of(column * tile, tile)
        for j in range(tile // piece):
            row = users_ref[slot] * tile + j * piece
            shard = lax.div(row, rows)
            within = lax.rem(row, rows)

            @pl.when(lax.div(within, half) == core)
            def _():
                back = lax.rem(z - shard + n_item, n_item)
                step = jnp.where(back == 0, 0, jnp.where(back * 2 <= n_item, 2 * back - 1, 2 * (n_item - back)))
                start = pl.multiple_of(step * half + lax.rem(within, half), piece)
                value = buf[slot, j * piece : (j + 1) * piece, :].astype(F32).astype(BF16)
                out_ref[pl.ds(start, piece), pl.ds(col, tile)] = value

        return carry

    for c in range(n_chunks):
        copies[c].wait()
        lax.fori_loop(c * chunk, jnp.clip(live, c * chunk, (c + 1) * chunk), place, 0)


def dense_counts(counts, users, items, live, rows, n_item, item_rows, n_user):
    slots, tile, _ = counts.shape
    chunk = 8
    out_rows = n_item * rows // 2
    return pl.pallas_call(
        functools.partial(dense_kernel, n_item, item_rows // n_user // tile, chunk, rows),
        in_specs=[pl.BlockSpec(memory_space=m) for m in (HBM, HBM, SMEM, HBM)],
        out_specs=pl.BlockSpec(memory_space=VMEM),
        out_shape=jax.ShapeDtypeStruct((out_rows, item_rows), BF16),
        scratch_shapes=[
            pltpu.SMEM(users.shape, jnp.int32),
            pltpu.SMEM(items.shape, jnp.int32),
            pltpu.VMEM((slots, tile, tile), jnp.int32),
            pltpu.SemaphoreType.DMA((slots // chunk,)),
            pltpu.SemaphoreType.DMA((2,)),
        ],
        compiler_params=pltpu.CompilerParams(vmem_limit_bytes=8 * MIB),
        cost_estimate=CHEAP,
        name="dense_counts",
    )(pinned(users), pinned(items), live, pinned(counts))


def stat_kernel(pieces, half, last, has_acc, at, *refs):
    refs = list(refs)
    take = lambda n: [refs.pop(0) for _ in range(n)]
    mine_ref, other_ref = take(2)
    mine = mine_ref[:half, :]
    other = other_ref[half : 2 * half, :] if at and not last else other_ref[:half, :]
    item_mine = take(pieces)
    item_other = take(pieces)
    (counts_ref,) = take(1)
    (acc_in,) = take(1) if has_acc else (None,)
    stat_refs = take(1 if at else 2)
    acc_refs = take(1 + pieces if last else 1)
    cols = mine.shape[1]
    total_mine = None
    total_other = None
    width = 256
    for p in range(pieces):
        rows = item_mine[p].shape[0] - EXTRA
        skip = item_other[p].shape[0] - EXTRA - rows
        for c in range(rows // width):
            left = item_mine[p][c * width : (c + 1) * width, :]
            right = item_other[p][skip + c * width : skip + (c + 1) * width, :]
            norm = lax.dot_general(mine, left, DIMS_NT, preferred_element_type=F32)
            norm += lax.dot_general(other, right, DIMS_NT, preferred_element_type=F32)
            columns = slice(p * rows + c * width, p * rows + (c + 1) * width)
            grid = counts_ref[at * half : (at + 1) * half, columns].astype(F32)
            ratio = (grid * reciprocal(norm)).astype(BF16)
            stat = jnp.dot(ratio, left, preferred_element_type=F32)
            total_mine = stat if total_mine is None else total_mine + stat
            stat = jnp.dot(ratio, right, preferred_element_type=F32)
            total_other = stat if total_other is None else total_other + stat
            for i, factors in enumerate((mine, other)):
                update = lax.dot_general(factors, ratio, DIMS_TN, preferred_element_type=F32)
                if has_acc:
                    update += acc_in[i * cols : (i + 1) * cols, columns]
                if last and i == 0:
                    acc_refs[0][:, columns] = update
                elif last:
                    acc_refs[1 + p][:, c * width : (c + 1) * width] = update.astype(BF16)
                else:
                    acc_refs[0][i * cols : (i + 1) * cols, columns] = update
    if at:
        stat_refs[0][:half, :] = total_mine.astype(BF16)
        stat_refs[0][half : 2 * half, :] = total_other.astype(BF16)
        stat_refs[0][2 * half :, :] = encode(row_totals(item_mine))
    else:
        stat_refs[0][...] = total_mine
        stat_refs[1][...] = total_other


def sum_totals(blocks):
    sums = None
    for block in blocks:
        came = decode(block)
        sums = came if sums is None else [a + b for a, b in zip(sums, came)]
    return sums


def row_totals(item_refs):
    return sum_totals([ref[-EXTRA:, :] for ref in item_refs])


def statistics(at, users, item_mine, item_other, dense, acc, last, half_rows):
    half = users[0].shape[1]
    item_rows = dense.shape[1]
    args = [*users, *item_mine, *item_other, dense]
    if acc is not None:
        args.append(acc)
    if at:
        out_shape = [jax.ShapeDtypeStruct((2 * half_rows + EXTRA, half), BF16)]
    else:
        out_shape = [jax.ShapeDtypeStruct((half_rows, half), F32)] * 2
    n_stats = len(out_shape)
    if last:
        out_shape.append(jax.ShapeDtypeStruct((half, item_rows), F32))
        out_shape += [jax.ShapeDtypeStruct((half, item_rows // len(item_mine)), BF16) for _ in item_mine]
    else:
        out_shape.append(jax.ShapeDtypeStruct((2 * half, item_rows), F32))
    spec = pl.BlockSpec(memory_space=VMEM)
    out = pl.pallas_call(
        functools.partial(stat_kernel, len(item_mine), half_rows, last, acc is not None, at),
        in_specs=[spec] * len(args),
        out_specs=[spec] * len(out_shape),
        out_shape=out_shape,
        compiler_params=pltpu.CompilerParams(vmem_limit_bytes=16 * MIB),
        cost_estimate=CHEAP,
        name="statistics_%d" % at,
    )(*args)
    return list(out[:n_stats]), list(out[n_stats:])


def add_kernel(stat_ref, came_ref, out_ref):
    rows = stat_ref.shape[0] - EXTRA
    out_ref[:rows, :] = (stat_ref[:rows, :].astype(F32) + came_ref[:rows, :].astype(F32)).astype(BF16)
    out_ref[rows:, :] = encode(sum_totals([stat_ref[rows:, :], came_ref[rows:, :]]))


def split_kernel(stat_ref, came_ref, other_ref, mine_ref):
    half = other_ref.shape[0] - EXTRA
    total = stat_ref[: 2 * half, :].astype(F32) + came_ref[: 2 * half, :].astype(F32)
    other_ref[:half, :] = total[half:, :].astype(BF16)
    other_ref[half:, :] = encode(sum_totals([stat_ref[2 * half :, :], came_ref[2 * half :, :]]))
    mine_ref[:half, :] = total[:half, :].astype(BF16)
    mine_ref[half:, :] = jnp.zeros((2 * EXTRA, mine_ref.shape[1]), BF16)


def add_came(stat, came, split):
    rows, cols = stat.shape
    half = (rows - EXTRA) // 2
    shapes = [half + EXTRA, half + 2 * EXTRA] if split else [rows]
    out = pl.pallas_call(
        split_kernel if split else add_kernel,
        in_specs=[pl.BlockSpec(memory_space=VMEM)] * 2,
        out_specs=[pl.BlockSpec(memory_space=VMEM)] * len(shapes),
        out_shape=[jax.ShapeDtypeStruct((r, cols), BF16) for r in shapes],
        compiler_params=pltpu.CompilerParams(vmem_limit_bytes=2 * MIB),
        cost_estimate=CHEAP,
        name="add_came",
    )(stat, came)
    return list(out)


def merge_items_kernel(p, mine_ref, came_ref, out_ref):
    width = out_ref.shape[1]
    out_ref[...] = (mine_ref[:, p * width : (p + 1) * width] + came_ref[...].astype(F32)).astype(BF16)


def merge_items(p, mine, came):
    return pl.pallas_call(
        functools.partial(merge_items_kernel, p),
        in_specs=[pl.BlockSpec(memory_space=VMEM)] * 2,
        out_specs=pl.BlockSpec(memory_space=VMEM),
        out_shape=jax.ShapeDtypeStruct(came.shape, BF16),
        compiler_params=pltpu.CompilerParams(vmem_limit_bytes=2 * MIB),
        cost_estimate=CHEAP,
        name="merge_items",
    )(mine, came)


def finish_rates_kernel(pieces, n_came, *refs):
    refs = list(refs)
    take = lambda n: [refs.pop(0) for _ in range(n)]
    item_refs = take(pieces)
    came = take(n_came)
    columns = take(2)
    outs = take(2)
    bufs = take(2)
    (sems,) = take(1)
    theta_total, beta_total = sum_totals([ref[-EXTRA:, :] for ref in item_refs + came])
    copies = []
    for i, total in enumerate((beta_total, theta_total)):
        rows = columns[i].shape[1]
        column = jnp.broadcast_to(columns[i][...], (total.shape[1], rows)).T
        bufs[i][...] = column + total
        copies.append(pltpu.make_async_copy(bufs[i], outs[i], sems.at[i]))
        copies[-1].start()
    for copy in copies:
        copy.wait()


def finish_rates(items, came, activity, popularity):
    args = [*items, *came, activity, popularity]
    out_shape = [jax.ShapeDtypeStruct((c.shape[1], items[0].shape[1]), F32) for c in (activity, popularity)]
    return pl.pallas_call(
        functools.partial(finish_rates_kernel, len(items), len(came)),
        in_specs=[pl.BlockSpec(memory_space=VMEM)] * len(args),
        out_specs=[pl.BlockSpec(memory_space=HBM)] * 2,
        out_shape=out_shape,
        scratch_shapes=[pltpu.VMEM(o.shape, F32) for o in out_shape] + [pltpu.SemaphoreType.DMA((2,))],
        compiler_params=pltpu.CompilerParams(vmem_limit_bytes=6 * MIB),
        cost_estimate=CHEAP,
        name="finish_rates",
    )(*args)


def finish_users_kernel(n_ahead, *refs):
    refs = list(refs)
    take = lambda n: [refs.pop(0) for _ in range(n)]
    both_ref, own_ref, other_ref, last_ref, mine_ref = take(5)
    ahead = take(n_ahead)
    out_ref, buf, sems = take(3)
    core = lax.axis_index("ka")
    half = own_ref.shape[0]

    def send(i, side, rows, total):
        here = pl.ds(pl.multiple_of(side * half, half), half)
        buf[here, :] = 0.3 + both_ref[rows, :].astype(F32) * total
        copy = pltpu.make_async_copy(buf.at[here], out_ref.at[here], sems.at[i])
        copy.start()
        return copy

    total = own_ref[...] + mine_ref[:half, :].astype(F32)
    for ref in ahead:
        total += ref[:half, :].astype(F32)
    other = other_ref[...].astype(F32) + last_ref[:half, :].astype(F32)
    copies = [send(0, core, slice(0, half), total), send(1, 1 - core, slice(half, 2 * half), other)]
    for copy in copies:
        copy.wait()


def finish_users(both, own, other_sum, other_last, mine, ahead):
    rows, half = both.shape
    args = [both, own, other_sum, other_last, mine, *ahead]
    return pl.pallas_call(
        functools.partial(finish_users_kernel, len(ahead)),
        in_specs=[pl.BlockSpec(memory_space=VMEM)] * len(args),
        out_specs=pl.BlockSpec(memory_space=HBM),
        out_shape=jax.ShapeDtypeStruct((rows, half), F32),
        scratch_shapes=[pltpu.VMEM((rows, half), F32), pltpu.SemaphoreType.DMA((2,))],
        compiler_params=pltpu.CompilerParams(vmem_limit_bytes=4 * MIB),
        cost_estimate=CHEAP,
        name="finish_users",
    )(*args)


def finish_items_kernel(n, exp_ref, own_ref, *refs):
    out_ref, buf, sems = refs[n:]
    rows = out_ref.shape[0]
    chunk = min(rows, 256)
    copies = []
    for j in range(rows // chunk):
        part = slice(j * chunk, (j + 1) * chunk)
        total = own_ref[:, part]
        for p in range(n):
            total += refs[p][:, part].astype(F32)
        buf[part, :] = 0.3 + exp_ref[part, :].astype(F32) * total.T
        here = pl.ds(j * chunk, chunk)
        copies.append(pltpu.make_async_copy(buf.at[here], out_ref.at[here], sems.at[j]))
        copies[-1].start()
    for copy in copies:
        copy.wait()


def finish_items(item_exp, own, came):
    half, rows = came[0].shape
    return pl.pallas_call(
        functools.partial(finish_items_kernel, len(came)),
        in_specs=[pl.BlockSpec(memory_space=VMEM)] * (2 + len(came)),
        out_specs=pl.BlockSpec(memory_space=HBM),
        out_shape=jax.ShapeDtypeStruct((rows, half), F32),
        scratch_shapes=[pltpu.VMEM((rows, half), F32), pltpu.SemaphoreType.DMA((rows // min(rows, 256),))],
        compiler_params=pltpu.CompilerParams(vmem_limit_bytes=6 * MIB),
        cost_estimate=CHEAP,
        name="finish_items",
    )(item_exp, own, *came)


def along_item(x, shift, n):
    return lax.ppermute(x, "item", [(i, (i + shift) % n) for i in range(n)])


def after(x, y):
    return lax.optimization_barrier((x, y))[0]


def along_user(x, distance, n):
    return lax.ppermute(x, "user", [(i, i ^ distance) for i in range(n)])


def body(
    n_item,
    n_user,
    n_ka,
    counts,
    tile_user,
    tile_item,
    tile_live,
    theta_shape,
    theta_rate,
    user_activity,
    beta_shape,
    beta_rate,
    item_popularity,
):
    def sibling(x):
        return lax.ppermute(x, "ka", [(h, n_ka - 1 - h) for h in range(n_ka)])

    both, wide, theta_local = expected_users(theta_shape[0], theta_rate[0])
    item_exp, pack = expected_items(beta_shape[0], beta_rate[0], both, theta_local)
    rows = both.shape[0]
    half_rows = rows // 2
    item_rows = beta_shape.shape[1] * n_user
    dense = dense_counts(
        counts[0, 0],
        tile_user[0, 0],
        tile_item[0, 0],
        tile_live[0],
        rows,
        n_item,
        item_rows,
        n_user,
    )
    came_pack = sibling(pack)

    ahead = range(1, n_item // 2)
    behind = range(1, n_item // 2 + 1)
    shards = {0: both}
    for d in behind:
        shards[2 * d - 1] = along_item(shards[max(2 * d - 3, 0)], 1, n_item)
    for d in ahead:
        shards[2 * d] = along_item(after(wide, shards[1]) if d == 1 else shards[2 * d - 2], -1, n_item)

    item_mine = [item_exp]
    for p in range(1, n_user):
        low = p & -p
        item_mine.append(along_user(after(item_mine[p ^ low], dense), low, n_user))
    item_other = [came_pack] + [sibling(x) for x in item_mine[1:]]

    order = [2 * d - 1 for d in behind] + [2 * d for d in ahead]
    order.insert(len(order) - 1, 0)
    acc = None
    stats = {}
    latest = None
    for i in order:
        passed = after(shards[i], stats[n_item - 1][0])[half_rows:rows] if i == order[-1] else shards[i]
        other = sibling(passed) if i else came_pack
        stats[i], accs = statistics(
            i, [shards[i], other], item_mine, item_other, dense, acc, i == order[-1], half_rows
        )
        acc = accs[0]
        latest = stats[i][0]
    own, own_other = stats[0]

    came = [sibling(accs[1])]
    for p in range(1, n_user):
        sent = merge_items(p, acc, sibling(accs[1 + p]))
        came.append(along_user(sent, p, n_user))
    new_beta_shape = finish_items(item_exp, acc, came)

    moving = []
    for d in reversed(ahead):
        stat = stats[2 * d][0]
        parts = add_came(stat, moving[0], False) if moving else [stat]
        moving = [along_item(x, 1, n_item) for x in parts]
    came_ahead = moving
    moving = []
    for d in reversed(behind):
        stat = stats[2 * d - 1][0]
        if d == 1 and n_user > 1:
            stat = after(stat, sent)
        parts = add_came(stat, moving[0], d == 1) if moving else [stat]
        moving = [along_item(x, -1, n_item) for x in parts]
    other_behind, mine_behind = moving

    other_sum = own_other
    for x in came_ahead:
        other_sum = lax.optimization_barrier(other_sum + x[half_rows:rows].astype(F32))
    other_sum = other_sum.astype(BF16)
    other_sum = sibling(other_sum)
    other_last = after(sibling(other_behind), new_beta_shape)
    new_theta_rate, new_beta_rate = finish_rates(
        item_mine, [*came_ahead, other_behind], user_activity, item_popularity
    )
    other_last = after(other_last, new_theta_rate)
    new_theta_shape = finish_users(both, own, other_sum, other_last, mine_behind, came_ahead)
    return (new_theta_shape[None], new_theta_rate[None], new_beta_shape[None], new_beta_rate[None])


def solution(mesh):
    in_specs = (
        P(("parts", "item"), "user", None, None, None),
        P(("parts", "item"), "user", None),
        P(("parts", "item"), "user", None),
        P(("parts", "item"), "user"),
        P(("parts", "user"), "item", "ka"),
        P(("parts", "user"), "item", "ka"),
        P(("parts", "user"), "item"),
        P(("parts", "item"), "user", "ka"),
        P(("parts", "item"), "user", "ka"),
        P(("parts", "item"), "user"),
    )
    out_specs = (
        P(("parts", "user"), "item", "ka"),
        P(("parts", "user"), "item", "ka"),
        P(("parts", "item"), "user", "ka"),
        P(("parts", "item"), "user", "ka"),
    )
    run = functools.partial(body, mesh.shape["item"], mesh.shape["user"], mesh.shape["ka"])
    return jax.shard_map(run, mesh=mesh, in_specs=in_specs, out_specs=out_specs, check_vma=False)
```

```python
import functools

import jax
import jax.numpy as jnp
from jax import lax
from jax.experimental import pallas as pl
from jax.experimental.pallas import tpu as pltpu
from jax.sharding import PartitionSpec as P

BF16 = jnp.bfloat16
F32 = jnp.float32
VMEM = pltpu.MemorySpace.VMEM
SMEM = pltpu.MemorySpace.SMEM
HBM = pltpu.MemorySpace.HBM
EXTRA = 16
MIB = 1024 * 1024
CHEAP = pl.CostEstimate(flops=1024, transcendentals=0, bytes_accessed=1024)
DIMS_NT = (((1,), (1,)), ((), ()))
DIMS_TN = (((0,), (0,)), ((), ()))


def pinned(x):
    return pltpu.with_memory_space_constraint(x, HBM)


def reciprocal(x):
    r = pl.reciprocal(x, approx=True)
    return r * (2.0 - x * r)


def exp_digamma(x, inv_rate):
    w = x * (x + 3.0)
    p = w * (w + 2.0)
    y = x + 4.0
    inv = reciprocal(y * p)
    iy = inv * p
    iy2 = iy * iy
    shift = (2.0 * x + 3.0) * (2.0 * w + 2.0) * (inv * y)
    series = iy * 0.5 + iy2 * (1.0 / 12.0 - iy2 * (1.0 / 120.0 - iy2 * (1.0 / 252.0)))
    return y * inv_rate * jnp.exp(-(series + shift))


def encode(values):
    row = lax.broadcasted_iota(jnp.int32, (EXTRA, values[0].shape[1]), 0)
    out = jnp.zeros(row.shape, F32)
    for i, rest in enumerate(values):
        for j in range(3):
            piece = rest.astype(BF16).astype(F32)
            rest = rest - piece
            out = jnp.where(row == 3 * i + j, piece, out)
    return out.astype(BF16)


def decode(block):
    block = block.astype(F32)
    return [block[3 * i : 3 * i + 1] + block[3 * i + 1 : 3 * i + 2] + block[3 * i + 2 : 3 * i + 3] for i in range(2)]


def chunk_copies(starts, chunk, refs, buffers, sems):
    copies = []
    for j, start in enumerate(starts):
        here = pl.ds(start, chunk)
        copies.append(
            [pltpu.make_async_copy(r.at[here], b.at[here], sems.at[i, j]) for i, (r, b) in enumerate(zip(refs, buffers))]
        )
    for group in copies:
        for copy in group:
            copy.start()
    return copies


def users_kernel(chunk, shape_ref, rate_ref, both_ref, wide_ref, total_ref, shape_buf, rate_buf, sems):
    core = lax.axis_index("ka")
    half = both_ref.shape[0] // 2
    steps = half // chunk
    starts = []
    for side in (core, 1 - core):
        starts += [pl.multiple_of(side * half + j * chunk, chunk) for j in range(steps)]
    copies = chunk_copies(starts, chunk, (shape_ref, rate_ref), (shape_buf, rate_buf), sems)
    total = jnp.zeros(total_ref.shape, F32)
    for j, start in enumerate(starts):
        for copy in copies[j]:
            copy.wait()
        x = shape_buf[pl.ds(start, chunk), :]
        inv_rate = reciprocal(rate_buf[pl.ds(start, chunk), :])
        value = exp_digamma(x, inv_rate).astype(BF16)
        both_ref[j * chunk : (j + 1) * chunk, :] = value
        wide_ref[j * chunk : (j + 1) * chunk, :] = value
        total += jnp.sum(x * inv_rate, axis=0, keepdims=True)
    total_ref[...] = total
    wide_ref[2 * half :, :] = jnp.zeros((wide_ref.shape[0] - 2 * half, wide_ref.shape[1]), BF16)


def expected_users(shape_arg, rate_arg):
    rows, cols = shape_arg.shape
    chunk = min(rows // 2, 128)
    return pl.pallas_call(
        functools.partial(users_kernel, chunk),
        in_specs=[pl.BlockSpec(memory_space=HBM)] * 2,
        out_specs=[pl.BlockSpec(memory_space=VMEM)] * 3,
        out_shape=[
            jax.ShapeDtypeStruct((rows, cols), BF16),
            jax.ShapeDtypeStruct((rows + 1 * EXTRA, cols), BF16),
            jax.ShapeDtypeStruct((1, cols), F32),
        ],
        scratch_shapes=[
            pltpu.VMEM((rows, cols), F32),
            pltpu.VMEM((rows, cols), F32),
            pltpu.SemaphoreType.DMA((2, rows // chunk)),
        ],
        compiler_params=pltpu.CompilerParams(vmem_limit_bytes=4 * MIB),
        cost_estimate=CHEAP,
        name="expected_users",
    )(pinned(shape_arg), pinned(rate_arg))


def items_kernel(chunk, shape_ref, rate_ref, both_ref, theta_ref, item_ref, pack_ref, shape_buf, rate_buf, sems):
    rows = shape_ref.shape[0]
    half = both_ref.shape[0] // 2
    starts = list(range(0, rows, chunk))
    copies = chunk_copies(starts, chunk, (shape_ref, rate_ref), (shape_buf, rate_buf), sems)
    pack_ref[:half, :] = both_ref[half:, :]
    total = jnp.zeros(theta_ref.shape, F32)
    for j, start in enumerate(starts):
        for copy in copies[j]:
            copy.wait()
        x = shape_buf[start : start + chunk, :]
        inv_rate = reciprocal(rate_buf[start : start + chunk, :])
        value = exp_digamma(x, inv_rate).astype(BF16)
        item_ref[start : start + chunk, :] = value
        pack_ref[half + start : half + start + chunk, :] = value
        total += jnp.sum(x * inv_rate, axis=0, keepdims=True)
    extra = encode([theta_ref[...], total])
    item_ref[rows:, :] = extra
    pack_ref[half + rows :, :] = extra


def expected_items(shape_arg, rate_arg, both, theta_local):
    rows, cols = shape_arg.shape
    chunk = min(rows, 128)
    return pl.pallas_call(
        functools.partial(items_kernel, chunk),
        in_specs=[pl.BlockSpec(memory_space=m) for m in (HBM, HBM, VMEM, VMEM)],
        out_specs=[pl.BlockSpec(memory_space=VMEM)] * 2,
        out_shape=[jax.ShapeDtypeStruct((r + EXTRA, cols), BF16) for r in (rows, both.shape[0] // 2 + rows)],
        scratch_shapes=[
            pltpu.VMEM((rows, cols), F32),
            pltpu.VMEM((rows, cols), F32),
            pltpu.SemaphoreType.DMA((2, rows // chunk)),
        ],
        compiler_params=pltpu.CompilerParams(vmem_limit_bytes=4 * MIB),
        cost_estimate=CHEAP,
        name="expected_items",
    )(pinned(shape_arg), pinned(rate_arg), both, theta_local)


def dense_kernel(n_item, shard_tiles, chunk, rows, users_in, items_in, live_ref, counts_ref, out_ref, *scratch):
    users_ref, items_ref, buf, sems, index_sems = scratch
    tile = counts_ref.shape[1]
    half = rows // 2
    piece = min(half, tile)
    n_chunks = counts_ref.shape[0] // chunk
    copies = [
        pltpu.make_async_copy(
            counts_ref.at[pl.ds(c * chunk, chunk)], buf.at[pl.ds(c * chunk, chunk)], sems.at[c]
        )
        for c in range(n_chunks)
    ]
    index_copies = [
        pltpu.make_async_copy(users_in, users_ref, index_sems.at[0]),
        pltpu.make_async_copy(items_in, items_ref, index_sems.at[1]),
    ]
    for copy in index_copies + copies:
        copy.start()
    out_ref[...] = jnp.zeros_like(out_ref)
    for copy in index_copies:
        copy.wait()
    z = lax.axis_index("item")
    x = lax.axis_index("user")
    core = lax.axis_index("ka")
    live = live_ref[0]

    def place(slot, carry):
        item = items_ref[slot]
        owner = lax.div(item, shard_tiles)
        column = (owner ^ x) * shard_tiles + lax.rem(item, shard_tiles)
        col = pl.multiple_of(column * tile, tile)
        for j in range(tile // piece):
            row = users_ref[slot] * tile + j * piece
            shard = lax.div(row, rows)
            within = lax.rem(row, rows)

            @pl.when(lax.div(within, half) == core)
            def _():
                back = lax.rem(z - shard + n_item, n_item)
                step = jnp.where(back == 0, 0, jnp.where(back * 2 <= n_item, 2 * back - 1, 2 * (n_item - back)))
                start = pl.multiple_of(step * half + lax.rem(within, half), piece)
                value = buf[slot, j * piece : (j + 1) * piece, :].astype(F32).astype(BF16)
                out_ref[pl.ds(start, piece), pl.ds(col, tile)] = value

        return carry

    for c in range(n_chunks):
        copies[c].wait()
        lax.fori_loop(c * chunk, jnp.clip(live, c * chunk, (c + 1) * chunk), place, 0)


def dense_counts(counts, users, items, live, rows, n_item, item_rows, n_user):
    slots, tile, _ = counts.shape
    chunk = 8
    out_rows = n_item * rows // 2
    return pl.pallas_call(
        functools.partial(dense_kernel, n_item, item_rows // n_user // tile, chunk, rows),
        in_specs=[pl.BlockSpec(memory_space=m) for m in (HBM, HBM, SMEM, HBM)],
        out_specs=pl.BlockSpec(memory_space=VMEM),
        out_shape=jax.ShapeDtypeStruct((out_rows, item_rows), BF16),
        scratch_shapes=[
            pltpu.SMEM(users.shape, jnp.int32),
            pltpu.SMEM(items.shape, jnp.int32),
            pltpu.VMEM((slots, tile, tile), jnp.int32),
            pltpu.SemaphoreType.DMA((slots // chunk,)),
            pltpu.SemaphoreType.DMA((2,)),
        ],
        compiler_params=pltpu.CompilerParams(vmem_limit_bytes=8 * MIB),
        cost_estimate=CHEAP,
        name="dense_counts",
    )(pinned(users), pinned(items), live, pinned(counts))


def stat_kernel(pieces, half, last, has_acc, at, *refs):
    refs = list(refs)
    take = lambda n: [refs.pop(0) for _ in range(n)]
    mine_ref, other_ref = take(2)
    mine = mine_ref[:half, :]
    other = other_ref[half : 2 * half, :] if at and not last else other_ref[:half, :]
    item_mine = take(pieces)
    item_other = take(pieces)
    (counts_ref,) = take(1)
    (acc_in,) = take(1) if has_acc else (None,)
    stat_refs = take(1 if at else 2)
    acc_refs = take(1 + pieces if last else 1)
    cols = mine.shape[1]
    total_mine = None
    total_other = None
    width = 256
    for p in range(pieces):
        rows = item_mine[p].shape[0] - EXTRA
        skip = item_other[p].shape[0] - EXTRA - rows
        for c in range(rows // width):
            left = item_mine[p][c * width : (c + 1) * width, :]
            right = item_other[p][skip + c * width : skip + (c + 1) * width, :]
            norm = lax.dot_general(mine, left, DIMS_NT, preferred_element_type=F32)
            norm += lax.dot_general(other, right, DIMS_NT, preferred_element_type=F32)
            columns = slice(p * rows + c * width, p * rows + (c + 1) * width)
            grid = counts_ref[at * half : (at + 1) * half, columns].astype(F32)
            ratio = (grid * reciprocal(norm)).astype(BF16)
            stat = jnp.dot(ratio, left, preferred_element_type=F32)
            total_mine = stat if total_mine is None else total_mine + stat
            stat = jnp.dot(ratio, right, preferred_element_type=F32)
            total_other = stat if total_other is None else total_other + stat
            for i, factors in enumerate((mine, other)):
                update = lax.dot_general(factors, ratio, DIMS_TN, preferred_element_type=F32)
                if has_acc:
                    update += acc_in[i * cols : (i + 1) * cols, columns]
                if last and i == 0:
                    acc_refs[0][:, columns] = update
                elif last:
                    acc_refs[1 + p][:, c * width : (c + 1) * width] = update.astype(BF16)
                else:
                    acc_refs[0][i * cols : (i + 1) * cols, columns] = update
    if at:
        stat_refs[0][:half, :] = total_mine.astype(BF16)
        stat_refs[0][half : 2 * half, :] = total_other.astype(BF16)
        stat_refs[0][2 * half :, :] = encode(row_totals(item_mine))
    else:
        stat_refs[0][...] = total_mine
        stat_refs[1][...] = total_other


def sum_totals(blocks):
    sums = None
    for block in blocks:
        came = decode(block)
        sums = came if sums is None else [a + b for a, b in zip(sums, came)]
    return sums


def row_totals(item_refs):
    return sum_totals([ref[-EXTRA:, :] for ref in item_refs])


def statistics(at, users, item_mine, item_other, dense, acc, last, half_rows):
    half = users[0].shape[1]
    item_rows = dense.shape[1]
    args = [*users, *item_mine, *item_other, dense]
    if acc is not None:
        args.append(acc)
    if at:
        out_shape = [jax.ShapeDtypeStruct((2 * half_rows + EXTRA, half), BF16)]
    else:
        out_shape = [jax.ShapeDtypeStruct((half_rows, half), F32)] * 2
    n_stats = len(out_shape)
    if last:
        out_shape.append(jax.ShapeDtypeStruct((half, item_rows), F32))
        out_shape += [jax.ShapeDtypeStruct((half, item_rows // len(item_mine)), BF16) for _ in item_mine]
    else:
        out_shape.append(jax.ShapeDtypeStruct((2 * half, item_rows), F32))
    spec = pl.BlockSpec(memory_space=VMEM)
    out = pl.pallas_call(
        functools.partial(stat_kernel, len(item_mine), half_rows, last, acc is not None, at),
        in_specs=[spec] * len(args),
        out_specs=[spec] * len(out_shape),
        out_shape=out_shape,
        compiler_params=pltpu.CompilerParams(vmem_limit_bytes=16 * MIB),
        cost_estimate=CHEAP,
        name="statistics_%d" % at,
    )(*args)
    return list(out[:n_stats]), list(out[n_stats:])


def add_kernel(stat_ref, came_ref, out_ref):
    rows = stat_ref.shape[0] - EXTRA
    out_ref[:rows, :] = (stat_ref[:rows, :].astype(F32) + came_ref[:rows, :].astype(F32)).astype(BF16)
    out_ref[rows:, :] = encode(sum_totals([stat_ref[rows:, :], came_ref[rows:, :]]))


def split_kernel(stat_ref, came_ref, other_ref, mine_ref):
    half = other_ref.shape[0] - EXTRA
    total = stat_ref[: 2 * half, :].astype(F32) + came_ref[: 2 * half, :].astype(F32)
    other_ref[:half, :] = total[half:, :].astype(BF16)
    other_ref[half:, :] = encode(sum_totals([stat_ref[2 * half :, :], came_ref[2 * half :, :]]))
    mine_ref[:half, :] = total[:half, :].astype(BF16)
    mine_ref[half:, :] = jnp.zeros((2 * EXTRA, mine_ref.shape[1]), BF16)


def add_came(stat, came, split):
    rows, cols = stat.shape
    half = (rows - EXTRA) // 2
    shapes = [half + EXTRA, half + 2 * EXTRA] if split else [rows]
    out = pl.pallas_call(
        split_kernel if split else add_kernel,
        in_specs=[pl.BlockSpec(memory_space=VMEM)] * 2,
        out_specs=[pl.BlockSpec(memory_space=VMEM)] * len(shapes),
        out_shape=[jax.ShapeDtypeStruct((r, cols), BF16) for r in shapes],
        compiler_params=pltpu.CompilerParams(vmem_limit_bytes=2 * MIB),
        cost_estimate=CHEAP,
        name="add_came",
    )(stat, came)
    return list(out)


def merge_items_kernel(p, mine_ref, came_ref, out_ref):
    width = out_ref.shape[1]
    out_ref[...] = (mine_ref[:, p * width : (p + 1) * width] + came_ref[...].astype(F32)).astype(BF16)


def merge_items(p, mine, came):
    return pl.pallas_call(
        functools.partial(merge_items_kernel, p),
        in_specs=[pl.BlockSpec(memory_space=VMEM)] * 2,
        out_specs=pl.BlockSpec(memory_space=VMEM),
        out_shape=jax.ShapeDtypeStruct(came.shape, BF16),
        compiler_params=pltpu.CompilerParams(vmem_limit_bytes=2 * MIB),
        cost_estimate=CHEAP,
        name="merge_items",
    )(mine, came)


def finish_rates_kernel(pieces, n_came, *refs):
    refs = list(refs)
    take = lambda n: [refs.pop(0) for _ in range(n)]
    item_refs = take(pieces)
    came = take(n_came)
    columns = take(2)
    outs = take(2)
    bufs = take(2)
    (sems,) = take(1)
    theta_total, beta_total = sum_totals([ref[-EXTRA:, :] for ref in item_refs + came])
    copies = []
    for i, total in enumerate((beta_total, theta_total)):
        rows = columns[i].shape[1]
        column = jnp.broadcast_to(columns[i][...], (total.shape[1], rows)).T
        bufs[i][...] = column + total
        copies.append(pltpu.make_async_copy(bufs[i], outs[i], sems.at[i]))
        copies[-1].start()
    for copy in copies:
        copy.wait()


def finish_rates(items, came, activity, popularity):
    args = [*items, *came, activity, popularity]
    out_shape = [jax.ShapeDtypeStruct((c.shape[1], items[0].shape[1]), F32) for c in (activity, popularity)]
    return pl.pallas_call(
        functools.partial(finish_rates_kernel, len(items), len(came)),
        in_specs=[pl.BlockSpec(memory_space=VMEM)] * len(args),
        out_specs=[pl.BlockSpec(memory_space=HBM)] * 2,
        out_shape=out_shape,
        scratch_shapes=[pltpu.VMEM(o.shape, F32) for o in out_shape] + [pltpu.SemaphoreType.DMA((2,))],
        compiler_params=pltpu.CompilerParams(vmem_limit_bytes=6 * MIB),
        cost_estimate=CHEAP,
        name="finish_rates",
    )(*args)


def finish_users_kernel(n_ahead, *refs):
    refs = list(refs)
    take = lambda n: [refs.pop(0) for _ in range(n)]
    both_ref, own_ref, other_ref, last_ref, mine_ref = take(5)
    ahead = take(n_ahead)
    out_ref, buf, sems = take(3)
    core = lax.axis_index("ka")
    half = own_ref.shape[0]

    def send(i, side, rows, total):
        here = pl.ds(pl.multiple_of(side * half, half), half)
        buf[here, :] = 0.3 + both_ref[rows, :].astype(F32) * total
        copy = pltpu.make_async_copy(buf.at[here], out_ref.at[here], sems.at[i])
        copy.start()
        return copy

    total = own_ref[...] + mine_ref[:half, :].astype(F32)
    for ref in ahead:
        total += ref[:half, :].astype(F32)
    other = other_ref[...].astype(F32) + last_ref[:half, :].astype(F32)
    copies = [send(0, core, slice(0, half), total), send(1, 1 - core, slice(half, 2 * half), other)]
    for copy in copies:
        copy.wait()


def finish_users(both, own, other_sum, other_last, mine, ahead):
    rows, half = both.shape
    args = [both, own, other_sum, other_last, mine, *ahead]
    return pl.pallas_call(
        functools.partial(finish_users_kernel, len(ahead)),
        in_specs=[pl.BlockSpec(memory_space=VMEM)] * len(args),
        out_specs=pl.BlockSpec(memory_space=HBM),
        out_shape=jax.ShapeDtypeStruct((rows, half), F32),
        scratch_shapes=[pltpu.VMEM((rows, half), F32), pltpu.SemaphoreType.DMA((2,))],
        compiler_params=pltpu.CompilerParams(vmem_limit_bytes=4 * MIB),
        cost_estimate=CHEAP,
        name="finish_users",
    )(*args)


def finish_items_kernel(n, exp_ref, own_ref, *refs):
    out_ref, buf, sems = refs[n:]
    rows = out_ref.shape[0]
    chunk = min(rows, 256)
    copies = []
    for j in range(rows // chunk):
        part = slice(j * chunk, (j + 1) * chunk)
        total = own_ref[:, part]
        for p in range(n):
            total += refs[p][:, part].astype(F32)
        buf[part, :] = 0.3 + exp_ref[part, :].astype(F32) * total.T
        here = pl.ds(j * chunk, chunk)
        copies.append(pltpu.make_async_copy(buf.at[here], out_ref.at[here], sems.at[j]))
        copies[-1].start()
    for copy in copies:
        copy.wait()


def finish_items(item_exp, own, came):
    half, rows = came[0].shape
    return pl.pallas_call(
        functools.partial(finish_items_kernel, len(came)),
        in_specs=[pl.BlockSpec(memory_space=VMEM)] * (2 + len(came)),
        out_specs=pl.BlockSpec(memory_space=HBM),
        out_shape=jax.ShapeDtypeStruct((rows, half), F32),
        scratch_shapes=[pltpu.VMEM((rows, half), F32), pltpu.SemaphoreType.DMA((rows // min(rows, 256),))],
        compiler_params=pltpu.CompilerParams(vmem_limit_bytes=6 * MIB),
        cost_estimate=CHEAP,
        name="finish_items",
    )(item_exp, own, *came)


def along_item(x, shift, n):
    return lax.ppermute(x, "item", [(i, (i + shift) % n) for i in range(n)])


def after(x, y):
    return lax.optimization_barrier((x, y))[0]


def along_user(x, distance, n):
    return lax.ppermute(x, "user", [(i, i ^ distance) for i in range(n)])


def body(
    n_item,
    n_user,
    n_ka,
    counts,
    tile_user,
    tile_item,
    tile_live,
    theta_shape,
    theta_rate,
    user_activity,
    beta_shape,
    beta_rate,
    item_popularity,
):
    def sibling(x):
        return lax.ppermute(x, "ka", [(h, n_ka - 1 - h) for h in range(n_ka)])

    both, wide, theta_local = expected_users(theta_shape[0], theta_rate[0])
    item_exp, pack = expected_items(beta_shape[0], beta_rate[0], both, theta_local)
    rows = both.shape[0]
    half_rows = rows // 2
    item_rows = beta_shape.shape[1] * n_user
    dense = dense_counts(
        counts[0, 0],
        tile_user[0, 0],
        tile_item[0, 0],
        tile_live[0],
        rows,
        n_item,
        item_rows,
        n_user,
    )
    came_pack = sibling(pack)

    ahead = range(1, n_item // 2)
    behind = range(1, n_item // 2 + 1)
    shards = {0: both}
    for d in behind:
        shards[2 * d - 1] = along_item(shards[max(2 * d - 3, 0)], 1, n_item)
    for d in ahead:
        shards[2 * d] = along_item(after(wide, shards[1]) if d == 1 else shards[2 * d - 2], -1, n_item)

    item_mine = [item_exp]
    for p in range(1, n_user):
        low = p & -p
        item_mine.append(along_user(after(item_mine[p ^ low], dense), low, n_user))
    item_other = [came_pack] + [sibling(x) for x in item_mine[1:]]

    order = [2 * d - 1 for d in behind] + [2 * d for d in ahead]
    order.insert(len(order) - 1, 0)
    acc = None
    stats = {}
    latest = None
    for i in order:
        passed = after(shards[i], stats[n_item - 1][0])[half_rows:rows] if i == order[-1] else shards[i]
        other = sibling(passed) if i else came_pack
        stats[i], accs = statistics(
            i, [shards[i], other], item_mine, item_other, dense, acc, i == order[-1], half_rows
        )
        acc = accs[0]
        latest = stats[i][0]
    own, own_other = stats[0]

    came = [sibling(accs[1])]
    for p in range(1, n_user):
        sent = merge_items(p, acc, sibling(accs[1 + p]))
        came.append(along_user(sent, p, n_user))
    new_beta_shape = finish_items(item_exp, acc, came)

    moving = []
    for d in reversed(ahead):
        stat = stats[2 * d][0]
        parts = add_came(stat, moving[0], False) if moving else [stat]
        moving = [along_item(x, 1, n_item) for x in parts]
    came_ahead = moving
    moving = []
    for d in reversed(behind):
        stat = stats[2 * d - 1][0]
        if d == 1 and n_user > 1:
            stat = after(stat, sent)
        parts = add_came(stat, moving[0], d == 1) if moving else [stat]
        moving = [along_item(x, -1, n_item) for x in parts]
    other_behind, mine_behind = moving

    other_sum = own_other
    for x in came_ahead:
        other_sum = lax.optimization_barrier(other_sum + x[half_rows:rows].astype(F32))
    other_sum = other_sum.astype(BF16)
    other_sum = sibling(other_sum)
    other_last = after(sibling(other_behind), new_beta_shape)
    new_theta_rate, new_beta_rate = finish_rates(
        item_mine, [*came_ahead, other_behind], user_activity, item_popularity
    )
    other_last = after(other_last, new_theta_rate)
    new_theta_shape = finish_users(both, own, other_sum, other_last, mine_behind, came_ahead)
    return (new_theta_shape[None], new_theta_rate[None], new_beta_shape[None], new_beta_rate[None])


def solution(mesh):
    in_specs = (
        P(("parts", "item"), "user", None, None, None),
        P(("parts", "item"), "user", None),
        P(("parts", "item"), "user", None),
        P(("parts", "item"), "user"),
        P(("parts", "user"), "item", "ka"),
        P(("parts", "user"), "item", "ka"),
        P(("parts", "user"), "item"),
        P(("parts", "item"), "user", "ka"),
        P(("parts", "item"), "user", "ka"),
        P(("parts", "item"), "user"),
    )
    out_specs = (
        P(("parts", "user"), "item", "ka"),
        P(("parts", "user"), "item", "ka"),
        P(("parts", "item"), "user", "ka"),
        P(("parts", "item"), "user", "ka"),
    )
    run = functools.partial(body, mesh.shape["item"], mesh.shape["user"], mesh.shape["ka"])
    return jax.shard_map(run, mesh=mesh, in_specs=in_specs, out_specs=out_specs, check_vma=False)
```

```python
import functools

import jax
import jax.numpy as jnp
from jax import lax
from jax.experimental import pallas as pl
from jax.experimental.pallas import tpu as pltpu
from jax.sharding import PartitionSpec as P

BF16 = jnp.bfloat16
F32 = jnp.float32
VMEM = pltpu.MemorySpace.VMEM
SMEM = pltpu.MemorySpace.SMEM
HBM = pltpu.MemorySpace.HBM
EXTRA = 16
MIB = 1024 * 1024
CHEAP = pl.CostEstimate(flops=1024, transcendentals=0, bytes_accessed=1024)
DIMS_NT = (((1,), (1,)), ((), ()))
DIMS_TN = (((0,), (0,)), ((), ()))


def pinned(x):
    return pltpu.with_memory_space_constraint(x, HBM)


def reciprocal(x):
    r = pl.reciprocal(x, approx=True)
    return r * (2.0 - x * r)


def exp_digamma(x, inv_rate):
    w = x * (x + 3.0)
    p = w * (w + 2.0)
    y = x + 4.0
    inv = reciprocal(y * p)
    iy = inv * p
    iy2 = iy * iy
    shift = (2.0 * x + 3.0) * (2.0 * w + 2.0) * (inv * y)
    series = iy * 0.5 + iy2 * (1.0 / 12.0 - iy2 * (1.0 / 120.0 - iy2 * (1.0 / 252.0)))
    return y * inv_rate * jnp.exp(-(series + shift))


def encode(values):
    row = lax.broadcasted_iota(jnp.int32, (EXTRA, values[0].shape[1]), 0)
    out = jnp.zeros(row.shape, F32)
    for i, rest in enumerate(values):
        for j in range(3):
            piece = rest.astype(BF16).astype(F32)
            rest = rest - piece
            out = jnp.where(row == 3 * i + j, piece, out)
    return out.astype(BF16)


def decode(block):
    block = block.astype(F32)
    return [block[3 * i : 3 * i + 1] + block[3 * i + 1 : 3 * i + 2] + block[3 * i + 2 : 3 * i + 3] for i in range(2)]


def chunk_copies(starts, chunk, refs, buffers, sems):
    copies = []
    for j, start in enumerate(starts):
        here = pl.ds(start, chunk)
        copies.append(
            [pltpu.make_async_copy(r.at[here], b.at[here], sems.at[i, j]) for i, (r, b) in enumerate(zip(refs, buffers))]
        )
    for group in copies:
        for copy in group:
            copy.start()
    return copies


def users_kernel(chunk, shape_ref, rate_ref, both_ref, keep_ref, give_ref, total_ref, shape_buf, rate_buf, sems):
    core = lax.axis_index("ka")
    half = both_ref.shape[0] // 2
    steps = half // chunk
    starts = []
    for side in (core, 1 - core):
        starts += [pl.multiple_of(side * half + j * chunk, chunk) for j in range(steps)]
    copies = chunk_copies(starts, chunk, (shape_ref, rate_ref), (shape_buf, rate_buf), sems)
    total = jnp.zeros(total_ref.shape, F32)
    for j, start in enumerate(starts):
        for copy in copies[j]:
            copy.wait()
        x = shape_buf[pl.ds(start, chunk), :]
        inv_rate = reciprocal(rate_buf[pl.ds(start, chunk), :])
        value = exp_digamma(x, inv_rate).astype(BF16)
        both_ref[j * chunk : (j + 1) * chunk, :] = value
        target = keep_ref if j < steps else give_ref
        target[(j % steps) * chunk : (j % steps + 1) * chunk, :] = value
        total += jnp.sum(x * inv_rate, axis=0, keepdims=True)
    total_ref[...] = total
    for target in (keep_ref, give_ref):
        target[half:, :] = jnp.zeros((32, target.shape[1]), BF16)


def expected_users(shape_arg, rate_arg):
    rows, cols = shape_arg.shape
    chunk = min(rows // 2, 128)
    return pl.pallas_call(
        functools.partial(users_kernel, chunk),
        in_specs=[pl.BlockSpec(memory_space=HBM)] * 2,
        out_specs=[pl.BlockSpec(memory_space=VMEM)] * 4,
        out_shape=[
            jax.ShapeDtypeStruct((rows, cols), BF16),
            jax.ShapeDtypeStruct((rows // 2 + 32, cols), BF16),
            jax.ShapeDtypeStruct((rows // 2 + 32, cols), BF16),
            jax.ShapeDtypeStruct((1, cols), F32),
        ],
        scratch_shapes=[
            pltpu.VMEM((rows, cols), F32),
            pltpu.VMEM((rows, cols), F32),
            pltpu.SemaphoreType.DMA((2, rows // chunk)),
        ],
        compiler_params=pltpu.CompilerParams(vmem_limit_bytes=4 * MIB),
        cost_estimate=CHEAP,
        name="expected_users",
    )(pinned(shape_arg), pinned(rate_arg))


def items_kernel(chunk, shape_ref, rate_ref, both_ref, theta_ref, item_ref, pack_ref, shape_buf, rate_buf, sems):
    rows = shape_ref.shape[0]
    half = both_ref.shape[0] // 2
    starts = list(range(0, rows, chunk))
    copies = chunk_copies(starts, chunk, (shape_ref, rate_ref), (shape_buf, rate_buf), sems)
    pack_ref[:half, :] = both_ref[half:, :]
    total = jnp.zeros(theta_ref.shape, F32)
    for j, start in enumerate(starts):
        for copy in copies[j]:
            copy.wait()
        x = shape_buf[start : start + chunk, :]
        inv_rate = reciprocal(rate_buf[start : start + chunk, :])
        value = exp_digamma(x, inv_rate).astype(BF16)
        item_ref[start : start + chunk, :] = value
        pack_ref[half + start : half + start + chunk, :] = value
        total += jnp.sum(x * inv_rate, axis=0, keepdims=True)
    extra = encode([theta_ref[...], total])
    item_ref[rows:, :] = extra
    pack_ref[half + rows :, :] = extra


def expected_items(shape_arg, rate_arg, both, theta_local):
    rows, cols = shape_arg.shape
    chunk = min(rows, 128)
    return pl.pallas_call(
        functools.partial(items_kernel, chunk),
        in_specs=[pl.BlockSpec(memory_space=m) for m in (HBM, HBM, VMEM, VMEM)],
        out_specs=[pl.BlockSpec(memory_space=VMEM)] * 2,
        out_shape=[jax.ShapeDtypeStruct((r + EXTRA, cols), BF16) for r in (rows, both.shape[0] // 2 + rows)],
        scratch_shapes=[
            pltpu.VMEM((rows, cols), F32),
            pltpu.VMEM((rows, cols), F32),
            pltpu.SemaphoreType.DMA((2, rows // chunk)),
        ],
        compiler_params=pltpu.CompilerParams(vmem_limit_bytes=4 * MIB),
        cost_estimate=CHEAP,
        name="expected_items",
    )(pinned(shape_arg), pinned(rate_arg), both, theta_local)


def dense_kernel(n_item, shard_tiles, chunk, rows, users_in, items_in, live_ref, counts_ref, out_ref, *scratch):
    users_ref, items_ref, buf, sems, index_sems = scratch
    tile = counts_ref.shape[1]
    half = rows // 2
    piece = min(half, tile)
    n_chunks = counts_ref.shape[0] // chunk
    copies = [
        pltpu.make_async_copy(
            counts_ref.at[pl.ds(c * chunk, chunk)], buf.at[pl.ds(c * chunk, chunk)], sems.at[c]
        )
        for c in range(n_chunks)
    ]
    index_copies = [
        pltpu.make_async_copy(users_in, users_ref, index_sems.at[0]),
        pltpu.make_async_copy(items_in, items_ref, index_sems.at[1]),
    ]
    for copy in index_copies + copies:
        copy.start()
    out_ref[...] = jnp.zeros_like(out_ref)
    for copy in index_copies:
        copy.wait()
    z = lax.axis_index("item")
    x = lax.axis_index("user")
    core = lax.axis_index("ka")
    live = live_ref[0]

    def place(slot, carry):
        item = items_ref[slot]
        owner = lax.div(item, shard_tiles)
        column = (owner ^ x) * shard_tiles + lax.rem(item, shard_tiles)
        col = pl.multiple_of(column * tile, tile)
        for j in range(tile // piece):
            row = users_ref[slot] * tile + j * piece
            shard = lax.div(row, rows)
            within = lax.rem(row, rows)

            @pl.when(lax.div(within, half) == core)
            def _():
                back = lax.rem(z - shard + n_item, n_item)
                step = jnp.where(back == 0, 0, jnp.where(back * 2 <= n_item, 2 * back - 1, 2 * (n_item - back)))
                start = pl.multiple_of(step * half + lax.rem(within, half), piece)
                value = buf[slot, j * piece : (j + 1) * piece, :].astype(F32).astype(BF16)
                out_ref[pl.ds(start, piece), pl.ds(col, tile)] = value

        return carry

    for c in range(n_chunks):
        copies[c].wait()
        lax.fori_loop(c * chunk, jnp.clip(live, c * chunk, (c + 1) * chunk), place, 0)


def dense_counts(counts, users, items, live, rows, n_item, item_rows, n_user):
    slots, tile, _ = counts.shape
    chunk = 8
    out_rows = n_item * rows // 2
    return pl.pallas_call(
        functools.partial(dense_kernel, n_item, item_rows // n_user // tile, chunk, rows),
        in_specs=[pl.BlockSpec(memory_space=m) for m in (HBM, HBM, SMEM, HBM)],
        out_specs=pl.BlockSpec(memory_space=VMEM),
        out_shape=jax.ShapeDtypeStruct((out_rows, item_rows), BF16),
        scratch_shapes=[
            pltpu.SMEM(users.shape, jnp.int32),
            pltpu.SMEM(items.shape, jnp.int32),
            pltpu.VMEM((slots, tile, tile), jnp.int32),
            pltpu.SemaphoreType.DMA((slots // chunk,)),
            pltpu.SemaphoreType.DMA((2,)),
        ],
        compiler_params=pltpu.CompilerParams(vmem_limit_bytes=8 * MIB),
        cost_estimate=CHEAP,
        name="dense_counts",
    )(pinned(users), pinned(items), live, pinned(counts))


def stat_kernel(pieces, half, last, has_acc, at, *refs):
    refs = list(refs)
    take = lambda n: [refs.pop(0) for _ in range(n)]
    mine_ref, other_ref = take(2)
    mine = mine_ref[:half, :]
    other = other_ref[:half, :]
    item_mine = take(pieces)
    item_other = take(pieces)
    (counts_ref,) = take(1)
    (acc_in,) = take(1) if has_acc else (None,)
    stat_refs = take(1 if at else 2)
    acc_refs = take(1 + pieces if last else 1)
    cols = mine.shape[1]
    total_mine = None
    total_other = None
    width = 256
    for p in range(pieces):
        rows = item_mine[p].shape[0] - EXTRA
        skip = item_other[p].shape[0] - EXTRA - rows
        for c in range(rows // width):
            left = item_mine[p][c * width : (c + 1) * width, :]
            right = item_other[p][skip + c * width : skip + (c + 1) * width, :]
            norm = lax.dot_general(mine, left, DIMS_NT, preferred_element_type=F32)
            norm += lax.dot_general(other, right, DIMS_NT, preferred_element_type=F32)
            columns = slice(p * rows + c * width, p * rows + (c + 1) * width)
            grid = counts_ref[at * half : (at + 1) * half, columns].astype(F32)
            ratio = (grid * reciprocal(norm)).astype(BF16)
            stat = jnp.dot(ratio, left, preferred_element_type=F32)
            total_mine = stat if total_mine is None else total_mine + stat
            stat = jnp.dot(ratio, right, preferred_element_type=F32)
            total_other = stat if total_other is None else total_other + stat
            for i, factors in enumerate((mine, other)):
                update = lax.dot_general(factors, ratio, DIMS_TN, preferred_element_type=F32)
                if has_acc:
                    update += acc_in[i * cols : (i + 1) * cols, columns]
                if last and i == 0:
                    acc_refs[0][:, columns] = update
                elif last:
                    acc_refs[1 + p][:, c * width : (c + 1) * width] = update.astype(BF16)
                else:
                    acc_refs[0][i * cols : (i + 1) * cols, columns] = update
    if at:
        stat_refs[0][:half, :] = total_mine.astype(BF16)
        stat_refs[0][half : 2 * half, :] = total_other.astype(BF16)
        stat_refs[0][2 * half :, :] = encode(row_totals(item_mine))
    else:
        stat_refs[0][...] = total_mine
        stat_refs[1][...] = total_other


def sum_totals(blocks):
    sums = None
    for block in blocks:
        came = decode(block)
        sums = came if sums is None else [a + b for a, b in zip(sums, came)]
    return sums


def row_totals(item_refs):
    return sum_totals([ref[-EXTRA:, :] for ref in item_refs])


def statistics(at, users, item_mine, item_other, dense, acc, last, half_rows):
    half = users[0].shape[1]
    item_rows = dense.shape[1]
    args = [*users, *item_mine, *item_other, dense]
    if acc is not None:
        args.append(acc)
    if at:
        out_shape = [jax.ShapeDtypeStruct((2 * half_rows + EXTRA, half), BF16)]
    else:
        out_shape = [jax.ShapeDtypeStruct((half_rows, half), F32)] * 2
    n_stats = len(out_shape)
    if last:
        out_shape.append(jax.ShapeDtypeStruct((half, item_rows), F32))
        out_shape += [jax.ShapeDtypeStruct((half, item_rows // len(item_mine)), BF16) for _ in item_mine]
    else:
        out_shape.append(jax.ShapeDtypeStruct((2 * half, item_rows), F32))
    spec = pl.BlockSpec(memory_space=VMEM)
    out = pl.pallas_call(
        functools.partial(stat_kernel, len(item_mine), half_rows, last, acc is not None, at),
        in_specs=[spec] * len(args),
        out_specs=[spec] * len(out_shape),
        out_shape=out_shape,
        compiler_params=pltpu.CompilerParams(vmem_limit_bytes=16 * MIB),
        cost_estimate=CHEAP,
        name="statistics_%d" % at,
    )(*args)
    return list(out[:n_stats]), list(out[n_stats:])


def add_kernel(stat_ref, came_ref, out_ref):
    rows = stat_ref.shape[0] - EXTRA
    out_ref[:rows, :] = (stat_ref[:rows, :].astype(F32) + came_ref[:rows, :].astype(F32)).astype(BF16)
    out_ref[rows:, :] = encode(sum_totals([stat_ref[rows:, :], came_ref[rows:, :]]))


def split_kernel(stat_ref, came_ref, other_ref, mine_ref):
    half = other_ref.shape[0] - EXTRA
    total = stat_ref[: 2 * half, :].astype(F32) + came_ref[: 2 * half, :].astype(F32)
    other_ref[:half, :] = total[half:, :].astype(BF16)
    other_ref[half:, :] = encode(sum_totals([stat_ref[2 * half :, :], came_ref[2 * half :, :]]))
    mine_ref[:half, :] = total[:half, :].astype(BF16)
    mine_ref[half:, :] = jnp.zeros((2 * EXTRA, mine_ref.shape[1]), BF16)


def add_came(stat, came, split):
    rows, cols = stat.shape
    half = (rows - EXTRA) // 2
    shapes = [half + EXTRA, half + 2 * EXTRA] if split else [rows]
    out = pl.pallas_call(
        split_kernel if split else add_kernel,
        in_specs=[pl.BlockSpec(memory_space=VMEM)] * 2,
        out_specs=[pl.BlockSpec(memory_space=VMEM)] * len(shapes),
        out_shape=[jax.ShapeDtypeStruct((r, cols), BF16) for r in shapes],
        compiler_params=pltpu.CompilerParams(vmem_limit_bytes=2 * MIB),
        cost_estimate=CHEAP,
        name="add_came",
    )(stat, came)
    return list(out)


def merge_items_kernel(p, mine_ref, came_ref, out_ref):
    width = out_ref.shape[1]
    out_ref[...] = (mine_ref[:, p * width : (p + 1) * width] + came_ref[...].astype(F32)).astype(BF16)


def merge_items(p, mine, came):
    return pl.pallas_call(
        functools.partial(merge_items_kernel, p),
        in_specs=[pl.BlockSpec(memory_space=VMEM)] * 2,
        out_specs=pl.BlockSpec(memory_space=VMEM),
        out_shape=jax.ShapeDtypeStruct(came.shape, BF16),
        compiler_params=pltpu.CompilerParams(vmem_limit_bytes=2 * MIB),
        cost_estimate=CHEAP,
        name="merge_items",
    )(mine, came)


def finish_rates_kernel(pieces, n_came, *refs):
    refs = list(refs)
    take = lambda n: [refs.pop(0) for _ in range(n)]
    item_refs = take(pieces)
    came = take(n_came)
    columns = take(2)
    outs = take(2)
    bufs = take(2)
    (sems,) = take(1)
    theta_total, beta_total = sum_totals([ref[-EXTRA:, :] for ref in item_refs + came])
    copies = []
    for i, total in enumerate((beta_total, theta_total)):
        rows = columns[i].shape[1]
        column = jnp.broadcast_to(columns[i][...], (total.shape[1], rows)).T
        bufs[i][...] = column + total
        copies.append(pltpu.make_async_copy(bufs[i], outs[i], sems.at[i]))
        copies[-1].start()
    for copy in copies:
        copy.wait()


def finish_rates(items, came, activity, popularity):
    args = [*items, *came, activity, popularity]
    out_shape = [jax.ShapeDtypeStruct((c.shape[1], items[0].shape[1]), F32) for c in (activity, popularity)]
    return pl.pallas_call(
        functools.partial(finish_rates_kernel, len(items), len(came)),
        in_specs=[pl.BlockSpec(memory_space=VMEM)] * len(args),
        out_specs=[pl.BlockSpec(memory_space=HBM)] * 2,
        out_shape=out_shape,
        scratch_shapes=[pltpu.VMEM(o.shape, F32) for o in out_shape] + [pltpu.SemaphoreType.DMA((2,))],
        compiler_params=pltpu.CompilerParams(vmem_limit_bytes=6 * MIB),
        cost_estimate=CHEAP,
        name="finish_rates",
    )(*args)


def finish_users_kernel(n_ahead, *refs):
    refs = list(refs)
    take = lambda n: [refs.pop(0) for _ in range(n)]
    both_ref, own_ref, other_ref, last_ref, mine_ref = take(5)
    ahead = take(n_ahead)
    out_ref, buf, sems = take(3)
    core = lax.axis_index("ka")
    half = own_ref.shape[0]

    def send(i, side, rows, total):
        here = pl.ds(pl.multiple_of(side * half, half), half)
        buf[here, :] = 0.3 + both_ref[rows, :].astype(F32) * total
        copy = pltpu.make_async_copy(buf.at[here], out_ref.at[here], sems.at[i])
        copy.start()
        return copy

    total = own_ref[...] + mine_ref[:half, :].astype(F32)
    for ref in ahead:
        total += ref[:half, :].astype(F32)
    other = other_ref[...].astype(F32) + last_ref[:half, :].astype(F32)
    copies = [send(0, core, slice(0, half), total), send(1, 1 - core, slice(half, 2 * half), other)]
    for copy in copies:
        copy.wait()


def finish_users(both, own, other_sum, other_last, mine, ahead):
    rows, half = both.shape
    args = [both, own, other_sum, other_last, mine, *ahead]
    return pl.pallas_call(
        functools.partial(finish_users_kernel, len(ahead)),
        in_specs=[pl.BlockSpec(memory_space=VMEM)] * len(args),
        out_specs=pl.BlockSpec(memory_space=HBM),
        out_shape=jax.ShapeDtypeStruct((rows, half), F32),
        scratch_shapes=[pltpu.VMEM((rows, half), F32), pltpu.SemaphoreType.DMA((2,))],
        compiler_params=pltpu.CompilerParams(vmem_limit_bytes=4 * MIB),
        cost_estimate=CHEAP,
        name="finish_users",
    )(*args)


def finish_items_kernel(n, exp_ref, own_ref, *refs):
    out_ref, buf, sems = refs[n:]
    rows = out_ref.shape[0]
    chunk = min(rows, 256)
    copies = []
    for j in range(rows // chunk):
        part = slice(j * chunk, (j + 1) * chunk)
        total = own_ref[:, part]
        for p in range(n):
            total += refs[p][:, part].astype(F32)
        buf[part, :] = 0.3 + exp_ref[part, :].astype(F32) * total.T
        here = pl.ds(j * chunk, chunk)
        copies.append(pltpu.make_async_copy(buf.at[here], out_ref.at[here], sems.at[j]))
        copies[-1].start()
    for copy in copies:
        copy.wait()


def finish_items(item_exp, own, came):
    half, rows = came[0].shape
    return pl.pallas_call(
        functools.partial(finish_items_kernel, len(came)),
        in_specs=[pl.BlockSpec(memory_space=VMEM)] * (2 + len(came)),
        out_specs=pl.BlockSpec(memory_space=HBM),
        out_shape=jax.ShapeDtypeStruct((rows, half), F32),
        scratch_shapes=[pltpu.VMEM((rows, half), F32), pltpu.SemaphoreType.DMA((rows // min(rows, 256),))],
        compiler_params=pltpu.CompilerParams(vmem_limit_bytes=6 * MIB),
        cost_estimate=CHEAP,
        name="finish_items",
    )(item_exp, own, *came)


def along_item(x, shift, n):
    return lax.ppermute(x, "item", [(i, (i + shift) % n) for i in range(n)])


def across_item(x, shift, n, n_ka):
    pairs = [(i * n_ka + h, (i + shift) % n * n_ka + n_ka - 1 - h) for i in range(n) for h in range(n_ka)]
    return lax.ppermute(x, ("item", "ka"), pairs)


def after(x, y):
    return lax.optimization_barrier((x, y))[0]


def along_user(x, distance, n):
    return lax.ppermute(x, "user", [(i, i ^ distance) for i in range(n)])


def body(
    n_item,
    n_user,
    n_ka,
    counts,
    tile_user,
    tile_item,
    tile_live,
    theta_shape,
    theta_rate,
    user_activity,
    beta_shape,
    beta_rate,
    item_popularity,
):
    def sibling(x):
        return lax.ppermute(x, "ka", [(h, n_ka - 1 - h) for h in range(n_ka)])

    both, keep, give, theta_local = expected_users(theta_shape[0], theta_rate[0])
    item_exp, pack = expected_items(beta_shape[0], beta_rate[0], both, theta_local)
    rows = both.shape[0]
    half_rows = rows // 2
    item_rows = beta_shape.shape[1] * n_user
    dense = dense_counts(
        counts[0, 0],
        tile_user[0, 0],
        tile_item[0, 0],
        tile_live[0],
        rows,
        n_item,
        item_rows,
        n_user,
    )
    came_pack = sibling(pack)

    ahead = range(1, n_item // 2)
    behind = range(1, n_item // 2 + 1)
    shards = {0: both}
    for d in behind:
        shards[2 * d - 1] = along_item(shards[max(2 * d - 3, 0)], 1, n_item)
    crossed = {}
    for d in ahead:
        if d == 1:
            shards[2] = along_item(after(keep, shards[1]), -1, n_item)
            crossed[2] = across_item(after(give, shards[1]), -1, n_item, n_ka)
        else:
            shards[2 * d] = along_item(shards[2 * d - 2], -1, n_item)
            crossed[2 * d] = along_item(crossed[2 * d - 2], -1, n_item)

    item_mine = [item_exp]
    for p in range(1, n_user):
        low = p & -p
        item_mine.append(along_user(after(item_mine[p ^ low], dense), low, n_user))
    item_other = [came_pack] + [sibling(x) for x in item_mine[1:]]

    order = [2 * d - 1 for d in behind] + [2 * d for d in ahead]
    order.insert(len(order) - 1, 0)
    acc = None
    stats = {}
    latest = None
    for i in order:
        if i == 0:
            other = came_pack
        else:
            other = sibling(shards[i][half_rows:]) if i % 2 else crossed[i]
        stats[i], accs = statistics(
            i, [shards[i], other], item_mine, item_other, dense, acc, i == order[-1], half_rows
        )
        acc = accs[0]
        latest = stats[i][0]
    own, own_other = stats[0]

    came = [sibling(accs[1])]
    for p in range(1, n_user):
        sent = merge_items(p, acc, sibling(accs[1 + p]))
        came.append(along_user(sent, p, n_user))
    new_beta_shape = finish_items(item_exp, acc, came)

    moving = []
    for d in reversed(ahead):
        stat = stats[2 * d][0]
        parts = add_came(stat, moving[0], False) if moving else [stat]
        moving = [along_item(x, 1, n_item) for x in parts]
    came_ahead = moving
    moving = []
    for d in reversed(behind):
        stat = stats[2 * d - 1][0]
        if d == 1 and n_user > 1:
            stat = after(stat, sent)
        parts = add_came(stat, moving[0], d == 1) if moving else [stat]
        moving = [along_item(x, -1, n_item) for x in parts]
    other_behind, mine_behind = moving

    other_sum = own_other
    for x in came_ahead:
        other_sum = lax.optimization_barrier(other_sum + x[half_rows:rows].astype(F32))
    other_sum = other_sum.astype(BF16)
    other_sum = sibling(other_sum)
    other_last = after(sibling(other_behind), new_beta_shape)
    new_theta_rate, new_beta_rate = finish_rates(
        item_mine, [*came_ahead, other_behind], user_activity, item_popularity
    )
    other_last = after(other_last, new_theta_rate)
    new_theta_shape = finish_users(both, own, other_sum, other_last, mine_behind, came_ahead)
    return (new_theta_shape[None], new_theta_rate[None], new_beta_shape[None], new_beta_rate[None])


def solution(mesh):
    in_specs = (
        P(("parts", "item"), "user", None, None, None),
        P(("parts", "item"), "user", None),
        P(("parts", "item"), "user", None),
        P(("parts", "item"), "user"),
        P(("parts", "user"), "item", "ka"),
        P(("parts", "user"), "item", "ka"),
        P(("parts", "user"), "item"),
        P(("parts", "item"), "user", "ka"),
        P(("parts", "item"), "user", "ka"),
        P(("parts", "item"), "user"),
    )
    out_specs = (
        P(("parts", "user"), "item", "ka"),
        P(("parts", "user"), "item", "ka"),
        P(("parts", "item"), "user", "ka"),
        P(("parts", "item"), "user", "ka"),
    )
    run = functools.partial(body, mesh.shape["item"], mesh.shape["user"], mesh.shape["ka"])
    return jax.shard_map(run, mesh=mesh, in_specs=in_specs, out_specs=out_specs, check_vma=False)
```

```python
import functools

import jax
import jax.numpy as jnp
from jax import lax
from jax.experimental import pallas as pl
from jax.experimental.pallas import tpu as pltpu
from jax.sharding import PartitionSpec as P

BF16 = jnp.bfloat16
F32 = jnp.float32
VMEM = pltpu.MemorySpace.VMEM
SMEM = pltpu.MemorySpace.SMEM
HBM = pltpu.MemorySpace.HBM
EXTRA = 16
MIB = 1024 * 1024
CHEAP = pl.CostEstimate(flops=1024, transcendentals=0, bytes_accessed=1024)
DIMS_NT = (((1,), (1,)), ((), ()))
DIMS_TN = (((0,), (0,)), ((), ()))


def pinned(x):
    return pltpu.with_memory_space_constraint(x, HBM)


def reciprocal(x):
    r = pl.reciprocal(x, approx=True)
    return r * (2.0 - x * r)


def exp_digamma(x, inv_rate):
    w = x * (x + 3.0)
    p = w * (w + 2.0)
    y = x + 4.0
    inv = reciprocal(y * p)
    iy = inv * p
    iy2 = iy * iy
    shift = (2.0 * x + 3.0) * (2.0 * w + 2.0) * (inv * y)
    series = iy * 0.5 + iy2 * (1.0 / 12.0 - iy2 * (1.0 / 120.0 - iy2 * (1.0 / 252.0)))
    return y * inv_rate * jnp.exp(-(series + shift))


def encode(values):
    row = lax.broadcasted_iota(jnp.int32, (EXTRA, values[0].shape[1]), 0)
    out = jnp.zeros(row.shape, F32)
    for i, rest in enumerate(values):
        for j in range(3):
            piece = rest.astype(BF16).astype(F32)
            rest = rest - piece
            out = jnp.where(row == 3 * i + j, piece, out)
    return out.astype(BF16)


def decode(block):
    block = block.astype(F32)
    return [block[3 * i : 3 * i + 1] + block[3 * i + 1 : 3 * i + 2] + block[3 * i + 2 : 3 * i + 3] for i in range(2)]


def chunk_copies(starts, chunk, refs, buffers, sems):
    copies = []
    for j, start in enumerate(starts):
        here = pl.ds(start, chunk)
        copies.append(
            [pltpu.make_async_copy(r.at[here], b.at[here], sems.at[i, j]) for i, (r, b) in enumerate(zip(refs, buffers))]
        )
    for group in copies:
        for copy in group:
            copy.start()
    return copies


def users_kernel(chunk, shape_ref, rate_ref, both_ref, wide_ref, total_ref, shape_buf, rate_buf, sems):
    core = lax.axis_index("ka")
    half = both_ref.shape[0] // 2
    steps = half // chunk
    starts = []
    for side in (core, 1 - core):
        starts += [pl.multiple_of(side * half + j * chunk, chunk) for j in range(steps)]
    copies = chunk_copies(starts, chunk, (shape_ref, rate_ref), (shape_buf, rate_buf), sems)
    total = jnp.zeros(total_ref.shape, F32)
    for j, start in enumerate(starts):
        for copy in copies[j]:
            copy.wait()
        x = shape_buf[pl.ds(start, chunk), :]
        inv_rate = reciprocal(rate_buf[pl.ds(start, chunk), :])
        value = exp_digamma(x, inv_rate).astype(BF16)
        both_ref[j * chunk : (j + 1) * chunk, :] = value
        wide_ref[j * chunk : (j + 1) * chunk, :] = value
        total += jnp.sum(x * inv_rate, axis=0, keepdims=True)
    total_ref[...] = total
    wide_ref[2 * half :, :] = jnp.zeros((wide_ref.shape[0] - 2 * half, wide_ref.shape[1]), BF16)


def expected_users(shape_arg, rate_arg):
    rows, cols = shape_arg.shape
    chunk = min(rows // 2, 128)
    return pl.pallas_call(
        functools.partial(users_kernel, chunk),
        in_specs=[pl.BlockSpec(memory_space=HBM)] * 2,
        out_specs=[pl.BlockSpec(memory_space=VMEM)] * 3,
        out_shape=[
            jax.ShapeDtypeStruct((rows, cols), BF16),
            jax.ShapeDtypeStruct((rows + 3 * EXTRA, cols), BF16),
            jax.ShapeDtypeStruct((1, cols), F32),
        ],
        scratch_shapes=[
            pltpu.VMEM((rows, cols), F32),
            pltpu.VMEM((rows, cols), F32),
            pltpu.SemaphoreType.DMA((2, rows // chunk)),
        ],
        compiler_params=pltpu.CompilerParams(vmem_limit_bytes=4 * MIB),
        cost_estimate=CHEAP,
        name="expected_users",
    )(pinned(shape_arg), pinned(rate_arg))


def items_kernel(chunk, shape_ref, rate_ref, both_ref, theta_ref, item_ref, pack_ref, shape_buf, rate_buf, sems):
    rows = shape_ref.shape[0]
    half = both_ref.shape[0] // 2
    starts = list(range(0, rows, chunk))
    copies = chunk_copies(starts, chunk, (shape_ref, rate_ref), (shape_buf, rate_buf), sems)
    pack_ref[:half, :] = both_ref[half:, :]
    total = jnp.zeros(theta_ref.shape, F32)
    for j, start in enumerate(starts):
        for copy in copies[j]:
            copy.wait()
        x = shape_buf[start : start + chunk, :]
        inv_rate = reciprocal(rate_buf[start : start + chunk, :])
        value = exp_digamma(x, inv_rate).astype(BF16)
        item_ref[start : start + chunk, :] = value
        pack_ref[half + start : half + start + chunk, :] = value
        total += jnp.sum(x * inv_rate, axis=0, keepdims=True)
    extra = encode([theta_ref[...], total])
    item_ref[rows:, :] = extra
    pack_ref[half + rows :, :] = extra


def expected_items(shape_arg, rate_arg, both, theta_local):
    rows, cols = shape_arg.shape
    chunk = min(rows, 128)
    return pl.pallas_call(
        functools.partial(items_kernel, chunk),
        in_specs=[pl.BlockSpec(memory_space=m) for m in (HBM, HBM, VMEM, VMEM)],
        out_specs=[pl.BlockSpec(memory_space=VMEM)] * 2,
        out_shape=[jax.ShapeDtypeStruct((r + EXTRA, cols), BF16) for r in (rows, both.shape[0] // 2 + rows)],
        scratch_shapes=[
            pltpu.VMEM((rows, cols), F32),
            pltpu.VMEM((rows, cols), F32),
            pltpu.SemaphoreType.DMA((2, rows // chunk)),
        ],
        compiler_params=pltpu.CompilerParams(vmem_limit_bytes=4 * MIB),
        cost_estimate=CHEAP,
        name="expected_items",
    )(pinned(shape_arg), pinned(rate_arg), both, theta_local)


def dense_kernel(n_item, shard_tiles, chunk, rows, users_in, items_in, live_ref, counts_ref, out_ref, *scratch):
    users_ref, items_ref, buf, sems, index_sems = scratch
    tile = counts_ref.shape[1]
    half = rows // 2
    piece = min(half, tile)
    n_chunks = counts_ref.shape[0] // chunk
    copies = [
        pltpu.make_async_copy(
            counts_ref.at[pl.ds(c * chunk, chunk)], buf.at[pl.ds(c * chunk, chunk)], sems.at[c]
        )
        for c in range(n_chunks)
    ]
    index_copies = [
        pltpu.make_async_copy(users_in, users_ref, index_sems.at[0]),
        pltpu.make_async_copy(items_in, items_ref, index_sems.at[1]),
    ]
    for copy in index_copies + copies:
        copy.start()
    out_ref[...] = jnp.zeros_like(out_ref)
    for copy in index_copies:
        copy.wait()
    z = lax.axis_index("item")
    x = lax.axis_index("user")
    core = lax.axis_index("ka")
    live = live_ref[0]

    def place(slot, carry):
        item = items_ref[slot]
        owner = lax.div(item, shard_tiles)
        column = (owner ^ x) * shard_tiles + lax.rem(item, shard_tiles)
        col = pl.multiple_of(column * tile, tile)
        for j in range(tile // piece):
            row = users_ref[slot] * tile + j * piece
            shard = lax.div(row, rows)
            within = lax.rem(row, rows)

            @pl.when(lax.div(within, half) == core)
            def _():
                back = lax.rem(z - shard + n_item, n_item)
                step = jnp.where(back == 0, 0, jnp.where(back * 2 <= n_item, 2 * back - 1, 2 * (n_item - back)))
                start = pl.multiple_of(step * half + lax.rem(within, half), piece)
                value = buf[slot, j * piece : (j + 1) * piece, :].astype(F32).astype(BF16)
                out_ref[pl.ds(start, piece), pl.ds(col, tile)] = value

        return carry

    for c in range(n_chunks):
        copies[c].wait()
        lax.fori_loop(c * chunk, jnp.clip(live, c * chunk, (c + 1) * chunk), place, 0)


def dense_counts(counts, users, items, live, rows, n_item, item_rows, n_user):
    slots, tile, _ = counts.shape
    chunk = 8
    out_rows = n_item * rows // 2
    return pl.pallas_call(
        functools.partial(dense_kernel, n_item, item_rows // n_user // tile, chunk, rows),
        in_specs=[pl.BlockSpec(memory_space=m) for m in (HBM, HBM, SMEM, HBM)],
        out_specs=pl.BlockSpec(memory_space=VMEM),
        out_shape=jax.ShapeDtypeStruct((out_rows, item_rows), BF16),
        scratch_shapes=[
            pltpu.SMEM(users.shape, jnp.int32),
            pltpu.SMEM(items.shape, jnp.int32),
            pltpu.VMEM((slots, tile, tile), jnp.int32),
            pltpu.SemaphoreType.DMA((slots // chunk,)),
            pltpu.SemaphoreType.DMA((2,)),
        ],
        compiler_params=pltpu.CompilerParams(vmem_limit_bytes=8 * MIB),
        cost_estimate=CHEAP,
        name="dense_counts",
    )(pinned(users), pinned(items), live, pinned(counts))


def stat_kernel(pieces, half, last, has_acc, at, *refs):
    refs = list(refs)
    take = lambda n: [refs.pop(0) for _ in range(n)]
    mine_ref, other_ref = take(2)
    mine = mine_ref[:half, :]
    other = other_ref[half : 2 * half, :] if at and not last else other_ref[:half, :]
    item_mine = take(pieces)
    item_other = take(pieces)
    (counts_ref,) = take(1)
    (acc_in,) = take(1) if has_acc else (None,)
    stat_refs = take(1 if at else 2)
    acc_refs = take(1 + pieces if last else 1)
    cols = mine.shape[1]
    total_mine = None
    total_other = None
    width = 256
    for p in range(pieces):
        rows = item_mine[p].shape[0] - EXTRA
        skip = item_other[p].shape[0] - EXTRA - rows
        for c in range(rows // width):
            left = item_mine[p][c * width : (c + 1) * width, :]
            right = item_other[p][skip + c * width : skip + (c + 1) * width, :]
            norm = lax.dot_general(mine, left, DIMS_NT, preferred_element_type=F32)
            norm += lax.dot_general(other, right, DIMS_NT, preferred_element_type=F32)
            columns = slice(p * rows + c * width, p * rows + (c + 1) * width)
            grid = counts_ref[at * half : (at + 1) * half, columns].astype(F32)
            ratio = (grid * reciprocal(norm)).astype(BF16)
            stat = jnp.dot(ratio, left, preferred_element_type=F32)
            total_mine = stat if total_mine is None else total_mine + stat
            stat = jnp.dot(ratio, right, preferred_element_type=F32)
            total_other = stat if total_other is None else total_other + stat
            for i, factors in enumerate((mine, other)):
                update = lax.dot_general(factors, ratio, DIMS_TN, preferred_element_type=F32)
                if has_acc:
                    update += acc_in[i * cols : (i + 1) * cols, columns]
                if last and i == 0:
                    acc_refs[0][:, columns] = update
                elif last:
                    acc_refs[1 + p][:, c * width : (c + 1) * width] = update.astype(BF16)
                else:
                    acc_refs[0][i * cols : (i + 1) * cols, columns] = update
    if at:
        stat_refs[0][:half, :] = total_mine.astype(BF16)
        stat_refs[0][half : 2 * half, :] = total_other.astype(BF16)
        stat_refs[0][2 * half :, :] = encode(row_totals(item_mine))
    else:
        stat_refs[0][...] = total_mine
        stat_refs[1][...] = total_other


def sum_totals(blocks):
    sums = None
    for block in blocks:
        came = decode(block)
        sums = came if sums is None else [a + b for a, b in zip(sums, came)]
    return sums


def row_totals(item_refs):
    return sum_totals([ref[-EXTRA:, :] for ref in item_refs])


def statistics(at, users, item_mine, item_other, dense, acc, last, half_rows):
    half = users[0].shape[1]
    item_rows = dense.shape[1]
    args = [*users, *item_mine, *item_other, dense]
    if acc is not None:
        args.append(acc)
    if at:
        out_shape = [jax.ShapeDtypeStruct((2 * half_rows + EXTRA, half), BF16)]
    else:
        out_shape = [jax.ShapeDtypeStruct((half_rows, half), F32)] * 2
    n_stats = len(out_shape)
    if last:
        out_shape.append(jax.ShapeDtypeStruct((half, item_rows), F32))
        out_shape += [jax.ShapeDtypeStruct((half, item_rows // len(item_mine)), BF16) for _ in item_mine]
    else:
        out_shape.append(jax.ShapeDtypeStruct((2 * half, item_rows), F32))
    spec = pl.BlockSpec(memory_space=VMEM)
    out = pl.pallas_call(
        functools.partial(stat_kernel, len(item_mine), half_rows, last, acc is not None, at),
        in_specs=[spec] * len(args),
        out_specs=[spec] * len(out_shape),
        out_shape=out_shape,
        compiler_params=pltpu.CompilerParams(vmem_limit_bytes=16 * MIB),
        cost_estimate=CHEAP,
        name="statistics_%d" % at,
    )(*args)
    return list(out[:n_stats]), list(out[n_stats:])


def add_kernel(stat_ref, came_ref, out_ref):
    rows = stat_ref.shape[0] - EXTRA
    out_ref[:rows, :] = (stat_ref[:rows, :].astype(F32) + came_ref[:rows, :].astype(F32)).astype(BF16)
    out_ref[rows:, :] = encode(sum_totals([stat_ref[rows:, :], came_ref[rows:, :]]))


def split_kernel(stat_ref, came_ref, other_ref, mine_ref):
    half = other_ref.shape[0] - EXTRA
    total = stat_ref[: 2 * half, :].astype(F32) + came_ref[: 2 * half, :].astype(F32)
    other_ref[:half, :] = total[half:, :].astype(BF16)
    other_ref[half:, :] = encode(sum_totals([stat_ref[2 * half :, :], came_ref[2 * half :, :]]))
    mine_ref[:half, :] = total[:half, :].astype(BF16)
    mine_ref[half:, :] = jnp.zeros((2 * EXTRA, mine_ref.shape[1]), BF16)


def add_came(stat, came, split):
    rows, cols = stat.shape
    half = (rows - EXTRA) // 2
    shapes = [half + EXTRA, half + 2 * EXTRA] if split else [rows]
    out = pl.pallas_call(
        split_kernel if split else add_kernel,
        in_specs=[pl.BlockSpec(memory_space=VMEM)] * 2,
        out_specs=[pl.BlockSpec(memory_space=VMEM)] * len(shapes),
        out_shape=[jax.ShapeDtypeStruct((r, cols), BF16) for r in shapes],
        compiler_params=pltpu.CompilerParams(vmem_limit_bytes=2 * MIB),
        cost_estimate=CHEAP,
        name="add_came",
    )(stat, came)
    return list(out)


def merge_items_kernel(p, mine_ref, came_ref, out_ref):
    width = out_ref.shape[1]
    out_ref[...] = (mine_ref[:, p * width : (p + 1) * width] + came_ref[...].astype(F32)).astype(BF16)


def merge_items(p, mine, came):
    return pl.pallas_call(
        functools.partial(merge_items_kernel, p),
        in_specs=[pl.BlockSpec(memory_space=VMEM)] * 2,
        out_specs=pl.BlockSpec(memory_space=VMEM),
        out_shape=jax.ShapeDtypeStruct(came.shape, BF16),
        compiler_params=pltpu.CompilerParams(vmem_limit_bytes=2 * MIB),
        cost_estimate=CHEAP,
        name="merge_items",
    )(mine, came)


def finish_rates_kernel(pieces, n_came, *refs):
    refs = list(refs)
    take = lambda n: [refs.pop(0) for _ in range(n)]
    item_refs = take(pieces)
    came = take(n_came)
    columns = take(2)
    outs = take(2)
    bufs = take(2)
    (sems,) = take(1)
    theta_total, beta_total = sum_totals([ref[-EXTRA:, :] for ref in item_refs + came])
    copies = []
    for i, total in enumerate((beta_total, theta_total)):
        rows = columns[i].shape[1]
        column = jnp.broadcast_to(columns[i][...], (total.shape[1], rows)).T
        bufs[i][...] = column + total
        copies.append(pltpu.make_async_copy(bufs[i], outs[i], sems.at[i]))
        copies[-1].start()
    for copy in copies:
        copy.wait()


def finish_rates(items, came, activity, popularity):
    args = [*items, *came, activity, popularity]
    out_shape = [jax.ShapeDtypeStruct((c.shape[1], items[0].shape[1]), F32) for c in (activity, popularity)]
    return pl.pallas_call(
        functools.partial(finish_rates_kernel, len(items), len(came)),
        in_specs=[pl.BlockSpec(memory_space=VMEM)] * len(args),
        out_specs=[pl.BlockSpec(memory_space=HBM)] * 2,
        out_shape=out_shape,
        scratch_shapes=[pltpu.VMEM(o.shape, F32) for o in out_shape] + [pltpu.SemaphoreType.DMA((2,))],
        compiler_params=pltpu.CompilerParams(vmem_limit_bytes=6 * MIB),
        cost_estimate=CHEAP,
        name="finish_rates",
    )(*args)


def finish_users_kernel(n_ahead, *refs):
    refs = list(refs)
    take = lambda n: [refs.pop(0) for _ in range(n)]
    both_ref, own_ref, other_ref, last_ref, mine_ref = take(5)
    ahead = take(n_ahead)
    out_ref, buf, sems = take(3)
    core = lax.axis_index("ka")
    half = own_ref.shape[0]

    def send(i, side, rows, total):
        here = pl.ds(pl.multiple_of(side * half, half), half)
        buf[here, :] = 0.3 + both_ref[rows, :].astype(F32) * total
        copy = pltpu.make_async_copy(buf.at[here], out_ref.at[here], sems.at[i])
        copy.start()
        return copy

    total = own_ref[...] + mine_ref[:half, :].astype(F32)
    for ref in ahead:
        total += ref[:half, :].astype(F32)
    other = other_ref[...].astype(F32) + last_ref[:half, :].astype(F32)
    copies = [send(0, core, slice(0, half), total), send(1, 1 - core, slice(half, 2 * half), other)]
    for copy in copies:
        copy.wait()


def finish_users(both, own, other_sum, other_last, mine, ahead):
    rows, half = both.shape
    args = [both, own, other_sum, other_last, mine, *ahead]
    return pl.pallas_call(
        functools.partial(finish_users_kernel, len(ahead)),
        in_specs=[pl.BlockSpec(memory_space=VMEM)] * len(args),
        out_specs=pl.BlockSpec(memory_space=HBM),
        out_shape=jax.ShapeDtypeStruct((rows, half), F32),
        scratch_shapes=[pltpu.VMEM((rows, half), F32), pltpu.SemaphoreType.DMA((2,))],
        compiler_params=pltpu.CompilerParams(vmem_limit_bytes=4 * MIB),
        cost_estimate=CHEAP,
        name="finish_users",
    )(*args)


def finish_items_kernel(n, exp_ref, own_ref, *refs):
    out_ref, buf, sems = refs[n:]
    rows = out_ref.shape[0]
    chunk = min(rows, 256)
    copies = []
    for j in range(rows // chunk):
        part = slice(j * chunk, (j + 1) * chunk)
        total = own_ref[:, part]
        for p in range(n):
            total += refs[p][:, part].astype(F32)
        buf[part, :] = 0.3 + exp_ref[part, :].astype(F32) * total.T
        here = pl.ds(j * chunk, chunk)
        copies.append(pltpu.make_async_copy(buf.at[here], out_ref.at[here], sems.at[j]))
        copies[-1].start()
    for copy in copies:
        copy.wait()


def finish_items(item_exp, own, came):
    half, rows = came[0].shape
    return pl.pallas_call(
        functools.partial(finish_items_kernel, len(came)),
        in_specs=[pl.BlockSpec(memory_space=VMEM)] * (2 + len(came)),
        out_specs=pl.BlockSpec(memory_space=HBM),
        out_shape=jax.ShapeDtypeStruct((rows, half), F32),
        scratch_shapes=[pltpu.VMEM((rows, half), F32), pltpu.SemaphoreType.DMA((rows // min(rows, 256),))],
        compiler_params=pltpu.CompilerParams(vmem_limit_bytes=6 * MIB),
        cost_estimate=CHEAP,
        name="finish_items",
    )(item_exp, own, *came)


def along_item(x, shift, n):
    return lax.ppermute(x, "item", [(i, (i + shift) % n) for i in range(n)])


def after(x, y):
    return lax.optimization_barrier((x, y))[0]


def along_user(x, distance, n):
    return lax.ppermute(x, "user", [(i, i ^ distance) for i in range(n)])


def body(
    n_item,
    n_user,
    n_ka,
    counts,
    tile_user,
    tile_item,
    tile_live,
    theta_shape,
    theta_rate,
    user_activity,
    beta_shape,
    beta_rate,
    item_popularity,
):
    def sibling(x):
        return lax.ppermute(x, "ka", [(h, n_ka - 1 - h) for h in range(n_ka)])

    both, wide, theta_local = expected_users(theta_shape[0], theta_rate[0])
    item_exp, pack = expected_items(beta_shape[0], beta_rate[0], both, theta_local)
    rows = both.shape[0]
    half_rows = rows // 2
    item_rows = beta_shape.shape[1] * n_user
    dense = dense_counts(
        counts[0, 0],
        tile_user[0, 0],
        tile_item[0, 0],
        tile_live[0],
        rows,
        n_item,
        item_rows,
        n_user,
    )
    came_pack = sibling(pack)

    ahead = range(1, n_item // 2)
    behind = range(1, n_item // 2 + 1)
    shards = {0: both}
    for d in behind:
        shards[2 * d - 1] = along_item(shards[max(2 * d - 3, 0)], 1, n_item)
    for d in ahead:
        shards[2 * d] = along_item(after(wide, shards[1]) if d == 1 else shards[2 * d - 2], -1, n_item)

    item_mine = [item_exp]
    for p in range(1, n_user):
        low = p & -p
        item_mine.append(along_user(after(item_mine[p ^ low], dense), low, n_user))
    item_other = [came_pack] + [sibling(x) for x in item_mine[1:]]

    order = [2 * d - 1 for d in behind] + [2 * d for d in ahead]
    order.insert(len(order) - 1, 0)
    acc = None
    stats = {}
    latest = None
    for i in order:
        passed = after(shards[i], stats[n_item - 1][0])[half_rows:rows] if i == order[-1] else shards[i]
        other = sibling(passed) if i else came_pack
        stats[i], accs = statistics(
            i, [shards[i], other], item_mine, item_other, dense, acc, i == order[-1], half_rows
        )
        acc = accs[0]
        latest = stats[i][0]
    own, own_other = stats[0]

    came = [sibling(accs[1])]
    for p in range(1, n_user):
        sent = merge_items(p, acc, sibling(accs[1 + p]))
        came.append(along_user(sent, p, n_user))
    new_beta_shape = finish_items(item_exp, acc, came)

    back = []
    for d in reversed(behind):
        if d > 1:
            stat = stats[2 * d - 1][0]
            back = [along_item(add_came(stat, back[0], False)[0] if back else stat, -1, n_item)]
    moving = []
    for d in reversed(ahead):
        stat = stats[2 * d][0]
        stat = after(stat, back[0]) if d == 1 else stat
        parts = add_came(stat, moving[0], False) if moving else [stat]
        moving = [along_item(x, 1, n_item) for x in parts]
    came_ahead = moving
    stat = after(stats[1][0], sent) if n_user > 1 else stats[1][0]
    moving = [along_item(x, -1, n_item) for x in add_came(stat, back[0], True)]
    other_behind, mine_behind = moving

    other_sum = own_other
    for x in came_ahead:
        other_sum = lax.optimization_barrier(other_sum + x[half_rows:rows].astype(F32))
    other_sum = other_sum.astype(BF16)
    other_sum = sibling(other_sum)
    other_last = after(sibling(other_behind), new_beta_shape)
    new_theta_rate, new_beta_rate = finish_rates(
        item_mine, [*came_ahead, other_behind], user_activity, item_popularity
    )
    other_last = after(other_last, new_theta_rate)
    new_theta_shape = finish_users(both, own, other_sum, other_last, mine_behind, came_ahead)
    return (new_theta_shape[None], new_theta_rate[None], new_beta_shape[None], new_beta_rate[None])


def solution(mesh):
    in_specs = (
        P(("parts", "item"), "user", None, None, None),
        P(("parts", "item"), "user", None),
        P(("parts", "item"), "user", None),
        P(("parts", "item"), "user"),
        P(("parts", "user"), "item", "ka"),
        P(("parts", "user"), "item", "ka"),
        P(("parts", "user"), "item"),
        P(("parts", "item"), "user", "ka"),
        P(("parts", "item"), "user", "ka"),
        P(("parts", "item"), "user"),
    )
    out_specs = (
        P(("parts", "user"), "item", "ka"),
        P(("parts", "user"), "item", "ka"),
        P(("parts", "item"), "user", "ka"),
        P(("parts", "item"), "user", "ka"),
    )
    run = functools.partial(body, mesh.shape["item"], mesh.shape["user"], mesh.shape["ka"])
    return jax.shard_map(run, mesh=mesh, in_specs=in_specs, out_specs=out_specs, check_vma=False)
```

```python
import functools

import jax
import jax.numpy as jnp
from jax import lax
from jax.experimental import pallas as pl
from jax.experimental.pallas import tpu as pltpu
from jax.sharding import PartitionSpec as P

BF16 = jnp.bfloat16
F32 = jnp.float32
VMEM = pltpu.MemorySpace.VMEM
SMEM = pltpu.MemorySpace.SMEM
HBM = pltpu.MemorySpace.HBM
EXTRA = 16
MIB = 1024 * 1024
CHEAP = pl.CostEstimate(flops=1024, transcendentals=0, bytes_accessed=1024)
DIMS_NT = (((1,), (1,)), ((), ()))
DIMS_TN = (((0,), (0,)), ((), ()))


def pinned(x):
    return pltpu.with_memory_space_constraint(x, HBM)


def reciprocal(x):
    r = pl.reciprocal(x, approx=True)
    return r * (2.0 - x * r)


def exp_digamma(x, inv_rate):
    w = x * (x + 3.0)
    p = w * (w + 2.0)
    y = x + 4.0
    inv = reciprocal(y * p)
    iy = inv * p
    iy2 = iy * iy
    shift = (2.0 * x + 3.0) * (2.0 * w + 2.0) * (inv * y)
    series = iy * 0.5 + iy2 * (1.0 / 12.0 - iy2 * (1.0 / 120.0 - iy2 * (1.0 / 252.0)))
    return y * inv_rate * jnp.exp(-(series + shift))


def encode(values):
    row = lax.broadcasted_iota(jnp.int32, (EXTRA, values[0].shape[1]), 0)
    out = jnp.zeros(row.shape, F32)
    for i, rest in enumerate(values):
        for j in range(3):
            piece = rest.astype(BF16).astype(F32)
            rest = rest - piece
            out = jnp.where(row == 3 * i + j, piece, out)
    return out.astype(BF16)


def decode(block):
    block = block.astype(F32)
    return [block[3 * i : 3 * i + 1] + block[3 * i + 1 : 3 * i + 2] + block[3 * i + 2 : 3 * i + 3] for i in range(2)]


def chunk_copies(starts, chunk, refs, buffers, sems):
    copies = []
    for j, start in enumerate(starts):
        here = pl.ds(start, chunk)
        copies.append(
            [pltpu.make_async_copy(r.at[here], b.at[here], sems.at[i, j]) for i, (r, b) in enumerate(zip(refs, buffers))]
        )
    for group in copies:
        for copy in group:
            copy.start()
    return copies


def users_kernel(chunk, shape_ref, rate_ref, both_ref, wide_ref, total_ref, shape_buf, rate_buf, sems):
    core = lax.axis_index("ka")
    half = both_ref.shape[0] // 2
    steps = half // chunk
    starts = []
    for side in (core, 1 - core):
        starts += [pl.multiple_of(side * half + j * chunk, chunk) for j in range(steps)]
    copies = chunk_copies(starts, chunk, (shape_ref, rate_ref), (shape_buf, rate_buf), sems)
    total = jnp.zeros(total_ref.shape, F32)
    for j, start in enumerate(starts):
        for copy in copies[j]:
            copy.wait()
        x = shape_buf[pl.ds(start, chunk), :]
        inv_rate = reciprocal(rate_buf[pl.ds(start, chunk), :])
        value = exp_digamma(x, inv_rate).astype(BF16)
        both_ref[j * chunk : (j + 1) * chunk, :] = value
        wide_ref[j * chunk : (j + 1) * chunk, :] = value
        total += jnp.sum(x * inv_rate, axis=0, keepdims=True)
    total_ref[...] = total
    wide_ref[2 * half :, :] = jnp.zeros((wide_ref.shape[0] - 2 * half, wide_ref.shape[1]), BF16)


def expected_users(shape_arg, rate_arg):
    rows, cols = shape_arg.shape
    chunk = min(rows // 2, 128)
    return pl.pallas_call(
        functools.partial(users_kernel, chunk),
        in_specs=[pl.BlockSpec(memory_space=HBM)] * 2,
        out_specs=[pl.BlockSpec(memory_space=VMEM)] * 3,
        out_shape=[
            jax.ShapeDtypeStruct((rows, cols), BF16),
            jax.ShapeDtypeStruct((rows + 2 * EXTRA, cols), BF16),
            jax.ShapeDtypeStruct((1, cols), F32),
        ],
        scratch_shapes=[
            pltpu.VMEM((rows, cols), F32),
            pltpu.VMEM((rows, cols), F32),
            pltpu.SemaphoreType.DMA((2, rows // chunk)),
        ],
        compiler_params=pltpu.CompilerParams(vmem_limit_bytes=4 * MIB),
        cost_estimate=CHEAP,
        name="expected_users",
    )(pinned(shape_arg), pinned(rate_arg))


def items_kernel(chunk, shape_ref, rate_ref, both_ref, theta_ref, item_ref, pack_ref, shape_buf, rate_buf, sems):
    rows = shape_ref.shape[0]
    half = both_ref.shape[0] // 2
    starts = list(range(0, rows, chunk))
    copies = chunk_copies(starts, chunk, (shape_ref, rate_ref), (shape_buf, rate_buf), sems)
    pack_ref[:half, :] = both_ref[half:, :]
    total = jnp.zeros(theta_ref.shape, F32)
    for j, start in enumerate(starts):
        for copy in copies[j]:
            copy.wait()
        x = shape_buf[start : start + chunk, :]
        inv_rate = reciprocal(rate_buf[start : start + chunk, :])
        value = exp_digamma(x, inv_rate).astype(BF16)
        item_ref[start : start + chunk, :] = value
        pack_ref[half + start : half + start + chunk, :] = value
        total += jnp.sum(x * inv_rate, axis=0, keepdims=True)
    extra = encode([theta_ref[...], total])
    item_ref[rows:, :] = extra
    pack_ref[half + rows :, :] = extra


def expected_items(shape_arg, rate_arg, both, theta_local):
    rows, cols = shape_arg.shape
    chunk = min(rows, 128)
    return pl.pallas_call(
        functools.partial(items_kernel, chunk),
        in_specs=[pl.BlockSpec(memory_space=m) for m in (HBM, HBM, VMEM, VMEM)],
        out_specs=[pl.BlockSpec(memory_space=VMEM)] * 2,
        out_shape=[jax.ShapeDtypeStruct((r + EXTRA, cols), BF16) for r in (rows, both.shape[0] // 2 + rows)],
        scratch_shapes=[
            pltpu.VMEM((rows, cols), F32),
            pltpu.VMEM((rows, cols), F32),
            pltpu.SemaphoreType.DMA((2, rows // chunk)),
        ],
        compiler_params=pltpu.CompilerParams(vmem_limit_bytes=4 * MIB),
        cost_estimate=CHEAP,
        name="expected_items",
    )(pinned(shape_arg), pinned(rate_arg), both, theta_local)


def dense_kernel(n_item, shard_tiles, chunk, rows, users_in, items_in, live_ref, counts_ref, out_ref, *scratch):
    users_ref, items_ref, buf, sems, index_sems = scratch
    tile = counts_ref.shape[1]
    half = rows // 2
    piece = min(half, tile)
    n_chunks = counts_ref.shape[0] // chunk
    copies = [
        pltpu.make_async_copy(
            counts_ref.at[pl.ds(c * chunk, chunk)], buf.at[pl.ds(c * chunk, chunk)], sems.at[c]
        )
        for c in range(n_chunks)
    ]
    index_copies = [
        pltpu.make_async_copy(users_in, users_ref, index_sems.at[0]),
        pltpu.make_async_copy(items_in, items_ref, index_sems.at[1]),
    ]
    for copy in index_copies + copies:
        copy.start()
    out_ref[...] = jnp.zeros_like(out_ref)
    for copy in index_copies:
        copy.wait()
    z = lax.axis_index("item")
    x = lax.axis_index("user")
    core = lax.axis_index("ka")
    live = live_ref[0]

    def place(slot, carry):
        item = items_ref[slot]
        owner = lax.div(item, shard_tiles)
        column = (owner ^ x) * shard_tiles + lax.rem(item, shard_tiles)
        col = pl.multiple_of(column * tile, tile)
        for j in range(tile // piece):
            row = users_ref[slot] * tile + j * piece
            shard = lax.div(row, rows)
            within = lax.rem(row, rows)

            @pl.when(lax.div(within, half) == core)
            def _():
                back = lax.rem(z - shard + n_item, n_item)
                step = jnp.where(back == 0, 0, jnp.where(back * 2 <= n_item, 2 * back - 1, 2 * (n_item - back)))
                start = pl.multiple_of(step * half + lax.rem(within, half), piece)
                value = buf[slot, j * piece : (j + 1) * piece, :].astype(F32).astype(BF16)
                out_ref[pl.ds(start, piece), pl.ds(col, tile)] = value

        return carry

    for c in range(n_chunks):
        copies[c].wait()
        lax.fori_loop(c * chunk, jnp.clip(live, c * chunk, (c + 1) * chunk), place, 0)


def dense_counts(counts, users, items, live, rows, n_item, item_rows, n_user):
    slots, tile, _ = counts.shape
    chunk = 8
    out_rows = n_item * rows // 2
    return pl.pallas_call(
        functools.partial(dense_kernel, n_item, item_rows // n_user // tile, chunk, rows),
        in_specs=[pl.BlockSpec(memory_space=m) for m in (HBM, HBM, SMEM, HBM)],
        out_specs=pl.BlockSpec(memory_space=VMEM),
        out_shape=jax.ShapeDtypeStruct((out_rows, item_rows), BF16),
        scratch_shapes=[
            pltpu.SMEM(users.shape, jnp.int32),
            pltpu.SMEM(items.shape, jnp.int32),
            pltpu.VMEM((slots, tile, tile), jnp.int32),
            pltpu.SemaphoreType.DMA((slots // chunk,)),
            pltpu.SemaphoreType.DMA((2,)),
        ],
        compiler_params=pltpu.CompilerParams(vmem_limit_bytes=8 * MIB),
        cost_estimate=CHEAP,
        name="dense_counts",
    )(pinned(users), pinned(items), live, pinned(counts))


def stat_kernel(pieces, half, last, has_acc, at, *refs):
    refs = list(refs)
    take = lambda n: [refs.pop(0) for _ in range(n)]
    mine_ref, other_ref = take(2)
    mine = mine_ref[:half, :]
    other = other_ref[half : 2 * half, :] if at and not last else other_ref[:half, :]
    item_mine = take(pieces)
    item_other = take(pieces)
    (counts_ref,) = take(1)
    (acc_in,) = take(1) if has_acc else (None,)
    stat_refs = take(1 if at else 2)
    acc_refs = take(1 + pieces if last else 1)
    cols = mine.shape[1]
    total_mine = None
    total_other = None
    width = 256
    for p in range(pieces):
        rows = item_mine[p].shape[0] - EXTRA
        skip = item_other[p].shape[0] - EXTRA - rows
        for c in range(rows // width):
            left = item_mine[p][c * width : (c + 1) * width, :]
            right = item_other[p][skip + c * width : skip + (c + 1) * width, :]
            norm = lax.dot_general(mine, left, DIMS_NT, preferred_element_type=F32)
            norm += lax.dot_general(other, right, DIMS_NT, preferred_element_type=F32)
            columns = slice(p * rows + c * width, p * rows + (c + 1) * width)
            grid = counts_ref[at * half : (at + 1) * half, columns].astype(F32)
            ratio = (grid * reciprocal(norm)).astype(BF16)
            stat = jnp.dot(ratio, left, preferred_element_type=F32)
            total_mine = stat if total_mine is None else total_mine + stat
            stat = jnp.dot(ratio, right, preferred_element_type=F32)
            total_other = stat if total_other is None else total_other + stat
            for i, factors in enumerate((mine, other)):
                update = lax.dot_general(factors, ratio, DIMS_TN, preferred_element_type=F32)
                if has_acc:
                    update += acc_in[i * cols : (i + 1) * cols, columns]
                if last and i == 0:
                    acc_refs[0][:, columns] = update
                elif last:
                    acc_refs[1 + p][:, c * width : (c + 1) * width] = update.astype(BF16)
                else:
                    acc_refs[0][i * cols : (i + 1) * cols, columns] = update
    if at:
        stat_refs[0][:half, :] = total_mine.astype(BF16)
        stat_refs[0][half : 2 * half, :] = total_other.astype(BF16)
        stat_refs[0][2 * half :, :] = encode(row_totals(item_mine))
    else:
        stat_refs[0][...] = total_mine
        stat_refs[1][...] = total_other


def sum_totals(blocks):
    sums = None
    for block in blocks:
        came = decode(block)
        sums = came if sums is None else [a + b for a, b in zip(sums, came)]
    return sums


def row_totals(item_refs):
    return sum_totals([ref[-EXTRA:, :] for ref in item_refs])


def statistics(at, users, item_mine, item_other, dense, acc, last, half_rows):
    half = users[0].shape[1]
    item_rows = dense.shape[1]
    args = [*users, *item_mine, *item_other, dense]
    if acc is not None:
        args.append(acc)
    if at:
        out_shape = [jax.ShapeDtypeStruct((2 * half_rows + EXTRA, half), BF16)]
    else:
        out_shape = [jax.ShapeDtypeStruct((half_rows, half), F32)] * 2
    n_stats = len(out_shape)
    if last:
        out_shape.append(jax.ShapeDtypeStruct((half, item_rows), F32))
        out_shape += [jax.ShapeDtypeStruct((half, item_rows // len(item_mine)), BF16) for _ in item_mine]
    else:
        out_shape.append(jax.ShapeDtypeStruct((2 * half, item_rows), F32))
    spec = pl.BlockSpec(memory_space=VMEM)
    out = pl.pallas_call(
        functools.partial(stat_kernel, len(item_mine), half_rows, last, acc is not None, at),
        in_specs=[spec] * len(args),
        out_specs=[spec] * len(out_shape),
        out_shape=out_shape,
        compiler_params=pltpu.CompilerParams(vmem_limit_bytes=16 * MIB),
        cost_estimate=CHEAP,
        name="statistics_%d" % at,
    )(*args)
    return list(out[:n_stats]), list(out[n_stats:])


def add_kernel(stat_ref, came_ref, out_ref):
    rows = stat_ref.shape[0] - EXTRA
    out_ref[:rows, :] = (stat_ref[:rows, :].astype(F32) + came_ref[:rows, :].astype(F32)).astype(BF16)
    out_ref[rows:, :] = encode(sum_totals([stat_ref[rows:, :], came_ref[rows:, :]]))


def split_kernel(stat_ref, came_ref, other_ref, mine_ref):
    half = other_ref.shape[0] - EXTRA
    total = stat_ref[: 2 * half, :].astype(F32) + came_ref[: 2 * half, :].astype(F32)
    other_ref[:half, :] = total[half:, :].astype(BF16)
    other_ref[half:, :] = encode(sum_totals([stat_ref[2 * half :, :], came_ref[2 * half :, :]]))
    mine_ref[:half, :] = total[:half, :].astype(BF16)
    mine_ref[half:, :] = jnp.zeros((2 * EXTRA, mine_ref.shape[1]), BF16)


def add_came(stat, came, split):
    rows, cols = stat.shape
    half = (rows - EXTRA) // 2
    shapes = [half + EXTRA, half + 2 * EXTRA] if split else [rows]
    out = pl.pallas_call(
        split_kernel if split else add_kernel,
        in_specs=[pl.BlockSpec(memory_space=VMEM)] * 2,
        out_specs=[pl.BlockSpec(memory_space=VMEM)] * len(shapes),
        out_shape=[jax.ShapeDtypeStruct((r, cols), BF16) for r in shapes],
        compiler_params=pltpu.CompilerParams(vmem_limit_bytes=2 * MIB),
        cost_estimate=CHEAP,
        name="add_came",
    )(stat, came)
    return list(out)


def merge_items_kernel(p, mine_ref, came_ref, out_ref):
    width = out_ref.shape[1]
    out_ref[...] = (mine_ref[:, p * width : (p + 1) * width] + came_ref[...].astype(F32)).astype(BF16)


def merge_items(p, mine, came):
    return pl.pallas_call(
        functools.partial(merge_items_kernel, p),
        in_specs=[pl.BlockSpec(memory_space=VMEM)] * 2,
        out_specs=pl.BlockSpec(memory_space=VMEM),
        out_shape=jax.ShapeDtypeStruct(came.shape, BF16),
        compiler_params=pltpu.CompilerParams(vmem_limit_bytes=2 * MIB),
        cost_estimate=CHEAP,
        name="merge_items",
    )(mine, came)


def finish_rates_kernel(pieces, n_came, *refs):
    refs = list(refs)
    take = lambda n: [refs.pop(0) for _ in range(n)]
    item_refs = take(pieces)
    came = take(n_came)
    columns = take(2)
    outs = take(2)
    bufs = take(2)
    (sems,) = take(1)
    theta_total, beta_total = sum_totals([ref[-EXTRA:, :] for ref in item_refs + came])
    copies = []
    for i, total in enumerate((beta_total, theta_total)):
        rows = columns[i].shape[1]
        column = jnp.broadcast_to(columns[i][...], (total.shape[1], rows)).T
        bufs[i][...] = column + total
        copies.append(pltpu.make_async_copy(bufs[i], outs[i], sems.at[i]))
        copies[-1].start()
    for copy in copies:
        copy.wait()


def finish_rates(items, came, activity, popularity):
    args = [*items, *came, activity, popularity]
    out_shape = [jax.ShapeDtypeStruct((c.shape[1], items[0].shape[1]), F32) for c in (activity, popularity)]
    return pl.pallas_call(
        functools.partial(finish_rates_kernel, len(items), len(came)),
        in_specs=[pl.BlockSpec(memory_space=VMEM)] * len(args),
        out_specs=[pl.BlockSpec(memory_space=HBM)] * 2,
        out_shape=out_shape,
        scratch_shapes=[pltpu.VMEM(o.shape, F32) for o in out_shape] + [pltpu.SemaphoreType.DMA((2,))],
        compiler_params=pltpu.CompilerParams(vmem_limit_bytes=6 * MIB),
        cost_estimate=CHEAP,
        name="finish_rates",
    )(*args)


def finish_users_kernel(n_ahead, *refs):
    refs = list(refs)
    take = lambda n: [refs.pop(0) for _ in range(n)]
    both_ref, own_ref, other_ref, last_ref, mine_ref = take(5)
    ahead = take(n_ahead)
    out_ref, buf, sems = take(3)
    core = lax.axis_index("ka")
    half = own_ref.shape[0]

    def send(i, side, rows, total):
        here = pl.ds(pl.multiple_of(side * half, half), half)
        buf[here, :] = 0.3 + both_ref[rows, :].astype(F32) * total
        copy = pltpu.make_async_copy(buf.at[here], out_ref.at[here], sems.at[i])
        copy.start()
        return copy

    total = own_ref[...] + mine_ref[:half, :].astype(F32)
    for ref in ahead:
        total += ref[:half, :].astype(F32)
    other = other_ref[...].astype(F32) + last_ref[:half, :].astype(F32)
    copies = [send(0, core, slice(0, half), total), send(1, 1 - core, slice(half, 2 * half), other)]
    for copy in copies:
        copy.wait()


def finish_users(both, own, other_sum, other_last, mine, ahead):
    rows, half = both.shape
    args = [both, own, other_sum, other_last, mine, *ahead]
    return pl.pallas_call(
        functools.partial(finish_users_kernel, len(ahead)),
        in_specs=[pl.BlockSpec(memory_space=VMEM)] * len(args),
        out_specs=pl.BlockSpec(memory_space=HBM),
        out_shape=jax.ShapeDtypeStruct((rows, half), F32),
        scratch_shapes=[pltpu.VMEM((rows, half), F32), pltpu.SemaphoreType.DMA((2,))],
        compiler_params=pltpu.CompilerParams(vmem_limit_bytes=4 * MIB),
        cost_estimate=CHEAP,
        name="finish_users",
    )(*args)


def finish_items_kernel(n, exp_ref, own_ref, *refs):
    out_ref, buf, sems = refs[n:]
    rows = out_ref.shape[0]
    chunk = min(rows, 256)
    copies = []
    for j in range(rows // chunk):
        part = slice(j * chunk, (j + 1) * chunk)
        total = own_ref[:, part]
        for p in range(n):
            total += refs[p][:, part].astype(F32)
        buf[part, :] = 0.3 + exp_ref[part, :].astype(F32) * total.T
        here = pl.ds(j * chunk, chunk)
        copies.append(pltpu.make_async_copy(buf.at[here], out_ref.at[here], sems.at[j]))
        copies[-1].start()
    for copy in copies:
        copy.wait()


def finish_items(item_exp, own, came):
    half, rows = came[0].shape
    return pl.pallas_call(
        functools.partial(finish_items_kernel, len(came)),
        in_specs=[pl.BlockSpec(memory_space=VMEM)] * (2 + len(came)),
        out_specs=pl.BlockSpec(memory_space=HBM),
        out_shape=jax.ShapeDtypeStruct((rows, half), F32),
        scratch_shapes=[pltpu.VMEM((rows, half), F32), pltpu.SemaphoreType.DMA((rows // min(rows, 256),))],
        compiler_params=pltpu.CompilerParams(vmem_limit_bytes=6 * MIB),
        cost_estimate=CHEAP,
        name="finish_items",
    )(item_exp, own, *came)


def along_item(x, shift, n):
    return lax.ppermute(x, "item", [(i, (i + shift) % n) for i in range(n)])


def after(x, y):
    return lax.optimization_barrier((x, y))[0]


def along_user(x, distance, n):
    return lax.ppermute(x, "user", [(i, i ^ distance) for i in range(n)])


def body(
    n_item,
    n_user,
    n_ka,
    counts,
    tile_user,
    tile_item,
    tile_live,
    theta_shape,
    theta_rate,
    user_activity,
    beta_shape,
    beta_rate,
    item_popularity,
):
    def sibling(x):
        return lax.ppermute(x, "ka", [(h, n_ka - 1 - h) for h in range(n_ka)])

    both, wide, theta_local = expected_users(theta_shape[0], theta_rate[0])
    item_exp, pack = expected_items(beta_shape[0], beta_rate[0], both, theta_local)
    rows = both.shape[0]
    half_rows = rows // 2
    item_rows = beta_shape.shape[1] * n_user
    dense = dense_counts(
        counts[0, 0],
        tile_user[0, 0],
        tile_item[0, 0],
        tile_live[0],
        rows,
        n_item,
        item_rows,
        n_user,
    )
    came_pack = sibling(pack)

    ahead = range(1, n_item // 2)
    behind = range(1, n_item // 2 + 1)
    shards = {0: both}
    for d in behind:
        shards[2 * d - 1] = along_item(shards[max(2 * d - 3, 0)], 1, n_item)
    for d in ahead:
        shards[2 * d] = along_item(after(wide, shards[1]) if d == 1 else shards[2 * d - 2], -1, n_item)

    item_mine = [item_exp]
    for p in range(1, n_user):
        low = p & -p
        item_mine.append(along_user(after(item_mine[p ^ low], dense), low, n_user))
    item_other = [came_pack] + [sibling(x) for x in item_mine[1:]]

    order = [2 * d - 1 for d in behind] + [2 * d for d in ahead]
    order.insert(len(order) - 1, 0)
    acc = None
    stats = {}
    latest = None
    for i in order:
        passed = after(shards[i], stats[n_item - 1][0])[half_rows:rows] if i == order[-1] else shards[i]
        other = sibling(passed) if i else came_pack
        stats[i], accs = statistics(
            i, [shards[i], other], item_mine, item_other, dense, acc, i == order[-1], half_rows
        )
        acc = accs[0]
        latest = stats[i][0]
    own, own_other = stats[0]

    came = [sibling(accs[1])]
    for p in range(1, n_user):
        sent = merge_items(p, acc, sibling(accs[1 + p]))
        came.append(along_user(sent, p, n_user))
    new_beta_shape = finish_items(item_exp, acc, came)

    moving = []
    for d in reversed(ahead):
        stat = stats[2 * d][0]
        parts = add_came(stat, moving[0], False) if moving else [stat]
        moving = [along_item(x, 1, n_item) for x in parts]
    came_ahead = moving
    moving = []
    for d in reversed(behind):
        stat = stats[2 * d - 1][0]
        if d == 1 and n_user > 1:
            stat = after(stat, sent)
        parts = add_came(stat, moving[0], d == 1) if moving else [stat]
        moving = [along_item(x, -1, n_item) for x in parts]
    other_behind, mine_behind = moving

    other_sum = own_other
    for x in came_ahead:
        other_sum = lax.optimization_barrier(other_sum + x[half_rows:rows].astype(F32))
    other_sum = other_sum.astype(BF16)
    other_sum = sibling(other_sum)
    other_last = after(sibling(other_behind), new_beta_shape)
    new_theta_rate, new_beta_rate = finish_rates(
        item_mine, [*came_ahead, other_behind], user_activity, item_popularity
    )
    other_last = after(other_last, new_theta_rate)
    new_theta_shape = finish_users(both, own, other_sum, other_last, mine_behind, came_ahead)
    return (new_theta_shape[None], new_theta_rate[None], new_beta_shape[None], new_beta_rate[None])


def solution(mesh):
    in_specs = (
        P(("parts", "item"), "user", None, None, None),
        P(("parts", "item"), "user", None),
        P(("parts", "item"), "user", None),
        P(("parts", "item"), "user"),
        P(("parts", "user"), "item", "ka"),
        P(("parts", "user"), "item", "ka"),
        P(("parts", "user"), "item"),
        P(("parts", "item"), "user", "ka"),
        P(("parts", "item"), "user", "ka"),
        P(("parts", "item"), "user"),
    )
    out_specs = (
        P(("parts", "user"), "item", "ka"),
        P(("parts", "user"), "item", "ka"),
        P(("parts", "item"), "user", "ka"),
        P(("parts", "item"), "user", "ka"),
    )
    run = functools.partial(body, mesh.shape["item"], mesh.shape["user"], mesh.shape["ka"])
    return jax.shard_map(run, mesh=mesh, in_specs=in_specs, out_specs=out_specs, check_vma=False)
```
